32 devices in a mesh: dp: 16 (over z, y, x), mp: 2 (over core).
Axes of the slice: x: 2, y: 2, z: 4, core: 2. Of those that a mesh axis runs over, the one named last changes fastest.
Arguments:
- token_ids: int32 [32, 1024], P('dp'), may hold values from 0 to 820
- segment_ids: int32 [32, 1024], P('dp'), may hold values from 0 to 15, never falling along the last dimension, each value on 1 to 128 neighbouring positions
- timesteps: int32 [32], P('dp'), may hold values from 0 to 1999
- noise: float32 [32, 1024, 128], P('dp'), may hold values from -6 to 6
- bucket_ids: int32 [32, 1024], P('dp'), may hold values from 0 to 15, as said below
- counted: int32 [32, 1024], P('dp'), may hold values from 0 to 1, as said below
- embed: float32 [821, 128], replicated, may hold values from -0.9 to 0.9
- up_weight: float32 [128, 768], replicated, may hold values from -0.5 to 0.5
- down_weight: float32 [768, 128], replicated, may hold values from -0.21875 to 0.21875
- qkv_weight: float32 [3, 768, 768], P(None, 'dp', 'mp'), may hold values from -0.21875 to 0.21875
- out_weight: float32 [768, 768], P('mp', 'dp'), may hold values from -0.625 to 0.625
- fc_weight: float32 [768, 3072], P('dp', 'mp'), may hold values from -0.21875 to 0.21875
- proj_weight: float32 [3072, 768], P('mp', 'dp'), may hold values from -0.109375 to 0.109375
- norm_params: float32 [6, 768], replicated, as said below
- embed_m: float32 [821, 128], replicated, may hold values from -2.3841858e-06 to 2.3841858e-06
- embed_v: float32 [821, 128], replicated, may hold values from 1.3542443e-14 to 5.4169773e-14
- up_m: float32 [128, 768], replicated, may hold values from -2.3841858e-06 to 2.3841858e-06
- up_v: float32 [128, 768], replicated, may hold values from 1.3542443e-14 to 5.4169773e-14
- down_m: float32 [768, 128], replicated, may hold values from -2.3841858e-06 to 2.3841858e-06
- down_v: float32 [768, 128], replicated, may hold values from 1.3542443e-14 to 5.4169773e-14
- qkv_m: float32 [3, 768, 768], P(None, 'dp', 'mp'), may hold values from -2.3841858e-06 to 2.3841858e-06
- qkv_v: float32 [3, 768, 768], P(None, 'dp', 'mp'), may hold values from 1.3542443e-14 to 5.4169773e-14
- out_m: float32 [768, 768], P('mp', 'dp'), may hold values from -2.3841858e-06 to 2.3841858e-06
- out_v: float32 [768, 768], P('mp', 'dp'), may hold values from 1.3542443e-14 to 5.4169773e-14
- fc_m: float32 [768, 3072], P('dp', 'mp'), may hold values from -2.3841858e-06 to 2.3841858e-06
- fc_v: float32 [768, 3072], P('dp', 'mp'), may hold values from 1.3542443e-14 to 5.4169773e-14
- proj_m: float32 [3072, 768], P('mp', 'dp'), may hold values from -2.3841858e-06 to 2.3841858e-06
- proj_v: float32 [3072, 768], P('mp', 'dp'), may hold values from 1.3542443e-14 to 5.4169773e-14
- norm_m: float32 [6, 768], replicated, may hold values from -2.2888184e-05 to 2.2888184e-05
- norm_v: float32 [6, 768], replicated, may hold values from 1.3542443e-12 to 5.416977e-12
Outputs:
- loss_sum: float32 [], replicated
- weight_total: float32 [], replicated
- grad_norm: float32 [], replicated
- embed_first: float32 [821, 128], replicated
- embed_second: float32 [821, 128], replicated
- embed_next: float32 [821, 128], replicated
- up_first: float32 [128, 768], replicated
- up_second: float32 [128, 768], replicated
- up_next: float32 [128, 768], replicated
- down_first: float32 [768, 128], replicated
- down_second: float32 [768, 128], replicated
- down_next: float32 [768, 128], replicated
- qkv_first: float32 [3, 768, 768], P(None, 'dp', 'mp')
- qkv_second: float32 [3, 768, 768], P(None, 'dp', 'mp')
- qkv_next: float32 [3, 768, 768], P(None, 'dp', 'mp')
- out_first: float32 [768, 768], P('mp', 'dp')
- out_second: float32 [768, 768], P('mp', 'dp')
- out_next: float32 [768, 768], P('mp', 'dp')
- fc_first: float32 [768, 3072], P('dp', 'mp')
- fc_second: float32 [768, 3072], P('dp', 'mp')
- fc_next: float32 [768, 3072], P('dp', 'mp')
- proj_first: float32 [3072, 768], P('mp', 'dp')
- proj_second: float32 [3072, 768], P('mp', 'dp')
- proj_next: float32 [3072, 768], P('mp', 'dp')
- norm_first: float32 [6, 768], replicated
- norm_second: float32 [6, 768], replicated
- norm_next: float32 [6, 768], replicated
The draws below stay inside these ranges and needn't reach their ends.
Inputs may be any that keep to these rules, and one draw needn't show every extreme that they name: `counted`: 1 marks a position whose loss counts. `bucket_ids`: one bucket, which differs from draw to draw, holds no position. `norm_params`: rows 0, 2 and 4 hold the gains and rows 1, 3 and 5 the shifts of the three norms.
All inputs are finite; a program needn't handle non-finite values.
Results may differ from the reference program's by a relative error of at most 0.0075.
Values may be sent and summed in bfloat16 or wider, within the bound.
A program may use at most 320 MiB of HBM per device.

```python
import math
import jax
import jax.numpy as jnp
import numpy as np
from jax import lax

D = 768
HEADS = 12
HEAD_DIM = 64
FF = 3072
EMB = 128
VOCAB = 821
LENGTH = 1024
SEG_MOST = 128
NB = 16
T_STEPS = 2000
STEP = 10
ROWS = 32


def draw_bucket_ids(key, part):
    key = jax.random.fold_in(key, 37)
    first_key, second_key, order_key, empty_key = jax.random.split(key, 4)
    first = jax.random.randint(first_key, (ROWS, LENGTH), 0, NB - 1)
    second = jax.random.randint(second_key, (ROWS, LENGTH), 0, NB - 1)
    order = jax.random.permutation(order_key, NB - 1).astype(jnp.int32)
    picked = order[jnp.minimum(first, second)]
    empty = jax.random.randint(empty_key, (), 1, NB - 1)
    return (picked + (picked >= empty).astype(jnp.int32)).astype(jnp.int32)


def draw_counted(key, part):
    key = jax.random.fold_in(key, 11)
    rank = jnp.arange(ROWS, dtype=jnp.int32)[:, None]
    level = 250 + 500 * rank // max(ROWS - 1, 1)
    picks = jax.random.randint(key, (ROWS, LENGTH), 0, 1000)
    return (picks < level).astype(jnp.int32)


def draw_norm_params(key, part):
    key = jax.random.fold_in(key, 23)
    first_key, second_key = jax.random.split(key)
    ramp = jnp.arange(D, dtype=jnp.float32) / (D - 1)
    gains = (0.5 + ramp)[None, :] * jax.random.uniform(first_key, (3, D), jnp.float32, 0.7, 1.4)
    shifts = 0.2 * jax.random.normal(second_key, (3, D), jnp.float32)
    return jnp.stack([gains, shifts], axis=1).reshape(6, D)


def set_ends(drawn, key, smallest, top_value):
    extent = drawn.shape
    spot = [jax.random.randint(jax.random.fold_in(key, axis), (), 0, extent[axis]) for axis in range(len(extent))]
    drawn = drawn.at[tuple(spot)].set(smallest)
    longest = extent.index(max(extent))
    spot[longest] = (spot[longest] + 1) % extent[longest]
    return drawn.at[tuple(spot)].set(top_value)


def block_levels(own_key, extent, shards, least, largest):
    factor_of = 1.0
    for position, shards_of in shards:
        heights = jax.random.uniform(jax.random.fold_in(jax.random.fold_in(own_key, 6), position), (shards_of,), jnp.float32, least / len(shards), largest / len(shards))
        factor_of = factor_of * jnp.repeat(jnp.exp(heights), extent[position] // shards_of).reshape((-1,) + (1,) * (len(extent) - 1 - position))
    return factor_of


def rank_bounds(number_of, skew):
    weights = [(1 << 20) // math.isqrt(grade ** skew) + 1 for grade in range(1, number_of + 1)]
    deviation = 1 + sum(weights) // (1 << 30)
    return np.cumsum(np.array([max(1, weight // deviation) for weight in weights]))


def skewed_ids(own_key, shape, amount, slope):
    grid = rank_bounds(amount, slope)
    pick = jax.random.randint(jax.random.fold_in(own_key, 1), shape, 0, int(grid[amount - 1]))
    grade = jnp.searchsorted(jnp.asarray(grid, jnp.int32), pick, side="right")
    return jax.random.permutation(jax.random.fold_in(own_key, 2), amount)[grade].astype(jnp.int32)


def profile(count, total, limit, slope):
    portions = [(1 << 20) // math.isqrt(grade ** slope) + 1 for grade in range(2, count + 1)]
    spare, holding = total - limit - (count - 1), [1] * (count - 1)
    while spare > 0:
        free = [i for i in range(count - 1) if holding[i] < limit]
        mass, left = sum([portions[i] for i in free]), spare
        for i in free:
            extra = min(limit - holding[i], max(1, left * portions[i] // mass), spare)
            holding[i] = holding[i] + extra
            spare = spare - extra
    return np.array([limit] + holding)


def uneven(own_key, amount, total, bound, skew):
    if amount == 2:
        one = jax.random.randint(own_key, (), max(1, total - bound), min(bound, total - 1) + 1)
        return jnp.stack([one, total - one])
    lengths = jnp.asarray(profile(amount, total, bound, skew), jnp.int32)
    couples = (amount - 1) // 2
    source_of, taker = lengths[1:1 + 2 * couples:2], lengths[2:2 + 2 * couples:2]
    slack = jnp.minimum(source_of - 1, bound - taker)
    moved = jax.random.randint(jax.random.fold_in(own_key, 1), (couples,), 0, 1 << 20) % (slack + 1)
    lengths = lengths.at[1:1 + 2 * couples:2].set(source_of - moved).at[2:2 + 2 * couples:2].set(taker + moved)
    return lengths[jax.random.permutation(jax.random.fold_in(own_key, 2), amount)]


def centred(rng, extent, scale, reach, shards=(), kind=jnp.bfloat16):
    loudness = block_levels(rng, extent, shards, -0.22, 0.18) if shards else 1.0
    values = jax.random.normal(rng, extent, jnp.float32) * scale * loudness
    return jnp.minimum(jnp.maximum(values, -reach), reach).astype(kind)


def setup_inputs(seed: int = 0) -> dict:
    keys = jax.random.split(jax.random.key(seed), 31)
    return {
        "token_ids": set_ends(skewed_ids(keys[0], (ROWS, LENGTH), VOCAB, 2), jax.random.fold_in(keys[0], 3), 0, VOCAB - 1).astype(jnp.int32),
        "segment_ids": jax.vmap(lambda own: jnp.searchsorted(jnp.cumsum(uneven(own, 2 * LENGTH // SEG_MOST, LENGTH, SEG_MOST, 1)), jnp.arange(LENGTH), side="right"))(jax.random.split(keys[1], ROWS)).reshape((ROWS, LENGTH)).astype(jnp.int32),
        "timesteps": set_ends(jax.random.randint(keys[2], (ROWS,), 0, T_STEPS), jax.random.fold_in(keys[2], 1), 0, T_STEPS - 1).astype(jnp.int32),
        "noise": centred(keys[3], (ROWS, LENGTH, EMB), 1.0, 6.0, ((0, 16),), jnp.float32),
        "bucket_ids": draw_bucket_ids(jax.random.fold_in(keys[30], 71), 0),
        "counted": draw_counted(jax.random.fold_in(keys[30], 71), 0),
        "embed": centred(keys[6], (VOCAB, EMB), 0.15, 0.9, (), jnp.float32),
        "up_weight": centred(keys[7], (EMB, D), EMB ** -0.5, 0.5, (), jnp.float32),
        "down_weight": centred(keys[8], (D, EMB), D ** -0.5, 0.21875, (), jnp.float32),
        "qkv_weight": centred(keys[9], (3, D, D), D ** -0.5, 0.21875, ((1, 16), (2, 2)), jnp.float32),
        "out_weight": centred(keys[10], (D, D), (D // 8) ** -0.5, 0.625, ((0, 2), (1, 16)), jnp.float32),
        "fc_weight": centred(keys[11], (D, FF), D ** -0.5, 0.21875, ((0, 16), (1, 2)), jnp.float32),
        "proj_weight": centred(keys[12], (FF, D), FF ** -0.5, 0.109375, ((0, 2), (1, 16)), jnp.float32),
        "norm_params": draw_norm_params(jax.random.fold_in(keys[30], 71), 0),
        "embed_m": centred(keys[14], (VOCAB, EMB), (0.0011 / (VOCAB * EMB + 2 * EMB * D + 4 * D * D + 2 * D * FF + 6 * D) ** 0.5), 2.384185791015625e-06, (), jnp.float32),
        "embed_v": jnp.clip(jnp.exp(jax.random.uniform(keys[15], (VOCAB, EMB), jnp.float32, math.log(1.3542443228831743e-14), math.log(5.416977291532697e-14))), 1.3542443228831743e-14, 5.416977291532697e-14),
        "up_m": centred(keys[16], (EMB, D), (0.0011 / (VOCAB * EMB + 2 * EMB * D + 4 * D * D + 2 * D * FF + 6 * D) ** 0.5), 2.384185791015625e-06, (), jnp.float32),
        "up_v": jnp.clip(jnp.exp(jax.random.uniform(keys[17], (EMB, D), jnp.float32, math.log(1.3542443228831743e-14), math.log(5.416977291532697e-14))), 1.3542443228831743e-14, 5.416977291532697e-14),
        "down_m": centred(keys[18], (D, EMB), (0.0011 / (VOCAB * EMB + 2 * EMB * D + 4 * D * D + 2 * D * FF + 6 * D) ** 0.5), 2.384185791015625e-06, (), jnp.float32),
        "down_v": jnp.clip(jnp.exp(jax.random.uniform(keys[19], (D, EMB), jnp.float32, math.log(1.3542443228831743e-14), math.log(5.416977291532697e-14))), 1.3542443228831743e-14, 5.416977291532697e-14),
        "qkv_m": centred(keys[20], (3, D, D), (0.0011 / (VOCAB * EMB + 2 * EMB * D + 4 * D * D + 2 * D * FF + 6 * D) ** 0.5), 2.384185791015625e-06, ((1, 16), (2, 2)), jnp.float32),
        "qkv_v": jnp.clip(jnp.exp(math.log(5.416977291532697e-14) - 1.3862944 * jax.random.uniform(keys[21], (3, D, D), jnp.float32) ** block_levels(keys[21], (3, D, D), ((1, 16), (2, 2)), -0.2, 0.2)), 1.3542443228831743e-14, 5.416977291532697e-14),
        "out_m": centred(keys[22], (D, D), (0.0011 / (VOCAB * EMB + 2 * EMB * D + 4 * D * D + 2 * D * FF + 6 * D) ** 0.5), 2.384185791015625e-06, ((0, 2), (1, 16)), jnp.float32),
        "out_v": jnp.clip(jnp.exp(math.log(5.416977291532697e-14) - 1.3862944 * jax.random.uniform(keys[23], (D, D), jnp.float32) ** block_levels(keys[23], (D, D), ((0, 2), (1, 16)), -0.2, 0.2)), 1.3542443228831743e-14, 5.416977291532697e-14),
        "fc_m": centred(keys[24], (D, FF), (0.0011 / (VOCAB * EMB + 2 * EMB * D + 4 * D * D + 2 * D * FF + 6 * D) ** 0.5), 2.384185791015625e-06, ((0, 16), (1, 2)), jnp.float32),
        "fc_v": jnp.clip(jnp.exp(math.log(5.416977291532697e-14) - 1.3862944 * jax.random.uniform(keys[25], (D, FF), jnp.float32) ** block_levels(keys[25], (D, FF), ((0, 16), (1, 2)), -0.2, 0.2)), 1.3542443228831743e-14, 5.416977291532697e-14),
        "proj_m": centred(keys[26], (FF, D), (0.0011 / (VOCAB * EMB + 2 * EMB * D + 4 * D * D + 2 * D * FF + 6 * D) ** 0.5), 2.384185791015625e-06, ((0, 2), (1, 16)), jnp.float32),
        "proj_v": jnp.clip(jnp.exp(math.log(5.416977291532697e-14) - 1.3862944 * jax.random.uniform(keys[27], (FF, D), jnp.float32) ** block_levels(keys[27], (FF, D), ((0, 2), (1, 16)), -0.2, 0.2)), 1.3542443228831743e-14, 5.416977291532697e-14),
        "norm_m": centred(keys[28], (6, D), (0.011 / (VOCAB * EMB + 2 * EMB * D + 4 * D * D + 2 * D * FF + 6 * D) ** 0.5), 2.288818359375e-05, (), jnp.float32),
        "norm_v": jnp.clip(jnp.exp(jax.random.uniform(keys[29], (6, D), jnp.float32, math.log(1.3542442991662518e-12), math.log(5.416977196665007e-12))), 1.3542442991662518e-12, 5.416977196665007e-12),
    }


@jax.custom_vjp
def low(v):
    return lax.optimization_barrier(v.astype(jnp.bfloat16)).astype(jnp.float32)

@jax.custom_vjp
def low_back(v):
    return v

def low_keep(v):
    return (low(v), None)

def low_pass(kept, grad):
    return (grad,)

def back_keep(v):
    return (v, None)

def back_low(kept, grad):
    return (low(grad),)
low.defvjp(low_keep, low_pass)
low_back.defvjp(back_keep, back_low)
NORM_EPS = 1e-05
MASKED = -1e+30
BETA_FIRST = 0.9
BETA_SECOND = 0.999
ADAM_EPS = 1e-08
MATRIX_RATE = 0.05
NORM_RATE = 0.5
WEIGHT_DECAY = 0.1
CLIP_NORM = 0.01
HIGHEST = lax.Precision.HIGHEST

def product(left, right):
    return jnp.dot(left, right, precision=HIGHEST, preferred_element_type=jnp.float32)

def layer_norm(values, gain, shift):
    center = values - lax.optimization_barrier(jnp.mean(values, axis=-1, keepdims=True))
    spread = lax.optimization_barrier(jnp.mean(center * center, axis=-1, keepdims=True))
    return center * lax.rsqrt(spread + NORM_EPS) * gain + shift

def sinusoid(where, width):
    half = width // 2
    freqs = jnp.exp(-math.log(10000.0) * jnp.arange(half, dtype=jnp.float32) / half)
    angles = where[:, None] * freqs[None, :]
    return jnp.concatenate([jnp.sin(angles), jnp.cos(angles)], axis=-1)

def row_loss(params, token_row, segment_row, timestep, noise_row, scale_row):
    embed, up_weight, down_weight, qkv_weight, out_weight, fc_weight, proj_weight, norms = params
    length = token_row.shape[0]
    start = embed[token_row]
    keep = 1.0 - jnp.sqrt(timestep.astype(jnp.float32) / T_STEPS + 0.0001)
    noisy = jnp.sqrt(keep) * start + jnp.sqrt(1.0 - keep) * noise_row
    hidden = low_back(product(low(noisy), low(up_weight)))
    hidden = hidden + sinusoid(jnp.arange(length, dtype=jnp.float32), D)
    hidden = hidden + sinusoid(timestep.astype(jnp.float32).reshape(1), D)
    normed = low(layer_norm(hidden, norms[0], norms[1]))
    heads = [low(low_back(product(normed, low(qkv_weight[index])))).reshape(length, HEADS, HEAD_DIM) for index in range(3)]
    scores = jnp.einsum('qhd,khd->hqk', heads[0], heads[1], precision=HIGHEST) * HEAD_DIM ** (-0.5)
    scores = low_back(scores)
    same = segment_row[:, None] == segment_row[None, :]
    probs = jax.nn.softmax(jnp.where(same[None], scores, MASKED), axis=-1)
    mixed = jnp.einsum('hqk,khd->qhd', low(probs), heads[2], precision=HIGHEST)
    mixed = low(low_back(mixed.reshape(length, D)))
    hidden_one = hidden + low_back(product(mixed, low(out_weight)))
    normed = low(layer_norm(hidden_one, norms[2], norms[3]))
    pre_act = low_back(product(normed, low(fc_weight)))
    hidden_two = hidden_one + low_back(product(low(jax.nn.gelu(pre_act)), low(proj_weight)))
    normed = low(layer_norm(hidden_two, norms[4], norms[5]))
    predicted = low_back(product(normed, low(down_weight)))
    logits = low_back(lax.dot_general(low(predicted), low(embed), (((1,), (1,)), ((), ())), precision=HIGHEST, preferred_element_type=jnp.float32))
    log_norm = jax.nn.logsumexp(logits, axis=-1)
    picked = jnp.take_along_axis(logits, token_row[:, None], axis=1)[:, 0]
    error = predicted - start
    per_token = lax.optimization_barrier(jnp.sum(error * error, axis=-1)) / EMB + log_norm - picked
    return jnp.sum(scale_row * per_token)

def adam_update(weight, grad, first, second, rate, decay):
    first_new = BETA_FIRST * first + (1.0 - BETA_FIRST) * grad
    second_new = BETA_SECOND * second + (1.0 - BETA_SECOND) * grad * grad
    first_hat = first_new / (1.0 - BETA_FIRST ** STEP)
    second_hat = second_new / (1.0 - BETA_SECOND ** STEP)
    weight_new = weight - rate * (first_hat / (jnp.sqrt(second_hat) + ADAM_EPS) + decay * weight)
    return (first_new, second_new, weight_new)

def reference(token_ids, segment_ids, timesteps, noise, bucket_ids, counted, embed, up_weight, down_weight, qkv_weight, out_weight, fc_weight, proj_weight, norm_params, embed_m, embed_v, up_m, up_v, down_m, down_v, qkv_m, qkv_v, out_m, out_v, fc_m, fc_v, proj_m, proj_v, norm_m, norm_v):
    live = counted.astype(jnp.float32)
    bucket_hot = (bucket_ids[..., None] == jnp.arange(NB)[None, None, :]).astype(jnp.float32)
    counts = lax.optimization_barrier(jnp.sum(live[..., None] * bucket_hot, axis=(0, 1)))
    live_total = jnp.sum(counts)
    bucket_weight = live_total / (NB * jnp.maximum(counts, 1.0))
    weight_total = jnp.sum(counts * bucket_weight)
    token_scale = live * lax.optimization_barrier(jnp.sum(bucket_hot * bucket_weight, axis=-1))
    params = (embed, up_weight, down_weight, qkv_weight, out_weight, fc_weight, proj_weight, norm_params)
    row_step = jax.checkpoint(row_loss)

    def total(weights):

        def accumulate(carry, row):
            return (carry + row_step(weights, *row), None)
        result, unused = lax.scan(accumulate, jnp.zeros((), jnp.float32), (token_ids, segment_ids, timesteps, noise, token_scale))
        return result
    loss_sum, pull = jax.vjp(total, params)
    grads = pull(jnp.ones((), jnp.float32) / weight_total)[0]
    grad_norm = jnp.sqrt(sum((jnp.sum(piece * piece) for piece in grads)))
    factor = jnp.minimum(1.0, CLIP_NORM / (grad_norm + 1e-06))
    states = ((embed_m, embed_v), (up_m, up_v), (down_m, down_v), (qkv_m, qkv_v), (out_m, out_v), (fc_m, fc_v), (proj_m, proj_v), (norm_m, norm_v))
    results = []
    for index in range(8):
        rate = NORM_RATE if index == 7 else MATRIX_RATE
        decay = 0.0 if index == 7 else WEIGHT_DECAY
        results.append(adam_update(params[index], factor * grads[index], states[index][0], states[index][1], rate, decay))
    embed_first, embed_second, embed_next = results[0]
    up_first, up_second, up_next = results[1]
    down_first, down_second, down_next = results[2]
    qkv_first, qkv_second, qkv_next = results[3]
    out_first, out_second, out_next = results[4]
    fc_first, fc_second, fc_next = results[5]
    proj_first, proj_second, proj_next = results[6]
    norm_first, norm_second, norm_next = results[7]
    return (loss_sum, weight_total, grad_norm, embed_first, embed_second, embed_next, up_first, up_second, up_next, down_first, down_second, down_next, qkv_first, qkv_second, qkv_next, out_first, out_second, out_next, fc_first, fc_second, fc_next, proj_first, proj_second, proj_next, norm_first, norm_second, norm_next)
```

```python
import functools
import math

import jax
import jax.numpy as jnp
import numpy as np
from jax import lax
from jax.experimental import pallas as pl
from jax.experimental.pallas import tpu as pltpu
from jax.sharding import PartitionSpec as P

HEAD_DIM = 64
NB = 16
T_STEPS = 2000
STEP = 10

NORM_EPS = 1e-05
MASKED = -1e30
BETA_FIRST = 0.9
BETA_SECOND = 0.999
ADAM_EPS = 1e-08
MATRIX_RATE = 0.05
NORM_RATE = 0.5
WEIGHT_DECAY = 0.1
CLIP_NORM = 0.01

TILE = 256
SPAN = 128
WINDOW = 384
MESH = pl.DeviceIdType.MESH
F32 = jnp.float32
BF16 = jnp.bfloat16
VMEM_LIMIT = 62 * 2**20


def nn(left, right):
    return jnp.dot(left, right, preferred_element_type=F32)


def nt(left, right):
    return lax.dot_general(
        left, right, (((1,), (1,)), ((), ())), preferred_element_type=F32
    )


def sinusoid(where, width):
    half = width // 2
    freqs = jnp.exp(-math.log(10000.0) * jnp.arange(half, dtype=F32) / half)
    angles = where[:, None] * freqs[None, :]
    return jnp.concatenate([jnp.sin(angles), jnp.cos(angles)], axis=-1)


def place_table(length, width):
    half = width // 2
    freqs = np.exp(-math.log(10000.0) * np.arange(half, dtype=np.float64) / half)
    angles = np.arange(length, dtype=np.float64)[:, None] * freqs[None, :]
    return np.concatenate([np.sin(angles), np.cos(angles)], axis=-1).astype(np.float32)


def norm_stats(values):
    width = values.shape[-1]
    center = values - jnp.sum(values, axis=-1, keepdims=True) * (1.0 / width)
    spread = jnp.sum(center * center, axis=-1, keepdims=True) * (1.0 / width)
    rate = lax.rsqrt(spread + NORM_EPS)
    return center * rate, rate


def norm_back(unit, rate, gain, upstream):
    width = unit.shape[-1]
    scaled = upstream * gain
    first = jnp.sum(scaled, axis=-1, keepdims=True) * (1.0 / width)
    second = jnp.sum(scaled * unit, axis=-1, keepdims=True) * (1.0 / width)
    return rate * (scaled - first - unit * second)


def column_sum(values):
    return jnp.sum(values, axis=0, keepdims=True)


def rows_at(index, count):
    return pl.ds(pl.multiple_of(index * count, count), count)


def guarded(condition, action):
    if condition is None:
        action()
    else:
        pl.when(condition)(action)


def position():
    me = lax.axis_index("dp")
    return me, lax.axis_index("mp"), me // 4, lax.rem(me // 2, 2), lax.rem(me, 2)


def index_of(z, y, x):
    return z * 4 + y * 2 + x


def neighbours():
    me, core, z, y, x = position()
    up = (jnp.minimum(me + 4, 15), core)
    down = (jnp.maximum(me - 4, 0), core)
    across_x = (index_of(z, y, 1 - x), core)
    across_y = (index_of(z, 1 - y, x), core)
    return up, down, across_x, across_y, (me, 1 - core)


def remote(source, target, send_sem, recv_sem, device):
    return pltpu.make_async_remote_copy(
        src_ref=source,
        dst_ref=target,
        send_sem=send_sem,
        recv_sem=recv_sem,
        device_id=device,
        device_id_type=MESH,
    )


def meet(devices):
    me, core = position()[:2]
    barrier = pltpu.get_barrier_semaphore()
    for device in devices:

        @pl.when(jnp.logical_or(device[0] != me, device[1] != core))
        def greet():
            pl.semaphore_signal(barrier, inc=1, device_id=device, device_id_type=MESH)

    pl.semaphore_wait(barrier, len(devices) - 1)


class Exchange:
    def __init__(self, source, slots, send_sems, recv_sems, devices):
        self.source, self.slots = source, slots
        self.send_sems, self.recv_sems = send_sems, recv_sems
        me, core = position()[:2]
        self.devices = [
            (slot, device, jnp.logical_or(device[0] != me, device[1] != core))
            for slot, device in enumerate(devices)
        ]
        self.mine = me if len(devices) == 16 else 2 * me + core

    def copy(self, slot, device):
        return remote(
            self.source, self.slots.at[self.mine], self.send_sems.at[slot], self.recv_sems.at[self.mine], device
        )

    def start(self):
        for slot, device, other in self.devices:
            guarded(other, lambda: self.copy(slot, device).start())

    def arrive(self):
        for slot, device, other in self.devices:

            def wait():
                remote(
                    self.slots.at[slot], self.slots.at[slot], self.send_sems.at[slot], self.recv_sems.at[slot], device
                ).wait_recv()

            guarded(other, wait)

    def total(self):
        self.slots[self.mine] = self.source[...]
        value = self.slots[0]
        for slot in range(1, len(self.devices)):
            value = value + self.slots[slot]
        return value

    def finish(self):
        for slot, device, other in self.devices:
            guarded(other, lambda: self.copy(slot, device).wait_send())


def same_core():
    core = position()[1]
    return [(d, core) for d in range(16)]


def every_device():
    return [(d, c) for d in range(16) for c in range(2)]


class Gather:
    def __init__(self, shard, whole, sems, rows, swapped):
        self.shard, self.whole, self.rows, self.swapped = shard, whole, rows, swapped
        (self.local_s, self.up_s, self.down_s, self.x_s, self.y_s, self.pair_s, self.recv, self.pair_recv) = sems
        self.up, self.down, self.xn, self.yn, self.pair = neighbours()
        self.me, self.core, self.z, self.y, self.x = position()
        self.sends = []

    def piece(self, b, c, d):
        return self.whole.at[b, c, rows_at(d, self.rows), :]

    def send(self, b, d, own, device, sem, condition=None, to_pair=False):
        source = self.shard.at[b] if own else self.piece(b, self.core, d)
        recv = self.pair_recv if to_pair else self.recv

        def copy():
            return remote(source, self.piece(b, self.core, d), sem, recv.at[b, d], device)

        self.sends.append((condition, copy))
        guarded(condition, lambda: copy().start())

    def arrive(self, b, c, d, recv):
        remote(self.piece(b, c, d), self.piece(b, c, d), self.pair_s.at[b, d], recv.at[b, d], self.pair).wait_recv()

    def first_second(self, b):
        if self.swapped(b):
            return (self.yn, self.y_s), (self.xn, self.x_s)
        return (self.xn, self.x_s), (self.yn, self.y_s)

    def spread(self, b, d, zz, own=False, condition=None):
        (first, first_s), (second, second_s) = self.first_second(b)
        self.send(b, d, own, first, first_s.at[b, zz], condition)
        self.send(b, d, own, second, second_s.at[b, 4 + zz], condition)
        self.send(b, d, own, self.pair, self.pair_s.at[b, d], condition, True)

    def local(self, b):
        return pltpu.make_async_copy(self.shard.at[b], self.piece(b, self.core, self.me), self.local_s.at[b])

    def begin(self, b):
        self.local(b).start()
        self.send(b, self.me, True, self.up, self.up_s.at[b, 0], self.z < 3)
        self.send(b, self.me, True, self.down, self.down_s.at[b, 0], self.z > 0)
        self.spread(b, self.me, self.z, True)

    def hop(self, b, distance):
        z = self.z
        for sign in (1, -1):
            if sign == 1:
                source, there, onward = jnp.maximum(z - distance, 0), z >= distance, z < 3
                device, sem = self.up, self.up_s
            else:
                source, there, onward = jnp.minimum(z + distance, 3), z + distance <= 3, z > 0
                device, sem = self.down, self.down_s
            d = index_of(source, self.y, self.x)
            guarded(there, lambda: self.arrive(b, self.core, d, self.recv))
            if distance < 3:
                self.send(b, d, False, device, sem.at[b, distance], jnp.logical_and(there, onward))
            self.spread(b, d, source, False, there)

    def turn(self, b):
        second, second_s = self.first_second(b)[1]
        yy, xx = (1 - self.y, self.x) if self.swapped(b) else (self.y, 1 - self.x)
        for zz in range(4):
            d = index_of(zz, yy, xx)
            self.arrive(b, self.core, d, self.recv)
            self.send(b, d, False, second, second_s.at[b, zz])
            self.send(b, d, False, self.pair, self.pair_s.at[b, d], None, True)

    def last(self, b):
        yy, xx = (self.y, 1 - self.x) if self.swapped(b) else (1 - self.y, self.x)
        for zz in range(4):
            for d in (index_of(zz, yy, xx), index_of(zz, 1 - self.y, 1 - self.x)):
                self.arrive(b, self.core, d, self.recv)
                self.send(b, d, False, self.pair, self.pair_s.at[b, d], None, True)

    def ready(self, b):
        self.local(b).wait()
        for d in range(16):
            self.arrive(b, 1 - self.core, d, self.pair_recv)

    def finish(self):
        for condition, copy in self.sends:
            guarded(condition, lambda copy=copy: copy().wait_send())


def gather_sems(count):
    dma = pltpu.SemaphoreType.DMA
    return [dma((count,)), dma((count, 4)), dma((count, 4)), dma((count, 8)), dma((count, 8)), dma((count, 16)), dma((count, 16)), dma((count, 16))]


class Scatter:
    def __init__(self, own, landed, loaded, near, far, base, stage, risen, fallen, out, sems, rows, swapped):
        self.own, self.landed, self.loaded, self.near, self.far = own, landed, loaded, near, far
        self.base, self.stage, self.risen, self.fallen, self.out = base, stage, risen, fallen, out
        (self.pair_s, self.pair_r, self.load_s, self.near_s, self.near_r, self.far_s, self.far_r, self.line_s, self.risen_r, self.fallen_r) = sems
        self.rows, self.swapped = rows, swapped
        self.up, self.down, self.xn, self.yn, self.pair = neighbours()
        self.me, self.core, self.z, self.y, self.x = position()

    def piece(self, b, zz, yy, xx):
        return self.own.at[b, rows_at(index_of(zz, yy, xx), self.rows), :]

    def pair_copy(self, b, source):
        return remote(source, self.landed.at[b], self.pair_s.at[b], self.pair_r.at[b], self.pair)

    def near_copy(self, b, zz, i):
        if self.swapped(b):
            place, device = (zz, i, 1 - self.x), self.xn
        else:
            place, device = (zz, 1 - self.y, i), self.yn
        return remote(
            self.piece(b, *place), self.near.at[b, zz, i], self.near_s.at[b, zz, i], self.near_r.at[b, zz, i], device
        )

    def far_place(self, b, zz):
        return (zz, 1 - self.y, self.x) if self.swapped(b) else (zz, self.y, 1 - self.x)

    def far_copy(self, b, zz):
        return remote(
            self.piece(b, *self.far_place(b, zz)), self.far.at[b, zz], self.far_s.at[b, zz], self.far_r.at[b, zz],
            self.yn if self.swapped(b) else self.xn,
        )

    def rise(self, b, t):
        return remote(self.stage.at[b, t], self.risen.at[b, t], self.line_s.at[b, t], self.risen_r.at[b, t], self.up)

    def fall(self, b, t):
        return remote(self.stage.at[b, t], self.fallen.at[b, t], self.line_s.at[b, t], self.fallen_r.at[b, t], self.down)

    def first(self, b):
        self.pair_copy(b, self.own.at[b]).wait_recv()
        load = pltpu.make_async_copy(self.landed.at[b], self.loaded, self.load_s.at[0])
        load.start()
        load.wait()

        def add(d, carry):
            at = rows_at(d, self.rows)
            self.own[b, at, :] = (self.own[b, at, :].astype(F32) + self.loaded[at, :].astype(F32)).astype(self.own.dtype)
            return carry

        lax.fori_loop(0, 16, add, 0)
        for zz in range(4):
            for i in range(2):
                self.near_copy(b, zz, i).start()

    def second(self, b):
        i = 1 - self.y if self.swapped(b) else 1 - self.x
        for zz in range(4):
            for j in range(2):
                self.near_copy(b, zz, j).wait_recv()
            place = self.far_place(b, zz)
            value = self.piece(b, *place)[...].astype(F32) + self.near[b, zz, i].astype(F32)
            self.piece(b, *place)[...] = value.astype(self.own.dtype)
            self.far_copy(b, zz).start()

    def line(self, b):
        z = self.z
        i = self.y if self.swapped(b) else self.x
        for zz in range(4):
            self.far_copy(b, zz).wait_recv()
            piece = self.piece(b, zz, self.y, self.x)[...].astype(F32)
            self.base[zz] = piece + self.near[b, zz, i].astype(F32) + self.far[b, zz].astype(F32)
        for t in (3, 2, 1):

            @pl.when(z < t)
            def going_up():
                @pl.when(z > 0)
                def add():
                    self.rise(b, t).wait_recv()
                    self.base[t] += self.risen[b, t].astype(F32)

                self.stage[b, t] = self.base[t].astype(self.stage.dtype)
                self.rise(b, t).start()

        for t in (0, 1, 2):

            @pl.when(z > t)
            def going_down():
                @pl.when(z < 3)
                def add():
                    self.fall(b, t).wait_recv()
                    self.base[t] += self.fallen[b, t].astype(F32)

                self.stage[b, t] = self.base[t].astype(self.stage.dtype)
                self.fall(b, t).start()

        self.out[b] = self.base[z]

    def result(self, b):
        z = self.z

        @pl.when(z > 0)
        def from_below():
            self.rise(b, z).wait_recv()
            self.out[b] += self.risen[b, z].astype(F32)

        @pl.when(z < 3)
        def from_above():
            self.fall(b, z).wait_recv()
            self.out[b] += self.fallen[b, z].astype(F32)

        value = self.out[b]
        return jnp.sum(value * value, keepdims=True)

    def finish(self, b):
        for zz in range(4):
            for i in range(2):
                self.near_copy(b, zz, i).wait_send()
            self.far_copy(b, zz).wait_send()
            guarded(self.z != zz, lambda: self.rise(b, zz).wait_send())


SCATTER_REFS = 18


def scatter_scratch(count, rows, columns):
    dma, vmem = pltpu.SemaphoreType.DMA, pltpu.VMEM
    return [
        vmem((count, 16 * rows, columns), BF16),
        vmem((16 * rows, columns), BF16),
        vmem((count, 4, 2, rows, columns), BF16),
        vmem((count, 4, rows, columns), BF16),
        vmem((4, rows, columns), F32),
        vmem((count, 4, rows, columns), BF16),
        vmem((count, 4, rows, columns), BF16),
        vmem((count, 4, rows, columns), BF16),
        dma((count,)), dma((count,)), dma((1,)), dma((count, 4, 2)), dma((count, 4, 2)),
        dma((count, 4)), dma((count, 4)), dma((count, 4)), dma((count, 4)), dma((count, 4)),
    ]


def scatter_of(refs, landed, out, rows, swapped):
    own, loaded, near, far, base, stage, risen, fallen = refs[:8]
    return Scatter(own, landed, loaded, near, far, base, stage, risen, fallen, out, refs[8:], rows, swapped)


def gelu_parts(values):
    root = 0.7978845608028654
    square = values * values
    bent = jnp.tanh(root * (values + 0.044715 * (square * values)))
    half = 0.5 * (1.0 + bent)
    slope = half + (0.5 * root) * values * (1.0 - bent * bent) * (1.0 + (3 * 0.044715) * square)
    return values * half, slope


def halves_of(shape, axis, scale):
    low = lax.broadcasted_iota(jnp.int32, shape, axis) < HEAD_DIM
    return jnp.where(low, scale, 0.0).astype(BF16), jnp.where(low, 0.0, scale).astype(BF16)


def pick_halves(wide):
    low = lax.broadcasted_iota(jnp.int32, (2 * HEAD_DIM, SPAN), 0) < HEAD_DIM
    return jnp.where(low, wide[:, :SPAN], wide[:, SPAN:])


def window_start(block, blocks):
    return min(max(block - 1, 0), blocks - WINDOW // SPAN) * SPAN


def forward_kernel(fused, shapes, *refs):
    length, width, pairs = shapes
    blocks = length // SPAN
    tiles = length // TILE
    (
        shard, count_in, tok, seg_col, seg_row, noise, embed3, up_low, norms, places, time_row, mix,
        whole, count_out, start, noisy, zero_out, one_out, two_out, qkv_out, keyt_out, att_out, probs_out, act_out, slope_out, first_t_out, second_t_out,
        h_zero, h_one, h_two, normed, normed_t, qkv, key_t, value_t, att, probs, act, slope, weights, bias,
        out_sems, probs_sems, weight_sems,
    ) = refs[:44]
    core = lax.axis_index("mp")
    saves = []

    def save(source, target):
        copy = pltpu.make_async_copy(source, target, out_sems.at[len(saves)])
        copy.start()
        saves.append(copy)

    if fused:
        rest = refs[44:]
        gather = Gather(shard, whole, rest[:8], shard.shape[1], lambda b: b % 2 == 1)
        counts, count_send, count_recv = rest[8:]
        meet(same_core() + [neighbours()[4]])
        exchange = Exchange(count_in, counts, count_send, count_recv, same_core())
        exchange.start()
        for b in range(6):
            gather.begin(b)
    else:
        gather = None

    def pump(*steps):
        if gather is not None:
            for name, b, *more in steps:
                getattr(gather, name)(b, *more)

    def load(b, c, slot):
        return pltpu.make_async_copy((whole if fused else shard).at[b, c], weights.at[slot], weight_sems.at[slot])

    def embed_tile(r):
        at = rows_at(r, TILE)
        hot = (tok[at, :] == lax.broadcasted_iota(jnp.int32, (TILE, embed3.shape[0]), 1)).astype(F32).astype(BF16)
        thirds = nn(hot, embed3[...])
        e = thirds.shape[1] // 3
        first = thirds[:, :e] + thirds[:, e : 2 * e] + thirds[:, 2 * e :]
        start[at, :] = first
        low = (mix[0, 0] * first + mix[0, 1] * noise[at, :]).astype(BF16)
        noisy[at, :] = low
        hidden = nn(low, up_low[...]) + places[at, :] + time_row[...]
        h_zero[at, :] = hidden
        unit = norm_stats(hidden)[0]
        scaled = unit * norms[0:1, :] + norms[1:2, :]
        normed[at, :] = scaled.astype(BF16)
        normed_t[0, :, at] = scaled.T.astype(BF16)

    steps = [
        [("hop", 0, 1), ("hop", 1, 1), ("hop", 2, 1), ("hop", 3, 1)],
        [("hop", 4, 1), ("hop", 5, 1), ("hop", 0, 2), ("hop", 1, 2)],
        [("hop", 2, 2), ("hop", 3, 2), ("hop", 0, 3), ("hop", 1, 3)],
        [("hop", 4, 2), ("hop", 5, 2), ("turn", 0), ("turn", 1)],
    ]
    for r in range(tiles):
        embed_tile(r)
        if r < 4:
            pump(*steps[r])
    save(h_zero, zero_out)
    save(normed_t.at[0], first_t_out)
    for i in range(blocks):
        w0 = window_start(i, blocks)
        same = seg_col[w0 : w0 + WINDOW, :] == seg_row[:, i * SPAN : (i + 1) * SPAN]
        bias[i] = jnp.where(same, 0.0, MASKED)
    pump(("hop", 2, 3), ("hop", 3, 3), ("hop", 4, 3), ("hop", 5, 3), ("last", 0), ("last", 1), ("turn", 2), ("turn", 3))
    pump(("ready", 0), ("ready", 1))
    for b in range(2):
        for c in range(2):
            load(b, c, 2 * b + c).start()
    for b in range(2):
        for c in range(2):
            load(b, c, 2 * b + c).wait()
    half = width // 2
    for c in range(2):

        def project(r, carry):
            at = rows_at(r, TILE)
            rows = normed[at, :]
            first = nn(rows, weights[c])
            values = nn(rows, weights[2 + c, :, :half])
            cols = slice(c * half, (c + 1) * half)
            qkv[0, at, cols] = first[:, :half].astype(BF16)
            qkv[1, at, cols] = first[:, half:].astype(BF16)
            qkv[2, at, cols] = values.astype(BF16)
            key_t[cols, at] = first[:, half:].T.astype(BF16)
            value_t[cols, at] = values.T.astype(BF16)
            return carry

        lax.fori_loop(0, tiles, project, 0)
    for j in range(3):
        save(qkv.at[j], qkv_out.at[j])
    save(key_t, keyt_out)

    def probs_copy(pair, slot):
        return pltpu.make_async_copy(probs.at[slot], probs_out.at[pl.ds(pair * blocks, blocks)], probs_sems.at[slot])

    low, high = halves_of((1, SPAN), 1, 0.125)

    def attend(pair, carry):
        slot = lax.rem(pair, 2)
        cols = pl.ds(pl.multiple_of(pair * SPAN, SPAN), SPAN)

        @pl.when(pair >= 2)
        def free():
            probs_copy(pair - 2, slot).wait()

        for i in range(blocks):
            w0 = window_start(i, blocks)
            queries = qkv[0, i * SPAN : (i + 1) * SPAN, cols]
            both = jnp.concatenate([queries * low, queries * high], axis=0)
            scores = nt(qkv[1, w0 : w0 + WINDOW, cols], both)
            mask = bias[i]
            scores = scores + jnp.concatenate([mask, mask], axis=1)
            most = jnp.max(scores, axis=0, keepdims=True)
            raised = jnp.exp(scores - most)
            share = 1.0 / jnp.sum(raised, axis=0, keepdims=True)
            prob = (raised * share).astype(BF16)
            probs[slot, i] = prob
            mixed = nn(value_t[cols, w0 : w0 + WINDOW], prob)
            att[i * SPAN : (i + 1) * SPAN, cols] = pick_halves(mixed).T.astype(BF16)
        probs_copy(pair, slot).start()
        return carry

    middle = [[("turn", 4), ("turn", 5)], [("last", 2), ("last", 3)], []]
    for step in range(3):
        lax.fori_loop(step * pairs // 3, (step + 1) * pairs // 3, attend, 0)
        pump(*middle[step])
    for pair in (pairs - 2, pairs - 1):
        probs_copy(pair, pair % 2).wait()
    save(att, att_out)

    def after_attention(r, carry):
        at = rows_at(r, TILE)
        mixed = att[at, :]
        total = nt(mixed[:, :half], weights[2, :, half:]) + nt(mixed[:, half:], weights[3, :, half:])
        hidden = h_zero[at, :] + total
        h_one[at, :] = hidden
        unit = norm_stats(hidden)[0]
        scaled = unit * norms[2:3, :] + norms[3:4, :]
        normed[at, :] = scaled.astype(BF16)
        normed_t[1, :, at] = scaled.T.astype(BF16)
        return carry

    lax.fori_loop(0, tiles, after_attention, 0)
    save(h_one, one_out)
    save(normed_t.at[1], second_t_out)
    pump(("ready", 2), ("ready", 3))
    for h in range(2):
        for c in range(2):
            load(2 + h, c, 4 + 2 * h + c).start()
    for j in range(4):
        load(2 + j // 2, j % 2, 4 + j).wait()

        def grow(r, carry):
            at = rows_at(r, TILE)
            before = nn(normed[at, :], weights[4 + j])
            active, bend = gelu_parts(before)
            act[j, at, :] = active.astype(BF16)
            slope[j, at, :] = bend.astype(BF16)
            return carry

        lax.fori_loop(0, tiles, grow, 0)
        save(act.at[j], act_out.at[j])
        save(slope.at[j], slope_out.at[j])
        if j == 1:
            pump(("last", 4), ("last", 5))
    pump(("ready", 4), ("ready", 5))
    for h in range(2):
        for c in range(2):
            load(4 + h, c, 2 * h + c).start()
    for j in range(4):
        load(4 + j // 2, j % 2, j).wait()

    def shrink(r, carry):
        at = rows_at(r, TILE)
        total = h_one[at, :]
        for j in range(4):
            total = total + nt(act[j, at, :], weights[j])
        h_two[at, :] = total
        return carry

    lax.fori_loop(0, tiles, shrink, 0)
    save(h_two, two_out)
    if fused:
        exchange.arrive()
        count_out[...] = exchange.total()
        gather.finish()
        exchange.finish()
    else:
        count_out[...] = count_in[...]
    for copy in saves:
        copy.wait()


def run_forward(fused, source, count_in, tok, seg_col, seg_row, noise, embed3, up_low, norms, places, time_row, mix):
    length, width = places.shape
    pairs = width // SPAN
    blocks = length // SPAN
    dma, vmem = pltpu.SemaphoreType.DMA, pltpu.VMEM
    anywhere, inside = pl.BlockSpec(memory_space=pl.ANY), pl.BlockSpec(memory_space=pltpu.VMEM)
    emb = noise.shape[1]

    def made(shape, dtype=BF16):
        return jax.ShapeDtypeStruct(shape, dtype)

    out_shape = [
        made((6, 2, width, width)),
        made(count_in.shape, F32),
        made((length, emb), F32),
        made((length, emb)),
        made((length, width), F32),
        made((length, width), F32),
        made((length, width), F32),
        made((3, length, width)),
        made((width, length)),
        made((length, width)),
        made((pairs * blocks, WINDOW, 2 * SPAN)),
        made((4, length, width)),
        made((4, length, width)),
        made((width, length)),
        made((width, length)),
    ]
    scratch = [
        vmem((length, width), F32),
        vmem((length, width), F32),
        vmem((length, width), F32),
        vmem((length, width), BF16),
        vmem((2, width, length), BF16),
        vmem((3, length, width), BF16),
        vmem((width, length), BF16),
        vmem((width, length), BF16),
        vmem((length, width), BF16),
        vmem((2, blocks, WINDOW, 2 * SPAN), BF16),
        vmem((4, length, width), BF16),
        vmem((4, length, width), BF16),
        vmem((8, width, width), BF16),
        vmem((blocks, WINDOW, SPAN), F32),
        dma((20,)),
        dma((2,)),
        dma((8,)),
    ]
    if fused:
        scratch += gather_sems(6) + [vmem((16,) + count_in.shape, F32), dma((16,)), dma((16,))]
        params = pltpu.CompilerParams(collective_id=0, has_side_effects=True, vmem_limit_bytes=VMEM_LIMIT)
    else:
        params = pltpu.CompilerParams(vmem_limit_bytes=VMEM_LIMIT)
    results = pl.pallas_call(
        functools.partial(forward_kernel, fused, (length, width, pairs)),
        out_shape=out_shape,
        in_specs=[anywhere] + [inside] * 10 + [pl.BlockSpec(memory_space=pltpu.SMEM)],
        out_specs=[anywhere, inside, inside, inside] + [anywhere] * 11,
        scratch_shapes=scratch,
        compiler_params=params,
        name="forward",
    )(source, count_in, tok, seg_col, seg_row, noise, embed3, up_low, norms, places, time_row, mix)
    return results


def backward_kernel(fused, shapes, *refs):
    length, width, pairs = shapes
    blocks = length // SPAN
    tiles = length // TILE
    half = width // 2
    (
        whole, columns, start, noisy, zero_in, one_in, two_in, qkv_in, keyt_in, att_in, probs_in, act_in, slope_in, first_t_in, second_t_in,
        embed_low, pad_row, up_low, down_low, norms, mix,
        out_blocks, out_small, out_loss, landed, small_landed,
        hidden, grad, back, branch, branch_t, normed_t, pre, slots, weights, acc, probs, error, small, norm_grads, posted, small_own, scalars,
        load_sems, slot_sems, weight_sems, probs_sems, post_sems,
    ) = refs[:48]
    core = lax.axis_index("mp")
    emb = start.shape[1]
    vocab = embed_low.shape[0]
    side = width // TILE

    if fused:
        rest = refs[48:]
        main_refs, rest = rest[:SCATTER_REFS], rest[SCATTER_REFS:]
        tiny_refs, rest = rest[:SCATTER_REFS], rest[SCATTER_REFS:]
        tiny_shard, tiny_whole, tiny_out, slots_all, all_send, all_recv = rest[:6]
        gather_refs = rest[6:]
        main = scatter_of(main_refs, landed, out_blocks, width // 16, lambda b: b in (1, 4, 5))
        tiny = scatter_of(tiny_refs, small_landed, tiny_out, 16, lambda b: False)
        own, tiny_own = main.own, tiny.own
        devices = every_device()
        meet(devices)
    else:
        own = small_own = None

    def pump(*steps):
        if fused:
            for name, b in steps:
                getattr(main, name)(b)

    def post(b, slot):
        if fused:
            main.pair_copy(b, posted.at[slot]).start()
        else:
            pltpu.make_async_copy(posted.at[slot], out_blocks.at[b, 1 - core], post_sems.at[slot]).start()

    def posted_wait(b, slot):
        if fused:
            main.pair_copy(b, posted.at[slot]).wait_send()
        else:
            pltpu.make_async_copy(posted.at[slot], out_blocks.at[b, 1 - core], post_sems.at[slot]).wait()

    def fetch(source, target, k):
        copy = pltpu.make_async_copy(source, target, load_sems.at[k])
        copy.start()
        return copy

    def load_weights(b, c, slot):
        return pltpu.make_async_copy(whole.at[b, c], weights.at[slot], weight_sems.at[slot])

    def load_slot(source, slot):
        return pltpu.make_async_copy(source, slots.at[slot], slot_sems.at[slot])

    def feed(s):
        h, c = s // 2, (1 - core if s % 2 == 0 else core)
        first = 2 * (s % 2)
        return [
            load_weights(2 + h, c, first),
            load_weights(4 + h, c, first + 1),
            load_slot(act_in.at[2 * h + c], first),
            load_slot(slope_in.at[2 * h + c], first + 1),
        ]

    two_copy = fetch(two_in, hidden, 0)
    normed_copy = fetch(second_t_in, normed_t, 1)
    for copy in feed(0):
        copy.start()
    norm_grads[...] = jnp.zeros(norm_grads.shape, F32)
    small[...] = jnp.zeros(small.shape, F32)
    two_copy.wait()
    ids = lax.broadcasted_iota(jnp.int32, (TILE, vocab), 1).astype(F32)
    d0, u0, e0 = 0, width, 2 * width

    def add_norm(row, upstream, unit):
        norm_grads[row : row + 1, :] += column_sum(upstream * unit)
        norm_grads[row + 1 : row + 2, :] += column_sum(upstream)

    def head(r, loss):
        at = rows_at(r, TILE)
        unit, rate = norm_stats(hidden[at, :])
        ended = (unit * norms[4:5, :] + norms[5:6, :]).astype(BF16)
        predicted = nn(ended, down_low[...])
        pred_low = predicted.astype(BF16)
        logits = nt(pred_low, embed_low[...]) + pad_row[...]
        most = jnp.max(logits, axis=-1, keepdims=True)
        raised = jnp.exp(logits - most)
        total = jnp.sum(raised, axis=-1, keepdims=True)
        hit = columns[at, 0:1] == ids
        picked = jnp.sum(jnp.where(hit, logits, 0.0), axis=-1, keepdims=True)
        miss = predicted - start[at, :]
        per_token = jnp.sum(miss * miss, axis=-1, keepdims=True) * (1.0 / emb) + (jnp.log(total) + most) - picked
        loss = loss + jnp.sum(columns[at, 1:2] * per_token, keepdims=True)
        coef = columns[at, 2:3]
        grad_logits = (coef * (raised * (1.0 / total) - jnp.where(hit, 1.0, 0.0))).astype(BF16)
        grad_error = coef * 2.0 * miss * (1.0 / emb)
        error[at, :] = grad_error
        grad_pred = nn(grad_logits, embed_low[...]) + grad_error
        grad_pred_low = grad_pred.astype(BF16)
        small[:, d0 : d0 + width] += nn(grad_pred.T.astype(BF16), ended)
        small[:, e0 : e0 + vocab] += nn(predicted.T.astype(BF16), grad_logits)
        upstream = nt(grad_pred_low, down_low[...])
        add_norm(4, upstream, unit)
        result = norm_back(unit, rate, norms[4:5, :], upstream)
        grad[at, :] = result
        branch[at, :] = result.astype(BF16)
        branch_t[:, at] = result.T.astype(BF16)
        return loss

    loss = lax.fori_loop(0, tiles, head, jnp.zeros((1, 1), F32))
    one_copy = fetch(one_in, hidden, 0)
    normed_copy.wait()

    for s in range(4):
        h = s // 2
        if s < 3:
            for copy in feed(s + 1):
                copy.start()
        for copy in feed(s):
            copy.wait()
        first = 2 * (s % 2)
        fc, proj, active, bend = weights.at[first], weights.at[first + 1], slots.at[first], slots.at[first + 1]

        def slide(r, carry):
            at = rows_at(r, TILE)
            through = nn(branch[at, :], proj[...])
            pushed = (through * bend[at, :].astype(F32)).astype(BF16)
            pre[at, :] = pushed
            value = nt(pushed, fc[...])
            if s == 0:
                back[at, :] = value
            else:
                back[at, :] += value
            return carry

        lax.fori_loop(0, tiles, slide, 0)
        mine = s % 2 == 1
        if s == 2:
            posted_wait(2, 0)
            posted_wait(4, 1)

        def weigh(m, carry):
            at = rows_at(m, TILE)
            fc_grad = nn(normed_t[at, :], pre[...]).astype(BF16)
            proj_grad = nn(branch_t[at, :], active[...]).astype(BF16)
            if mine and fused:
                own[2 + h, at, :] = fc_grad
                own[4 + h, at, :] = proj_grad
            else:
                posted[2 if mine else 0, at, :] = fc_grad
                posted[3 if mine else 1, at, :] = proj_grad
            return carry

        if mine and not fused and s == 3:
            for slot, b in ((2, 2), (3, 4)):
                pltpu.make_async_copy(posted.at[slot], out_blocks.at[b, core], post_sems.at[slot]).wait()
        lax.fori_loop(0, side, weigh, 0)
        if not mine:
            post(2 + h, 0)
            post(4 + h, 1)
        elif not fused:
            for slot, b in ((2, 2 + h), (3, 4 + h)):
                pltpu.make_async_copy(posted.at[slot], out_blocks.at[b, core], post_sems.at[slot]).start()
        if s == 1:
            pump(("first", 2), ("first", 4))
        if s == 2:
            pump(("second", 2), ("second", 4))
        if s == 3:
            pump(("first", 3), ("first", 5))

    for c in range(2):
        load_weights(0, c, c).start()
        load_weights(1, c, 2 + c).start()
    att_copy = fetch(att_in, pre, 2)
    first_t_copy = fetch(first_t_in, normed_t, 1)
    load_slot(qkv_in.at[0], 0).start()
    load_slot(qkv_in.at[2], 2).start()
    one_copy.wait()

    def through_two(r, carry):
        at = rows_at(r, TILE)
        unit, rate = norm_stats(hidden[at, :])
        upstream = back[at, :]
        add_norm(2, upstream, unit)
        result = grad[at, :] + norm_back(unit, rate, norms[2:3, :], upstream)
        grad[at, :] = result
        branch[at, :] = result.astype(BF16)
        branch_t[:, at] = result.T.astype(BF16)
        return carry

    lax.fori_loop(0, tiles, through_two, 0)
    zero_copy = fetch(zero_in, hidden, 0)
    pump(("second", 3), ("second", 5), ("line", 2), ("line", 4))
    att_copy.wait()
    posted_wait(3, 0)
    posted_wait(5, 1)
    if not fused:
        for slot, b in ((2, 3), (3, 5)):
            pltpu.make_async_copy(posted.at[slot], out_blocks.at[b, core], post_sems.at[slot]).wait()

    def other_half(c):
        return pl.ds(pl.multiple_of(c * half, SPAN), half)

    def store(which, b, at, cols, value):
        if which == 1 and fused:
            own[b, at, cols] = value
        else:
            posted[2 * which + (1 - b), at, cols] = value

    def out_weigh(m, carry):
        at = rows_at(m, TILE)
        for which in range(2):
            c = core if which else 1 - core
            store(which, 1, at, slice(half, width), nn(branch_t[at, :], pre[:, other_half(c)]).astype(BF16))
        return carry

    lax.fori_loop(0, side, out_weigh, 0)
    for c in range(2):
        load_weights(0, c, c).wait()
        load_weights(1, c, 2 + c).wait()
    keyt_copy = fetch(keyt_in, branch_t, 3)

    def spread_att(r, carry):
        at = rows_at(r, TILE)
        rows = branch[at, :]
        for c in range(2):
            slots[3, at, c * half : (c + 1) * half] = nn(rows, weights[2 + c, :, half:]).astype(BF16)
        return carry

    lax.fori_loop(0, tiles, spread_att, 0)
    count = blocks // 2

    def probs_copy(unit):
        slot = lax.rem(unit, 2)
        return pltpu.make_async_copy(probs_in.at[pl.ds(unit * count, count)], probs.at[slot], probs_sems.at[slot])

    probs_copy(0).start()
    load_slot(qkv_in.at[0], 0).wait()
    load_slot(qkv_in.at[2], 2).wait()
    keyt_copy.wait()
    low, high = halves_of((1, SPAN), 1, 0.125)
    low_one, high_one = halves_of((1, SPAN), 1, 1.0)

    def attend(pair, carry):
        cols = pl.ds(pl.multiple_of(pair * SPAN, SPAN), SPAN)
        acc[...] = jnp.zeros(acc.shape, F32)
        for part in range(2):
            unit = 2 * pair + part

            @pl.when(unit + 1 < 2 * pairs)
            def ahead():
                probs_copy(unit + 1).start()

            probs_copy(unit).wait()
            for k in range(count):
                i = part * count + k
                w0 = window_start(i, blocks)
                here = slice(i * SPAN, (i + 1) * SPAN)
                there = slice(w0, w0 + WINDOW)
                up_rows = slots[3, here, cols]
                ups = jnp.concatenate([up_rows * low_one, up_rows * high_one], axis=0)
                queries = slots[0, here, cols]
                asks = jnp.concatenate([queries * low, queries * high], axis=0)
                prob = probs[part, k]
                wide = prob.astype(F32)
                grad_probs = nt(slots[2, there, cols], ups)
                inner = jnp.sum(grad_probs * wide, axis=0, keepdims=True)
                grad_scores = (wide * (grad_probs - inner)).astype(BF16)
                acc[0, there, :] += nn(grad_scores, asks)
                acc[1, there, :] += nn(prob, ups)
                asked = nn(branch_t[cols, there], grad_scores)
                slots[0, here, cols] = (pick_halves(asked).T * 0.125).astype(BF16)
        slots[1, :, cols] = acc[0].astype(BF16)
        slots[2, :, cols] = acc[1].astype(BF16)
        return carry

    middle = [[("line", 3), ("line", 5)], [], []]
    for step in range(3):
        lax.fori_loop(step * pairs // 3, (step + 1) * pairs // 3, attend, 0)
        pump(*middle[step])
    first_t_copy.wait()

    def qkv_weigh(which):
        c = core if which else 1 - core
        cols = other_half(c)

        def body(m, carry):
            at = rows_at(m, TILE)
            rows = normed_t[at, :]
            store(which, 1, at, slice(0, half), nn(rows, slots[2, :, cols]).astype(BF16))
            store(which, 0, at, slice(0, half), nn(rows, slots[0, :, cols]).astype(BF16))
            store(which, 0, at, slice(half, width), nn(rows, slots[1, :, cols]).astype(BF16))
            return carry

        lax.fori_loop(0, side, body, 0)

    qkv_weigh(0)
    post(1, 0)
    post(0, 1)
    qkv_weigh(1)
    if not fused:
        for slot, b in ((2, 1), (3, 0)):
            pltpu.make_async_copy(posted.at[slot], out_blocks.at[b, core], post_sems.at[slot]).start()
    zero_copy.wait()
    pump(("first", 1), ("first", 0))

    def through_one(r, carry):
        at = rows_at(r, TILE)
        upstream = jnp.zeros((TILE, width), F32)
        for c in range(2):
            cols = slice(c * half, (c + 1) * half)
            upstream = upstream + nt(slots[0, at, cols], weights[c, :, :half])
            upstream = upstream + nt(slots[1, at, cols], weights[c, :, half:])
            upstream = upstream + nt(slots[2, at, cols], weights[2 + c, :, :half])
        unit, rate = norm_stats(hidden[at, :])
        add_norm(0, upstream, unit)
        grad_zero = (grad[at, :] + norm_back(unit, rate, norms[0:1, :], upstream)).astype(BF16)
        small[:, u0 : u0 + width] += nn(noisy[at, :].astype(F32).T.astype(BF16), grad_zero)
        grad_start = (mix[0, 0] * nt(grad_zero, up_low[...]) - error[at, :]).T
        upper = grad_start.astype(BF16)
        lower = (grad_start - upper.astype(F32)).astype(BF16)
        hot = (columns[at, 0:1] == ids).astype(F32).astype(BF16)
        small[:, e0 : e0 + vocab] += nn(upper, hot) + nn(lower, hot)
        return carry

    lax.fori_loop(0, tiles, through_one, 0)
    lanes = emb
    n0 = e0 + vocab
    for k in range(6):
        for j in range(width // lanes):
            row = k * (width // lanes) + j
            small[row : row + 1, n0 : n0 + lanes] = norm_grads[k : k + 1, j * lanes : (j + 1) * lanes]
    if not fused:
        out_small[...] = small[...]
        out_loss[...] = jnp.broadcast_to(loss, out_loss.shape)
        posted_wait(1, 0)
        posted_wait(0, 1)
        for slot, b in ((2, 1), (3, 0)):
            pltpu.make_async_copy(posted.at[slot], out_blocks.at[b, core], post_sems.at[slot]).wait()
        return

    group = small.shape[1] // 4
    for q in range(4):
        value = small[:, q * group : (q + 1) * group].astype(BF16)
        rows = slice((q % 2) * small.shape[0], (q % 2 + 1) * small.shape[0])
        mine = core == q // 2

        @pl.when(mine)
        def keep():
            tiny.own[0, rows, :] = value

        @pl.when(jnp.logical_not(mine))
        def give():
            small_own[rows, :] = value

    give_copy = tiny.pair_copy(0, small_own)
    give_copy.start()
    pump(("second", 1), ("second", 0))
    tiny.first(0)
    squares = main.result(2) + main.result(4)
    squares = squares + main.result(3) + main.result(5)
    tiny.second(0)
    pump(("line", 1), ("line", 0))
    tiny.line(0)
    squares = squares + tiny.result(0)
    squares = squares + main.result(1) + main.result(0)
    row = lax.broadcasted_iota(jnp.int32, scalars.shape, 0)
    scalars[...] = jnp.where(row == 0, squares, jnp.where(row == 1, loss, 0.0))
    exchange = Exchange(scalars, slots_all, all_send, all_recv, devices)
    exchange.start()
    tiny_shard[0] = tiny_out[0].astype(BF16)
    gather = Gather(tiny_shard, tiny_whole, gather_refs, 16, lambda b: False)
    gather.begin(0)
    for distance in (1, 2, 3):
        gather.hop(0, distance)
    gather.turn(0)
    gather.last(0)
    gather.ready(0)
    exchange.arrive()
    out_loss[...] = exchange.total()
    for q in range(4):
        rows = slice((q % 2) * small.shape[0], (q % 2 + 1) * small.shape[0])
        out_small[:, q * group : (q + 1) * group] = tiny_whole[0, q // 2, rows, :].astype(F32)
    posted_wait(1, 0)
    posted_wait(0, 1)
    give_copy.wait_send()
    gather.finish()
    exchange.finish()
    for b in range(6):
        main.finish(b)
    tiny.finish(0)


def run_backward(fused, whole, columns, start, noisy, kept, embed_low, pad_row, up_low, down_low, norms, mix):
    zero, one, two, qkv, key_t, att, probs, act, slope, first_t, second_t = kept
    length, width = zero.shape
    pairs = width // SPAN
    blocks = length // SPAN
    emb, vocab = start.shape[1], embed_low.shape[0]
    dma, vmem = pltpu.SemaphoreType.DMA, pltpu.VMEM
    anywhere, inside = pl.BlockSpec(memory_space=pl.ANY), pl.BlockSpec(memory_space=pltpu.VMEM)
    spread = 2 * width + vocab + emb
    group = spread // 4
    rows = width // 16

    def made(shape, dtype=BF16):
        return jax.ShapeDtypeStruct(shape, dtype)

    blocks_out = made((6, rows, width), F32) if fused else made((6, 2, width, width))
    out_shape = [blocks_out, made((emb, spread), F32), made((8, 128), F32)]
    out_shape += [made((6, width, width)) if fused else made((8, 128)), made((1, 2 * emb, group)) if fused else made((8, 128))]
    scratch = [
        vmem((length, width), F32),
        vmem((length, width), F32),
        vmem((length, width), F32),
        vmem((length, width), BF16),
        vmem((width, length), BF16),
        vmem((width, length), BF16),
        vmem((length, width), BF16),
        vmem((4, length, width), BF16),
        vmem((4, width, width), BF16),
        vmem((2, length, SPAN), F32),
        vmem((2, blocks // 2, WINDOW, 2 * SPAN), BF16),
        vmem((length, emb), F32),
        vmem((emb, spread), F32),
        vmem((8, width), F32),
        vmem((2 if fused else 4, width, width), BF16),
        vmem((2 * emb, group), BF16),
        vmem((8, 128), F32),
        dma((4,)),
        dma((4,)),
        dma((4,)),
        dma((2,)),
        dma((4,)),
    ]
    if fused:
        scratch += scatter_scratch(6, rows, width) + scatter_scratch(1, 16, group)
        scratch += [
            vmem((1, 16, group), BF16),
            vmem((1, 2, 2 * emb, group), BF16),
            vmem((1, 16, group), F32),
            vmem((32, 8, 128), F32),
            dma((32,)),
            dma((32,)),
        ] + gather_sems(1)
        params = pltpu.CompilerParams(collective_id=1, has_side_effects=True, vmem_limit_bytes=VMEM_LIMIT)
    else:
        params = pltpu.CompilerParams(vmem_limit_bytes=VMEM_LIMIT)
    return pl.pallas_call(
        functools.partial(backward_kernel, fused, (length, width, pairs)),
        out_shape=out_shape,
        in_specs=[anywhere] + [inside] * 3 + [anywhere] * 11 + [inside] * 5 + [pl.BlockSpec(memory_space=pltpu.SMEM)],
        out_specs=[inside if fused else anywhere, inside, inside, anywhere, anywhere],
        scratch_shapes=scratch,
        compiler_params=params,
        name="backward",
    )(whole, columns, start, noisy, zero, one, two, qkv, key_t, att, probs, act, slope, first_t, second_t, embed_low, pad_row, up_low, down_low, norms, mix)[:3]


def adam_update(weight, grad, first, second, rate, decay):
    first_new = BETA_FIRST * first + (1.0 - BETA_FIRST) * grad
    second_new = BETA_SECOND * second + (1.0 - BETA_SECOND) * grad * grad
    first_hat = first_new / (1.0 - BETA_FIRST**STEP)
    second_hat = second_new / (1.0 - BETA_SECOND**STEP)
    weight_new = weight - rate * (first_hat / (jnp.sqrt(second_hat) + ADAM_EPS) + decay * weight)
    return (first_new, second_new, weight_new)


def per_device(fused, token_ids, segment_ids, timesteps, noise, bucket_ids, counted, embed, up_weight, down_weight, qkv_weight, out_weight, fc_weight, proj_weight, norm_params, embed_m, embed_v, up_m, up_v, down_m, down_v, qkv_m, qkv_v, out_m, out_v, fc_m, fc_v, proj_m, proj_v, norm_m, norm_v):
    row = lax.axis_index("mp")
    length = token_ids.shape[1]
    vocab, emb = embed.shape
    width = up_weight.shape[1]
    half = width // 2
    hidden = fc_weight.shape[1] // 2

    def my(array):
        return lax.dynamic_index_in_dim(array, row, 0, keepdims=False)

    live = counted.astype(F32)
    hot = (bucket_ids[..., None] == jnp.arange(NB)[None, None, :]).astype(F32)
    local_counts = jnp.sum(live[..., None] * hot, axis=(0, 1))
    tokens, segments, step, row_noise = my(token_ids), my(segment_ids), my(timesteps), my(noise)
    keep = 1.0 - jnp.sqrt(step.astype(F32) / T_STEPS + 0.0001)
    mix = jnp.stack([jnp.sqrt(keep), jnp.sqrt(1.0 - keep)])[None]
    time_row = sinusoid(step.astype(F32).reshape(1), width)
    places = jnp.asarray(place_table(length, width))
    up_low, down_low = up_weight.astype(BF16), down_weight.astype(BF16)
    padded = -(-vocab // 128) * 128
    table = jnp.pad(embed, ((0, padded - vocab), (0, 0)))
    upper = table.astype(BF16)
    rest = table - upper.astype(F32)
    middle = rest.astype(BF16)
    lower = (rest - middle.astype(F32)).astype(BF16)
    embed3 = jnp.concatenate([upper, middle, lower], axis=1)
    pad_row = jnp.where(jnp.arange(padded) < vocab, 0.0, MASKED).astype(F32)[None]

    out_t, proj_t = out_weight.T, proj_weight.T
    shard = jnp.stack(
        [
            jnp.concatenate([qkv_weight[0], qkv_weight[1]], axis=1),
            jnp.concatenate([qkv_weight[2], out_t], axis=1),
            fc_weight[:, :hidden],
            fc_weight[:, hidden:],
            proj_t[:, :hidden],
            proj_t[:, hidden:],
        ]
    ).astype(BF16)
    if fused:
        source = shard
    else:
        source = lax.all_gather(lax.all_gather(shard, "dp", axis=1, tiled=True), "mp", axis=1)
        local_counts = lax.psum(local_counts, "dp")
    count_in = jnp.zeros((8, 128), F32).at[0, :NB].set(local_counts)
    whole, count_out, start, noisy, *kept = run_forward(
        fused, source, count_in, tokens[:, None], segments[:, None], segments[None], row_noise, embed3, up_low, norm_params, places, time_row, mix
    )
    if not fused:
        whole = source
    counts = count_out[0, :NB]
    live_total = jnp.sum(counts)
    bucket_weight = live_total / (NB * jnp.maximum(counts, 1.0))
    weight_total = jnp.sum(counts * bucket_weight)
    scale = my(live) * jnp.sum(my(hot) * bucket_weight, axis=-1)
    columns = jnp.stack([tokens.astype(F32), scale, scale / weight_total], axis=1)
    blocks, small, loss = run_backward(fused, whole, columns, start, noisy, kept, upper, pad_row, up_low, down_low, norm_params, mix)
    if fused:
        squares, loss_sum = loss[0, 0], loss[1, 0]
    else:
        blocks = lax.psum_scatter(blocks.astype(F32), "mp", scatter_dimension=1, tiled=False)
        blocks = lax.psum_scatter(blocks, "dp", scatter_dimension=1, tiled=True)
        small, loss_sum = lax.psum((small, loss[0, 0]), ("dp", "mp"))
        squares = lax.psum(jnp.sum(blocks * blocks), ("dp", "mp")) + jnp.sum(small * small)
    grad_norm = jnp.sqrt(squares)
    factor = jnp.minimum(1.0, CLIP_NORM / (grad_norm + 1e-06))
    grad_down = small[:, :width].T
    grad_up = small[:, width : 2 * width]
    grad_embed = small[:, 2 * width : 2 * width + vocab].T
    grad_norms = small[: 6 * width // emb, 2 * width + padded :].reshape(6, width)
    grad_qkv = jnp.stack([blocks[0][:, :half], blocks[0][:, half:], blocks[1][:, :half]])
    grad_out = blocks[1][:, half:].T
    grad_fc = jnp.concatenate([blocks[2], blocks[3]], axis=1)
    grad_proj = jnp.concatenate([blocks[4], blocks[5]], axis=1).T
    results = [loss_sum, weight_total, grad_norm]
    for weight, grad, first, second, rate, decay in (
        (embed, grad_embed, embed_m, embed_v, MATRIX_RATE, WEIGHT_DECAY),
        (up_weight, grad_up, up_m, up_v, MATRIX_RATE, WEIGHT_DECAY),
        (down_weight, grad_down, down_m, down_v, MATRIX_RATE, WEIGHT_DECAY),
        (qkv_weight, grad_qkv, qkv_m, qkv_v, MATRIX_RATE, WEIGHT_DECAY),
        (out_weight, grad_out, out_m, out_v, MATRIX_RATE, WEIGHT_DECAY),
        (fc_weight, grad_fc, fc_m, fc_v, MATRIX_RATE, WEIGHT_DECAY),
        (proj_weight, grad_proj, proj_m, proj_v, MATRIX_RATE, WEIGHT_DECAY),
        (norm_params, grad_norms, norm_m, norm_v, NORM_RATE, 0.0),
    ):
        results.extend(adam_update(weight, factor * grad, first, second, rate, decay))
    return tuple(results)


def solution(mesh):
    fused = mesh.shape["dp"] == 16 and mesh.shape["mp"] == 2
    state = {"copied": P(), "qkv": P(None, "dp", "mp"), "tall": P("mp", "dp"), "wide": P("dp", "mp")}
    kinds = ["copied"] * 3 + ["qkv", "tall", "wide", "tall", "copied"]
    weights = [state[kind] for kind in kinds]
    moments = [state[kind] for kind in kinds for unused in range(2)]
    placed = (
        P("dp", None), P("dp", None), P("dp"), P("dp", None, None), P("dp", None), P("dp", None),
        *weights,
        *moments,
    )
    outs = (P(), P(), P()) + tuple(state[kind] for kind in kinds for unused in range(3))
    return jax.shard_map(
        functools.partial(per_device, fused), mesh=mesh, in_specs=placed, out_specs=outs, check_vma=False
    )
```

```python
import functools
import math

import jax
import jax.numpy as jnp
import numpy as np
from jax import lax
from jax.experimental import pallas as pl
from jax.experimental.pallas import tpu as pltpu
from jax.sharding import PartitionSpec as P

HEAD_DIM = 64
NB = 16
T_STEPS = 2000
STEP = 10

NORM_EPS = 1e-05
MASKED = -1e30
BETA_FIRST = 0.9
BETA_SECOND = 0.999
ADAM_EPS = 1e-08
MATRIX_RATE = 0.05
NORM_RATE = 0.5
WEIGHT_DECAY = 0.1
CLIP_NORM = 0.01

TILE = 256
SPAN = 128
WINDOW = 384
MESH = pl.DeviceIdType.MESH
F32 = jnp.float32
BF16 = jnp.bfloat16
VMEM_LIMIT = 62 * 2**20


def nn(left, right):
    return jnp.dot(left, right, preferred_element_type=F32)


def nt(left, right):
    return lax.dot_general(
        left, right, (((1,), (1,)), ((), ())), preferred_element_type=F32
    )


def sine_row(step, width):
    half = width // 2
    lane = lax.broadcasted_iota(jnp.int32, (1, half), 1).astype(F32)
    angles = step * jnp.exp(lane * (-math.log(10000.0) / half))
    return jnp.concatenate([jnp.sin(angles), jnp.cos(angles)], axis=1)


def place_table(length, width):
    half = width // 2
    freqs = np.exp(-math.log(10000.0) * np.arange(half, dtype=np.float64) / half)
    angles = np.arange(length, dtype=np.float64)[:, None] * freqs[None, :]
    return np.concatenate([np.sin(angles), np.cos(angles)], axis=-1).astype(np.float32)


def norm_stats(values):
    width = values.shape[-1]
    center = values - jnp.sum(values, axis=-1, keepdims=True) * (1.0 / width)
    spread = jnp.sum(center * center, axis=-1, keepdims=True) * (1.0 / width)
    rate = lax.rsqrt(spread + NORM_EPS)
    return center * rate, rate


def norm_back(unit, rate, gain, upstream):
    width = unit.shape[-1]
    scaled = upstream * gain
    first = jnp.sum(scaled, axis=-1, keepdims=True) * (1.0 / width)
    second = jnp.sum(scaled * unit, axis=-1, keepdims=True) * (1.0 / width)
    return rate * (scaled - first - unit * second)


def column_sum(values):
    return jnp.sum(values, axis=0, keepdims=True)


def rows_at(index, count):
    return pl.ds(pl.multiple_of(index * count, count), count)


def guarded(condition, action):
    if condition is None:
        action()
    else:
        pl.when(condition)(action)


def position():
    me = lax.axis_index("dp")
    return me, lax.axis_index("mp"), me // 4, lax.rem(me // 2, 2), lax.rem(me, 2)


def index_of(z, y, x):
    return z * 4 + y * 2 + x


def neighbours():
    me, core, z, y, x = position()
    return (index_of(z, y, 1 - x), core), (index_of(z, 1 - y, x), core), (me, 1 - core)


def remote(source, target, send_sem, recv_sem, device):
    return pltpu.make_async_remote_copy(
        src_ref=source,
        dst_ref=target,
        send_sem=send_sem,
        recv_sem=recv_sem,
        device_id=device,
        device_id_type=MESH,
    )


def greet(devices):
    me, core = position()[:2]
    barrier = pltpu.get_barrier_semaphore()
    for device in devices:

        @pl.when(jnp.logical_or(device[0] != me, device[1] != core))
        def signal():
            pl.semaphore_signal(barrier, inc=1, device_id=device, device_id_type=MESH)


def assemble(devices):
    pl.semaphore_wait(pltpu.get_barrier_semaphore(), len(devices) - 1)


class Exchange:
    def __init__(self, source, slots, send_sems, recv_sems, devices):
        self.source, self.slots = source, slots
        self.send_sems, self.recv_sems = send_sems, recv_sems
        me, core = position()[:2]
        self.devices = [
            (slot, device, jnp.logical_or(device[0] != me, device[1] != core))
            for slot, device in enumerate(devices)
        ]
        self.mine = me if len(devices) == 16 else 2 * me + core

    def copy(self, slot, device):
        return remote(
            self.source, self.slots.at[self.mine], self.send_sems.at[slot], self.recv_sems.at[self.mine], device
        )

    def start(self):
        for slot, device, other in self.devices:
            guarded(other, lambda: self.copy(slot, device).start())

    def arrive(self):
        for slot, device, other in self.devices:

            def wait():
                remote(
                    self.slots.at[slot], self.slots.at[slot], self.send_sems.at[slot], self.recv_sems.at[slot], device
                ).wait_recv()

            guarded(other, wait)

    def total(self):
        self.slots[self.mine] = self.source[...]
        value = self.slots[0]
        for slot in range(1, len(self.devices)):
            value = value + self.slots[slot]
        return value

    def finish(self):
        for slot, device, other in self.devices:
            guarded(other, lambda: self.copy(slot, device).wait_send())


def same_core():
    core = position()[1]
    return [(d, core) for d in range(16)]


def every_device():
    return [(d, c) for d in range(16) for c in range(2)]


class Gather:
    def __init__(self, shard, whole, sems, rows):
        self.shard, self.whole, self.rows = shard, whole, rows
        (self.local_s, self.up_s, self.down_s, self.plane_s, self.pair_s, self.recv, self.pair_recv) = sems
        self.xn, self.yn, self.pair = neighbours()
        self.me, self.core, self.z, self.y, self.x = position()
        self.up = (jnp.minimum(self.me + 4, 15), self.core)
        self.down = (jnp.maximum(self.me - 4, 0), self.core)
        self.sends = []

    def piece(self, b, c, d):
        return self.whole.at[b, c, rows_at(d, self.rows), :]

    def send(self, b, d, own, device, sem, condition=None, to_pair=False):
        source = self.shard.at[b] if own else self.piece(b, self.core, d)
        recv = self.pair_recv if to_pair else self.recv

        def copy():
            return remote(source, self.piece(b, self.core, d), sem, recv.at[b, d], device)

        self.sends.append((condition, copy))
        guarded(condition, lambda: copy().start())

    def arrive(self, b, c, d, recv):
        remote(self.piece(b, c, d), self.piece(b, c, d), self.pair_s.at[b, d], recv.at[b, d], self.pair).wait_recv()

    def spread(self, b, d, zz, own=False, condition=None):
        odd = lax.rem(zz, 2)
        for step in range(2):
            along_y = odd if step == 0 else 1 - odd
            device = (index_of(self.z, jnp.where(along_y == 1, 1 - self.y, self.y), jnp.where(along_y == 1, self.x, 1 - self.x)), self.core)
            self.send(b, d, own, device, self.plane_s.at[b, step, zz], condition)
        self.send(b, d, own, self.pair, self.pair_s.at[b, d], condition, True)

    def local(self, b):
        return pltpu.make_async_copy(self.shard.at[b], self.piece(b, self.core, self.me), self.local_s.at[b])

    def begin(self, b):
        self.local(b).start()
        self.send(b, self.me, True, self.up, self.up_s.at[b, 0], self.z < 3)
        self.send(b, self.me, True, self.down, self.down_s.at[b, 0], self.z > 0)
        self.spread(b, self.me, self.z, True)

    def hop(self, b, distance):
        z = self.z
        for source, there, onward, device, sem in (
            (jnp.maximum(z - distance, 0), z >= distance, z < 3, self.up, self.up_s),
            (jnp.minimum(z + distance, 3), z + distance <= 3, z > 0, self.down, self.down_s),
        ):
            d = index_of(source, self.y, self.x)
            guarded(there, lambda: self.arrive(b, self.core, d, self.recv))
            if distance < 3:
                self.send(b, d, False, device, sem.at[b, distance], jnp.logical_and(there, onward))
            self.spread(b, d, source, False, there)

    def turn(self, b):
        for zz in range(4):
            yy, xx = (1 - self.y, self.x) if zz % 2 else (self.y, 1 - self.x)
            d = index_of(zz, yy, xx)
            self.arrive(b, self.core, d, self.recv)
            self.send(b, d, False, self.xn if zz % 2 else self.yn, self.plane_s.at[b, 2, zz])
            self.send(b, d, False, self.pair, self.pair_s.at[b, d], None, True)

    def last(self, b):
        for zz in range(4):
            yy, xx = (self.y, 1 - self.x) if zz % 2 else (1 - self.y, self.x)
            for d in (index_of(zz, yy, xx), index_of(zz, 1 - self.y, 1 - self.x)):
                self.arrive(b, self.core, d, self.recv)
                self.send(b, d, False, self.pair, self.pair_s.at[b, d], None, True)

    def ready(self, b):
        self.local(b).wait()
        for d in range(16):
            self.arrive(b, 1 - self.core, d, self.pair_recv)

    def finish(self):
        for condition, copy in self.sends:
            guarded(condition, lambda copy=copy: copy().wait_send())


class QuickGather:
    def __init__(self, shard, whole, sems, rows):
        self.shard, self.whole, self.rows = shard, whole, rows
        self.local_s, self.line_s, self.plane_s, self.recv = sems
        self.me, self.core, self.z, self.y, self.x = position()
        self.sends = []

    def piece(self, c, d):
        return self.whole.at[c, rows_at(d, self.rows), :]

    def send(self, d, own, device, sem, condition=None):
        def copy():
            source = self.shard if own else self.piece(self.core, d)
            return remote(source, self.piece(self.core, d), sem, self.recv.at[self.core, d], device)

        self.sends.append((condition, copy))
        guarded(condition, lambda: copy().start())

    def arrive(self, c, d):
        remote(self.piece(c, d), self.piece(c, d), self.line_s.at[0, 0], self.recv.at[c, d], (self.me, 1 - self.core)).wait_recv()

    def local(self):
        return pltpu.make_async_copy(self.shard, self.piece(self.core, self.me), self.local_s.at[0])

    def plane(self, zz, own, condition=None):
        d = index_of(zz, self.y, self.x)
        for k, (yy, xx) in enumerate(((self.y, 1 - self.x), (1 - self.y, self.x), (1 - self.y, 1 - self.x))):
            for c in range(2):
                self.send(d, own, (index_of(self.z, yy, xx), c), self.plane_s.at[zz, k, c], condition)

    def begin(self):
        self.local().start()
        for zz in range(4):
            for c in range(2):
                there = (index_of(zz, self.y, self.x), c)
                other = jnp.logical_or(self.z != zz, self.core != c)
                self.send(self.me, True, there, self.line_s.at[zz, c], other)
        self.plane(self.z, True)

    def spread(self):
        for zz in range(4):
            guarded(self.z != zz, lambda: self.arrive(self.core, index_of(zz, self.y, self.x)))
            self.plane(zz, False, self.z != zz)

    def ready(self):
        self.local().wait()
        for d in range(16):
            same = jnp.logical_and(lax.rem(d, 4) == lax.rem(self.me, 4), True)
            guarded(jnp.logical_not(same), lambda: self.arrive(self.core, d))
            self.arrive(1 - self.core, d)

    def finish(self):
        for condition, copy in self.sends:
            guarded(condition, lambda copy=copy: copy().wait_send())


def quick_sems():
    dma = pltpu.SemaphoreType.DMA
    return [dma((1,)), dma((4, 2)), dma((4, 3, 2)), dma((2, 16))]


GATHER_REFS = 7


def gather_sems(count):
    dma = pltpu.SemaphoreType.DMA
    return [dma((count,)), dma((count, 4)), dma((count, 4)), dma((count, 3, 4)), dma((count, 16)), dma((count, 16)), dma((count, 16))]


class Scatter:
    def __init__(self, refs, landed, loaded, out, rows):
        (self.own, self.near, self.far, self.lined, self.pair_s, self.pair_r, self.load_s) = refs[:7]
        self.near_s, self.near_r, self.far_s, self.far_r, self.line_s, self.line_r = refs[7:]
        self.landed, self.loaded, self.out, self.rows = landed, loaded, out, rows
        self.xn, self.yn, self.pair = neighbours()
        self.me, self.core, self.z, self.y, self.x = position()

    def piece(self, b, zz, yy, xx):
        return self.own.at[b, rows_at(index_of(zz, yy, xx), self.rows), :]

    def pair_copy(self, b, source):
        return remote(source, self.landed.at[b], self.pair_s.at[b], self.pair_r.at[b], self.pair)

    def load(self, b):
        return pltpu.make_async_copy(self.landed.at[b], self.loaded[b], self.load_s.at[b])

    def near_copy(self, b, zz, i):
        place, device = ((zz, i, 1 - self.x), self.xn) if zz % 2 else ((zz, 1 - self.y, i), self.yn)
        return remote(
            self.piece(b, *place), self.near.at[b, zz, i], self.near_s.at[b, zz, i], self.near_r.at[b, zz, i], device
        )

    def onward(self, zz):
        return 1 - self.y if zz % 2 else 1 - self.x

    def far_place(self, zz):
        return (zz, 1 - self.y, self.x) if zz % 2 else (zz, self.y, 1 - self.x)

    def far_copy(self, b, zz):
        return remote(
            self.piece(b, *self.far_place(zz)), self.far.at[b, zz], self.far_s.at[b, zz], self.far_r.at[b, zz],
            self.yn if zz % 2 else self.xn,
        )

    def line_copy(self, b, zz):
        there = (index_of(zz, self.y, self.x), self.core)
        return remote(
            self.near.at[b, zz, 1 - self.onward(zz)], self.lined.at[b, self.z], self.line_s.at[b, zz], self.line_r.at[b, self.z], there
        )

    def take(self, b):
        self.pair_copy(b, self.own.at[b]).wait_recv()
        self.load(b).start()

    def first(self, b):
        self.load(b).wait()
        loaded = self.loaded[b]

        def add(d, carry):
            at = rows_at(d, self.rows)
            self.own[b, at, :] = (self.own[b, at, :].astype(F32) + loaded[at, :].astype(F32)).astype(self.own.dtype)
            return carry

        lax.fori_loop(0, 16, add, 0)
        for zz in range(4):
            self.near_copy(b, zz, self.onward(zz)).start()
        for zz in range(4):
            self.near_copy(b, zz, 1 - self.onward(zz)).start()

    def second(self, b):
        for zz in range(4):
            i = self.onward(zz)
            self.near_copy(b, zz, i).wait_recv()
            place = self.far_place(zz)
            value = self.piece(b, *place)[...].astype(F32) + self.near[b, zz, i].astype(F32)
            self.piece(b, *place)[...] = value.astype(self.own.dtype)
            self.far_copy(b, zz).start()

    def third(self, b):
        for zz in range(4):
            i = 1 - self.onward(zz)
            self.near_copy(b, zz, i).wait_recv()
            self.far_copy(b, zz).wait_recv()
            value = self.piece(b, zz, self.y, self.x)[...].astype(F32) + self.near[b, zz, i].astype(F32) + self.far[b, zz].astype(F32)

            @pl.when(self.z == zz)
            def keep():
                self.out[b] = value

            @pl.when(self.z != zz)
            def give():
                self.near[b, zz, i] = value.astype(self.near.dtype)
                self.line_copy(b, zz).start()

    def result(self, b):
        for zz in range(4):

            @pl.when(self.z != zz)
            def add():
                remote(
                    self.lined.at[b, zz], self.lined.at[b, zz], self.line_s.at[b, zz], self.line_r.at[b, zz], self.pair
                ).wait_recv()
                self.out[b] += self.lined[b, zz].astype(F32)

        value = self.out[b]
        return jnp.sum(value * value, keepdims=True)

    def finish(self, b):
        for zz in range(4):
            for i in range(2):
                self.near_copy(b, zz, i).wait_send()
            self.far_copy(b, zz).wait_send()
            guarded(self.z != zz, lambda: self.line_copy(b, zz).wait_send())


SCATTER_REFS = 13


def scatter_scratch(count, rows, columns):
    dma, vmem = pltpu.SemaphoreType.DMA, pltpu.VMEM
    return [
        vmem((count, 16 * rows, columns), BF16),
        vmem((count, 4, 2, rows, columns), BF16),
        vmem((count, 4, rows, columns), BF16),
        vmem((count, 4, rows, columns), BF16),
        dma((count,)), dma((count,)), dma((count,)),
        dma((count, 4, 2)), dma((count, 4, 2)), dma((count, 4)), dma((count, 4)), dma((count, 4)), dma((count, 4)),
    ]


def gelu_parts(values):
    root = 0.7978845608028654
    square = values * values
    bent = jnp.tanh(root * (values + 0.044715 * (square * values)))
    half = 0.5 * (1.0 + bent)
    slope = half + (0.5 * root) * values * (1.0 - bent * bent) * (1.0 + (3 * 0.044715) * square)
    return values * half, slope


def halves_of(shape, axis, scale):
    low = lax.broadcasted_iota(jnp.int32, shape, axis) < HEAD_DIM
    return jnp.where(low, scale, 0.0).astype(BF16), jnp.where(low, 0.0, scale).astype(BF16)


def pick_halves(wide):
    low = lax.broadcasted_iota(jnp.int32, (2 * HEAD_DIM, SPAN), 0) < HEAD_DIM
    return jnp.where(low, wide[:, :SPAN], wide[:, SPAN:])


def window_start(block, blocks):
    return min(max(block - 1, 0), blocks - WINDOW // SPAN) * SPAN


def column_table(rows, length):
    rows = rows + [jnp.zeros((1, length), F32)] * (8 - len(rows))
    return jnp.concatenate(rows, axis=0).T


def one_hot(ids, vocab):
    lanes = lax.broadcasted_iota(jnp.int32, (ids.shape[0], vocab), 1).astype(F32)
    return ids == lanes


def forward_kernel(fused, shapes, *refs):
    length, width, pairs = shapes
    blocks = length // SPAN
    tiles = length // TILE
    half = width // 2
    sources = 4 if fused else 2
    (
        tokens, segments, steps, noise_in, buckets, counted, embed_in, up_in, norms, places_in,
        wide_whole, thin_whole, count_out, start, noisy, table_low, zero_out, one_out, two_out, qkv_out, keyt_out, att_out, probs_out, act_out, slope_out, first_t_out, second_t_out,
        h_zero, h_one, h_two, normed, normed_t, qkv, key_t, value_t, att, probs, act, slope, weights, bias, places, table, table3, columns, count_own, noise, embed, up_weight,
        out_sems, probs_sems, weight_sems, in_sems,
    ) = refs[sources : sources + 53]
    rest = refs[sources + 53 :]
    core = lax.axis_index("mp")
    saves = []

    def save(source, target):
        copy = pltpu.make_async_copy(source, target, out_sems.at[len(saves)])
        copy.start()
        saves.append(copy)

    if fused:
        everyone = same_core() + [neighbours()[2]]
        greet(everyone)
        qkv_weight, out_weight, fc_weight, proj_weight = rest[:4]
        wide_shard, thin_shard, counts, count_send, count_recv = rest[4:9]
        rows = wide_shard.shape[1]
        wide = Gather(wide_shard, wide_whole, rest[9 : 9 + GATHER_REFS], rows)
        thin = Gather(thin_shard, thin_whole, rest[9 + GATHER_REFS :], rows)
        gathers = {"wide": wide, "thin": thin}
        moves = list(zip(refs[:4], rest[:4]))
    else:
        moves = []
    moves += [(noise_in.at[core], noise), (embed_in, embed), (up_in, up_weight), (places_in, places)]
    fetches = [pltpu.make_async_copy(source, target, in_sems.at[k]) for k, (source, target) in enumerate(moves)]
    for copy in fetches:
        copy.start()
    if fused:
        wide_from, thin_from = wide_whole, thin_whole
        for copy in fetches[:4]:
            copy.wait()
        for j in range(3):
            thin_shard[j] = qkv_weight[j].astype(BF16)
        thin_shard[3] = out_weight[...].astype(BF16)
        for h in range(2):
            cols = slice(h * width, (h + 1) * width)
            wide_shard[h] = fc_weight[:, cols].astype(BF16)
            wide_shard[2 + h] = proj_weight[:, cols].astype(BF16)
    else:
        wide_from, thin_from = refs[:2]

    def pump(*items):
        if fused:
            for which, name, b, *more in items:
                getattr(gathers[which], name)(b, *more)

    live = counted[...].astype(F32)
    lane = lax.broadcasted_iota(jnp.int32, count_own.shape, 1)
    own_counts = jnp.zeros(count_own.shape, F32)
    for bucket in range(NB):
        found = jnp.sum(jnp.where(buckets[...] == bucket, live, 0.0), keepdims=True)
        own_counts = jnp.where(lane == bucket, found, own_counts)
    count_own[...] = own_counts
    token_row = tokens[pl.ds(core, 1), :].astype(F32)
    segment_row = segments[pl.ds(core, 1), :].astype(F32)
    columns[...] = column_table([token_row, segment_row], length)
    emb = embed.shape[1]
    for copy in fetches[-4:]:
        copy.wait()
    table[...] = jnp.zeros(table.shape, F32)
    table[: embed.shape[0], :] = embed[...]
    left = table[...]
    for third in range(3):
        part = left.astype(BF16)
        table3[:, third * emb : (third + 1) * emb] = part
        if third == 0:
            table_low[...] = part
        left = left - part.astype(F32)
    step = jnp.full((1, 1), steps[core], jnp.int32).astype(F32)
    keep = 1.0 - jnp.sqrt(step * (1.0 / T_STEPS) + 0.0001)
    keep_root, noise_root = jnp.sqrt(keep), jnp.sqrt(1.0 - keep)
    time_row = sine_row(step, width)
    up_low = up_weight[...].astype(BF16)

    def embed_tile(r):
        at = rows_at(r, TILE)
        hot = one_hot(columns[at, 0:1], table.shape[0]).astype(F32).astype(BF16)
        thirds = nn(hot, table3[...])
        first = thirds[:, :emb] + thirds[:, emb : 2 * emb] + thirds[:, 2 * emb :]
        start[at, :] = first
        low = (keep_root * first + noise_root * noise[at, :]).astype(BF16)
        noisy[at, :] = low
        hidden = nn(low, up_low) + places[at, :] + time_row
        h_zero[at, :] = hidden
        unit = norm_stats(hidden)[0]
        scaled = unit * norms[0:1, :] + norms[1:2, :]
        normed[at, :] = scaled.astype(BF16)
        normed_t[0, :, at] = scaled.T.astype(BF16)

    if fused:
        assemble(everyone)
        exchange = Exchange(count_own, counts, count_send, count_recv, same_core())
        exchange.start()
    early = range(3)
    pump(*[("thin", "begin", b) for b in early])
    for r in range(tiles):
        embed_tile(r)
        if r < 3:
            pump(*[("thin", "hop", b, r + 1) for b in early])
    pump(*[("thin", "turn", b) for b in early])
    pump(("thin", "begin", 3), ("wide", "begin", 0), ("wide", "begin", 1))
    save(h_zero, zero_out)
    save(normed_t.at[0], first_t_out)
    for i in range(blocks):
        w0 = window_start(i, blocks)
        same = columns[w0 : w0 + WINDOW, 1:2] == segment_row[:, i * SPAN : (i + 1) * SPAN]
        bias[i] = jnp.where(same, 0.0, MASKED)
    pump(*[("thin", "last", b) for b in early])
    pump(("wide", "begin", 2), ("wide", "begin", 3))

    def load_wide(b, c, slot):
        return pltpu.make_async_copy(wide_from.at[b, c], weights.at[slot], weight_sems.at[slot])

    def load_thin(b, c):
        slot, side = 2 * (b // 2) + c, b % 2
        return pltpu.make_async_copy(
            thin_from.at[b, c], weights.at[slot, :, side * half : (side + 1) * half], weight_sems.at[slot + 8 * side]
        )

    pump(*[("thin", "ready", b) for b in early])
    for c in range(2):
        for b in early:
            load_thin(b, c).start()
    pump(("thin", "hop", 3, 1), ("wide", "hop", 0, 1))
    for c in range(2):
        for b in early:
            load_thin(b, c).wait()
    for c in range(2):

        def project(r, carry):
            at = rows_at(r, TILE)
            rows = normed[at, :]
            first = nn(rows, weights[c])
            values = nn(rows, weights[2 + c, :, :half])
            cols = slice(c * half, (c + 1) * half)
            qkv[0, at, cols] = first[:, :half].astype(BF16)
            qkv[1, at, cols] = first[:, half:].astype(BF16)
            qkv[2, at, cols] = values.astype(BF16)
            key_t[cols, at] = first[:, half:].T.astype(BF16)
            value_t[cols, at] = values.T.astype(BF16)
            return carry

        lax.fori_loop(0, tiles, project, 0)
        if c == 0:
            pump(("thin", "hop", 3, 2), ("wide", "hop", 0, 2), ("wide", "hop", 1, 1))
        else:
            pump(("thin", "hop", 3, 3), ("wide", "hop", 0, 3), ("wide", "hop", 1, 2), ("wide", "hop", 2, 1), ("wide", "hop", 3, 1))
    for j in range(3):
        save(qkv.at[j], qkv_out.at[j])
    save(key_t, keyt_out)

    def probs_copy(pair, slot):
        return pltpu.make_async_copy(probs.at[slot], probs_out.at[pl.ds(pair * blocks, blocks)], probs_sems.at[slot])

    low, high = halves_of((1, SPAN), 1, 0.125)

    def attend(pair, carry):
        slot = lax.rem(pair, 2)
        cols = pl.ds(pl.multiple_of(pair * SPAN, SPAN), SPAN)

        @pl.when(pair >= 2)
        def free():
            probs_copy(pair - 2, slot).wait()

        for i in range(blocks):
            w0 = window_start(i, blocks)
            queries = qkv[0, i * SPAN : (i + 1) * SPAN, cols]
            both = jnp.concatenate([queries * low, queries * high], axis=0)
            scores = nt(qkv[1, w0 : w0 + WINDOW, cols], both)
            mask = bias[i]
            scores = scores + jnp.concatenate([mask, mask], axis=1)
            most = jnp.max(scores, axis=0, keepdims=True)
            raised = jnp.exp(scores - most)
            share = 1.0 / jnp.sum(raised, axis=0, keepdims=True)
            prob = (raised * share).astype(BF16)
            probs[slot, i] = prob
            mixed = nn(value_t[cols, w0 : w0 + WINDOW], prob)
            att[i * SPAN : (i + 1) * SPAN, cols] = pick_halves(mixed).T.astype(BF16)
        probs_copy(pair, slot).start()
        return carry

    middle = [
        [("wide", "hop", 1, 3), ("wide", "hop", 2, 2), ("wide", "hop", 3, 2)],
        [("wide", "hop", 2, 3), ("wide", "hop", 3, 3), ("thin", "turn", 3), ("wide", "turn", 0)],
        [("wide", "turn", 1), ("wide", "turn", 2)],
        [("wide", "turn", 3), ("thin", "last", 3), ("wide", "last", 0)],
        [("wide", "last", 1)],
        [],
    ]
    for part in range(6):
        lax.fori_loop(part * pairs // 6, (part + 1) * pairs // 6, attend, 0)
        pump(*middle[part])
    for pair in (pairs - 2, pairs - 1):
        probs_copy(pair, pair % 2).wait()
    save(att, att_out)
    pump(("thin", "ready", 3))
    for c in range(2):
        load_thin(3, c).start()
    for c in range(2):
        load_thin(3, c).wait()
    pump(("wide", "ready", 0), ("wide", "ready", 1))
    for h in range(2):
        for c in range(2):
            load_wide(h, c, 4 + 2 * h + c).start()

    def after_attention(r, carry):
        at = rows_at(r, TILE)
        mixed = att[at, :]
        total = nt(mixed[:, :half], weights[2, :, half:]) + nt(mixed[:, half:], weights[3, :, half:])
        hidden = h_zero[at, :] + total
        h_one[at, :] = hidden
        unit = norm_stats(hidden)[0]
        scaled = unit * norms[2:3, :] + norms[3:4, :]
        normed[at, :] = scaled.astype(BF16)
        normed_t[1, :, at] = scaled.T.astype(BF16)
        return carry

    lax.fori_loop(0, tiles, after_attention, 0)
    save(h_one, one_out)
    save(normed_t.at[1], second_t_out)
    pump(("wide", "last", 2), ("wide", "last", 3))
    for j in range(4):
        load_wide(j // 2, j % 2, 4 + j).wait()

        def grow(r, carry):
            at = rows_at(r, TILE)
            before = nn(normed[at, :], weights[4 + j])
            active, bend = gelu_parts(before)
            act[j, at, :] = active.astype(BF16)
            slope[j, at, :] = bend.astype(BF16)
            return carry

        lax.fori_loop(0, tiles, grow, 0)
        save(act.at[j], act_out.at[j])
        save(slope.at[j], slope_out.at[j])
        if j == 0:
            pump(("wide", "ready", 2), ("wide", "ready", 3))
            for k in range(4):
                load_wide(2 + k // 2, k % 2, k).start()
    for j in range(4):
        load_wide(2 + j // 2, j % 2, j).wait()

    def shrink(r, carry):
        at = rows_at(r, TILE)
        total = h_one[at, :]
        for j in range(4):
            total = total + nt(act[j, at, :], weights[j])
        h_two[at, :] = total
        return carry

    lax.fori_loop(0, tiles, shrink, 0)
    save(h_two, two_out)
    if fused:
        exchange.arrive()
        count_out[...] = exchange.total()
        wide.finish()
        thin.finish()
        exchange.finish()
    else:
        count_out[...] = count_own[...]
    for copy in saves:
        copy.wait()


def run_forward(fused, sources, tokens, segments, steps, noise, buckets, counted, embed, up_weight, norms, places):
    length, width = places.shape
    pairs = width // SPAN
    blocks = length // SPAN
    dma, vmem = pltpu.SemaphoreType.DMA, pltpu.VMEM
    anywhere, inside = pl.BlockSpec(memory_space=pl.ANY), pl.BlockSpec(memory_space=pltpu.VMEM)
    vocab, emb = embed.shape
    padded = -(-vocab // 128) * 128

    def made(shape, dtype=BF16):
        return jax.ShapeDtypeStruct(shape, dtype)

    out_shape = [
        made((4, 2, width, width)),
        made((4, 2, width, width // 2)),
        made((8, 128), F32),
        made((length, emb), F32),
        made((length, emb)),
        made((padded, emb)),
        made((length, width), F32),
        made((length, width), F32),
        made((length, width), F32),
        made((3, length, width)),
        made((width, length)),
        made((length, width)),
        made((pairs * blocks, WINDOW, 2 * SPAN)),
        made((4, length, width)),
        made((4, length, width)),
        made((width, length)),
        made((width, length)),
    ]
    scratch = [
        vmem((length, width), F32),
        vmem((length, width), F32),
        vmem((length, width), F32),
        vmem((length, width), BF16),
        vmem((2, width, length), BF16),
        vmem((3, length, width), BF16),
        vmem((width, length), BF16),
        vmem((width, length), BF16),
        vmem((length, width), BF16),
        vmem((2, blocks, WINDOW, 2 * SPAN), BF16),
        vmem((4, length, width), BF16),
        vmem((4, length, width), BF16),
        vmem((8, width, width), BF16),
        vmem((blocks, WINDOW, SPAN), F32),
        vmem((length, width), F32),
        vmem((padded, emb), F32),
        vmem((padded, 3 * emb), BF16),
        vmem((length, 8), F32),
        vmem((8, 128), F32),
        vmem((length, emb), F32),
        vmem((vocab, emb), F32),
        vmem((emb, width), F32),
        dma((20,)),
        dma((2,)),
        dma((12,)),
        dma((8,)),
    ]
    params = dict(vmem_limit_bytes=VMEM_LIMIT)
    if fused:
        rows = width // 16
        scratch += [vmem(source.shape, F32) for source in sources]
        scratch += [vmem((4, rows, width), BF16), vmem((4, rows, width // 2), BF16)]
        scratch += [vmem((16, 8, 128), F32), dma((16,)), dma((16,))] + gather_sems(4) + gather_sems(4)
        params.update(collective_id=0, has_side_effects=True)
    return pl.pallas_call(
        functools.partial(forward_kernel, fused, (length, width, pairs)),
        out_shape=out_shape,
        in_specs=[anywhere] * len(sources)
        + [inside, inside, pl.BlockSpec(memory_space=pltpu.SMEM), anywhere]
        + [inside] * 2
        + [anywhere] * 2
        + [inside, anywhere],
        out_specs=[anywhere] * 2 + [inside] * 4 + [anywhere] * 11,
        scratch_shapes=scratch,
        compiler_params=pltpu.CompilerParams(**params),
        name="forward",
    )(*sources, tokens, segments, steps, noise, buckets, counted, embed, up_weight, norms, places)


def backward_kernel(fused, shapes, *refs):
    length, width, pairs, vocab_used = shapes
    blocks = length // SPAN
    tiles = length // TILE
    half = width // 2
    (
        wide_whole, thin_whole, tokens, buckets, counted, counts, start, noisy, zero_in, one_in, two_in, qkv_in, keyt_in, att_in, probs_in, act_in, slope_in, first_t_in, second_t_in,
        embed_low, up_weight, down_weight, norms, steps,
        out_wide, out_thin, out_small, out_scalars, wide_landed, thin_landed, small_landed,
        hidden, grad, back, branch, branch_t, normed_t, pre, slots, weights, acc, probs, error, norm_grads, posted, thin_posted, small_own, scalars, columns, up_low, down_low,
        load_sems, slot_sems, weight_sems, probs_sems, post_sems,
    ) = refs[:56]
    core = lax.axis_index("mp")
    small = out_small
    emb = start.shape[1]
    vocab = embed_low.shape[0]
    side = width // TILE

    if fused:
        rest = refs[56:]
        n = SCATTER_REFS
        loaded, tiny_loaded, tiny_shard, tiny_whole, tiny_out, slots_all, all_send, all_recv = rest[3 * n : 3 * n + 8]
        gather_refs = rest[3 * n + 8 :]
        wide_loaded = [loaded.at[b // 2] for b in range(4)]
        thin_loaded = [loaded.at[b // 2, :, (b % 2) * half : (b % 2 + 1) * half] for b in range(4)]
        wide = Scatter(rest[:n], wide_landed, wide_loaded, out_wide, width // 16)
        thin = Scatter(rest[n : 2 * n], thin_landed, thin_loaded, out_thin, width // 16)
        tiny = Scatter(rest[2 * n : 3 * n], small_landed, [tiny_loaded], tiny_out, 16)
        devices = every_device()
        greet(devices)

    def pump(scatter_name, *steps):
        if fused:
            scatter = wide if scatter_name == "wide" else thin
            for name, *members in steps:
                for b in members:
                    getattr(scatter, name)(b)

    def post_copy(b, slot):
        if fused:
            return wide.pair_copy(b, posted.at[slot])
        return pltpu.make_async_copy(posted.at[slot], out_wide.at[b, 1 - core], post_sems.at[slot])

    def thin_copy(b):
        if fused:
            return thin.pair_copy(b, thin_posted.at[b])
        return pltpu.make_async_copy(thin_posted.at[b], out_thin.at[b, 1 - core], post_sems.at[4 + b])

    def kept_copy(b, slot):
        return pltpu.make_async_copy(posted.at[slot], out_wide.at[b, core], post_sems.at[slot])

    def thin_kept(b):
        return pltpu.make_async_copy(thin_posted.at[4 + b], out_thin.at[b, core], post_sems.at[8 + b])

    def sent(copy):
        (copy.wait_send if fused else copy.wait)()

    def fetch(source, target, k):
        copy = pltpu.make_async_copy(source, target, load_sems.at[k])
        copy.start()
        return copy

    def load_weights(b, c, slot):
        return pltpu.make_async_copy(wide_whole.at[b, c], weights.at[slot], weight_sems.at[slot])

    def load_thin(b, c):
        slot, part = 2 * (b // 2) + c, b % 2
        return pltpu.make_async_copy(
            thin_whole.at[b, c], weights.at[slot, :, part * half : (part + 1) * half], weight_sems.at[4 + 2 * b + c]
        )

    def load_slot(source, slot):
        return pltpu.make_async_copy(source, slots.at[slot], slot_sems.at[slot])

    def feed(s):
        h, c = s // 2, (1 - core if s % 2 == 0 else core)
        first = 2 * (s % 2)
        return [
            load_weights(h, c, first),
            load_weights(2 + h, c, first + 1),
            load_slot(act_in.at[2 * h + c], first),
            load_slot(slope_in.at[2 * h + c], first + 1),
        ]

    two_copy = fetch(two_in, hidden, 0)
    normed_copy = fetch(second_t_in, normed_t, 1)
    for copy in feed(0):
        copy.start()
    norm_grads[...] = jnp.zeros(norm_grads.shape, F32)
    small[...] = jnp.zeros(small.shape, F32)
    count_row = counts[0:1, :]
    live_total = jnp.sum(count_row, keepdims=True)
    bucket_weight = live_total / (NB * jnp.maximum(count_row, 1.0))
    weight_total = jnp.sum(count_row * bucket_weight, keepdims=True)
    bucket_row = buckets[pl.ds(core, 1), :]
    scale = jnp.zeros((1, length), F32)
    for bucket in range(NB):
        scale = jnp.where(bucket_row == bucket, bucket_weight[:, bucket : bucket + 1], scale)
    scale = scale * counted[pl.ds(core, 1), :].astype(F32)
    columns[...] = column_table([tokens[pl.ds(core, 1), :].astype(F32), scale, scale / weight_total], length)
    step = jnp.full((1, 1), steps[core], jnp.int32).astype(F32)
    keep_root = jnp.sqrt(1.0 - jnp.sqrt(step * (1.0 / T_STEPS) + 0.0001))
    up_low[...] = up_weight[...].astype(BF16)
    down_low[...] = down_weight[...].astype(BF16)
    ids = lax.broadcasted_iota(jnp.int32, (TILE, vocab), 1).astype(F32)
    pad_row = jnp.where(lax.broadcasted_iota(jnp.int32, (1, vocab), 1) < vocab_used, 0.0, MASKED)
    two_copy.wait()
    d0, u0, e0 = 0, width, 2 * width

    def add_norm(row, upstream, unit):
        norm_grads[row : row + 1, :] += column_sum(upstream * unit)
        norm_grads[row + 1 : row + 2, :] += column_sum(upstream)

    def head(r, loss):
        at = rows_at(r, TILE)
        unit, rate = norm_stats(hidden[at, :])
        ended = (unit * norms[4:5, :] + norms[5:6, :]).astype(BF16)
        predicted = nn(ended, down_low[...])
        pred_low = predicted.astype(BF16)
        logits = nt(pred_low, embed_low[...]) + pad_row
        most = jnp.max(logits, axis=-1, keepdims=True)
        raised = jnp.exp(logits - most)
        total = jnp.sum(raised, axis=-1, keepdims=True)
        hit = columns[at, 0:1] == ids
        picked = jnp.sum(jnp.where(hit, logits, 0.0), axis=-1, keepdims=True)
        miss = predicted - start[at, :]
        per_token = jnp.sum(miss * miss, axis=-1, keepdims=True) * (1.0 / emb) + (jnp.log(total) + most) - picked
        loss = loss + jnp.sum(columns[at, 1:2] * per_token, keepdims=True)
        coef = columns[at, 2:3]
        grad_logits = (coef * (raised * (1.0 / total) - jnp.where(hit, 1.0, 0.0))).astype(BF16)
        grad_error = coef * 2.0 * miss * (1.0 / emb)
        error[at, :] = grad_error
        grad_pred = nn(grad_logits, embed_low[...]) + grad_error
        grad_pred_low = grad_pred.astype(BF16)
        small[:, d0 : d0 + width] += nn(grad_pred.T.astype(BF16), ended)
        small[:, e0 : e0 + vocab] += nn(predicted.T.astype(BF16), grad_logits)
        upstream = nt(grad_pred_low, down_low[...])
        add_norm(4, upstream, unit)
        result = norm_back(unit, rate, norms[4:5, :], upstream)
        grad[at, :] = result
        branch[at, :] = result.astype(BF16)
        branch_t[:, at] = result.T.astype(BF16)
        return loss

    loss = lax.fori_loop(0, tiles, head, jnp.zeros((1, 1), F32))
    one_copy = fetch(one_in, hidden, 0)
    normed_copy.wait()

    for s in range(4):
        h = s // 2
        if s < 3:
            for copy in feed(s + 1):
                copy.start()
        for copy in feed(s):
            copy.wait()
        first = 2 * (s % 2)
        fc, proj, active, bend = weights.at[first], weights.at[first + 1], slots.at[first], slots.at[first + 1]

        def slide(r, carry):
            at = rows_at(r, TILE)
            through = nn(branch[at, :], proj[...])
            pushed = (through * bend[at, :].astype(F32)).astype(BF16)
            pre[at, :] = pushed
            value = nt(pushed, fc[...])
            if s == 0:
                back[at, :] = value
            else:
                back[at, :] += value
            return carry

        lax.fori_loop(0, tiles, slide, 0)
        mine = s % 2 == 1
        if s == 2:
            sent(post_copy(0, 0))
            sent(post_copy(2, 1))
        if s == 2:
            pump("wide", ("first", 0, 2))
        if s == 3 and not fused:
            kept_copy(0, 2).wait()
            kept_copy(2, 3).wait()

        def weigh(m, carry):
            at = rows_at(m, TILE)
            fc_grad = nn(normed_t[at, :], pre[...]).astype(BF16)
            proj_grad = nn(branch_t[at, :], active[...]).astype(BF16)
            if mine and fused:
                wide.own[h, at, :] = fc_grad
                wide.own[2 + h, at, :] = proj_grad
            else:
                posted[2 if mine else 0, at, :] = fc_grad
                posted[3 if mine else 1, at, :] = proj_grad
            return carry

        lax.fori_loop(0, side, weigh, 0)
        if s == 0 and fused:
            assemble(devices)
        if not mine:
            post_copy(h, 0).start()
            post_copy(2 + h, 1).start()
        elif not fused:
            kept_copy(h, 2).start()
            kept_copy(2 + h, 3).start()
        if mine:
            pump("wide", ("take", h, 2 + h))

    for c in range(2):
        for b in range(4):
            load_thin(b, c).start()
    att_copy = fetch(att_in, pre, 2)
    first_t_copy = fetch(first_t_in, normed_t, 1)
    load_slot(qkv_in.at[0], 0).start()
    load_slot(qkv_in.at[2], 2).start()
    one_copy.wait()

    def through_two(r, carry):
        at = rows_at(r, TILE)
        unit, rate = norm_stats(hidden[at, :])
        upstream = back[at, :]
        add_norm(2, upstream, unit)
        result = grad[at, :] + norm_back(unit, rate, norms[2:3, :], upstream)
        grad[at, :] = result
        branch[at, :] = result.astype(BF16)
        branch_t[:, at] = result.T.astype(BF16)
        return carry

    lax.fori_loop(0, tiles, through_two, 0)
    zero_copy = fetch(zero_in, hidden, 0)
    pump("wide", ("first", 1, 3), ("second", 0, 2))
    att_copy.wait()

    def other_half(c):
        return pl.ds(pl.multiple_of(c * half, SPAN), half)

    def store(which, b, at, value):
        if which == 1 and fused:
            thin.own[b, at, :] = value
        else:
            thin_posted[4 * which + b, at, :] = value

    def out_weigh(m, carry):
        at = rows_at(m, TILE)
        for which in range(2):
            c = core if which else 1 - core
            store(which, 3, at, nn(branch_t[at, :], pre[:, other_half(c)]).astype(BF16))
        return carry

    lax.fori_loop(0, side, out_weigh, 0)
    thin_copy(3).start()
    if not fused:
        thin_kept(3).start()
    for c in range(2):
        for b in range(4):
            load_thin(b, c).wait()
    keyt_copy = fetch(keyt_in, branch_t, 3)

    def spread_att(r, carry):
        at = rows_at(r, TILE)
        rows = branch[at, :]
        for c in range(2):
            slots[3, at, c * half : (c + 1) * half] = nn(rows, weights[2 + c, :, half:]).astype(BF16)
        return carry

    lax.fori_loop(0, tiles, spread_att, 0)
    pump("thin", ("take", 3), ("first", 3))
    count = blocks // 2

    def probs_copy(unit):
        slot = lax.rem(unit, 2)
        return pltpu.make_async_copy(probs_in.at[pl.ds(unit * count, count)], probs.at[slot], probs_sems.at[slot])

    probs_copy((1 - core) * pairs).start()
    load_slot(qkv_in.at[0], 0).wait()
    load_slot(qkv_in.at[2], 2).wait()
    keyt_copy.wait()
    low, high = halves_of((1, SPAN), 1, 0.125)
    low_one, high_one = halves_of((1, SPAN), 1, 1.0)

    def attend(pair, carry):
        cols = pl.ds(pl.multiple_of(pair * SPAN, SPAN), SPAN)
        acc[...] = jnp.zeros(acc.shape, F32)
        for part in range(2):
            unit = 2 * pair + part

            @pl.when(lax.rem(unit + 1, pairs) != 0)
            def ahead():
                probs_copy(unit + 1).start()

            probs_copy(unit).wait()
            for k in range(count):
                i = part * count + k
                w0 = window_start(i, blocks)
                here = slice(i * SPAN, (i + 1) * SPAN)
                there = slice(w0, w0 + WINDOW)
                up_rows = slots[3, here, cols]
                ups = jnp.concatenate([up_rows * low_one, up_rows * high_one], axis=0)
                queries = slots[0, here, cols]
                asks = jnp.concatenate([queries * low, queries * high], axis=0)
                prob = probs[part, k]
                wide = prob.astype(F32)
                grad_probs = nt(slots[2, there, cols], ups)
                inner = jnp.sum(grad_probs * wide, axis=0, keepdims=True)
                grad_scores = (wide * (grad_probs - inner)).astype(BF16)
                acc[0, there, :] += nn(grad_scores, asks)
                acc[1, there, :] += nn(prob, ups)
                asked = nn(branch_t[cols, there], grad_scores)
                slots[0, here, cols] = (pick_halves(asked).T * 0.125).astype(BF16)
        slots[1, :, cols] = acc[0].astype(BF16)
        slots[2, :, cols] = acc[1].astype(BF16)
        return carry

    def qkv_weigh(which):
        cols = other_half(core if which else 1 - core)

        def body(m, carry):
            at = rows_at(m, TILE)
            rows = normed_t[at, :]
            for j in range(3):
                store(which, j, at, nn(rows, slots[j, :, cols]).astype(BF16))
            return carry

        lax.fori_loop(0, side, body, 0)

    few = pairs // 2
    for which in range(2):
        base = (core if which else 1 - core) * few
        lax.fori_loop(base, base + 1, attend, 0)
        if which == 0:
            pump("wide", ("second", 1, 3))
        else:
            pump("wide", ("third", 1, 3))
        lax.fori_loop(base + 1, base + few, attend, 0)
        if which == 0:
            probs_copy(core * pairs).start()
            first_t_copy.wait()
            pump("thin", ("second", 3))
            pump("wide", ("third", 0, 2))
        else:
            pump("thin", ("third", 3), ("take", 0, 1))
        qkv_weigh(which)
        for j in range(3):
            if which == 0:
                thin_copy(j).start()
            elif not fused:
                thin_kept(j).start()
    zero_copy.wait()
    pump("thin", ("take", 2), ("first", 0, 1, 2))

    def through_one(r, carry):
        at = rows_at(r, TILE)
        upstream = jnp.zeros((TILE, width), F32)
        for c in range(2):
            cols = slice(c * half, (c + 1) * half)
            upstream = upstream + nt(slots[0, at, cols], weights[c, :, :half])
            upstream = upstream + nt(slots[1, at, cols], weights[c, :, half:])
            upstream = upstream + nt(slots[2, at, cols], weights[2 + c, :, :half])
        unit, rate = norm_stats(hidden[at, :])
        add_norm(0, upstream, unit)
        grad_zero = (grad[at, :] + norm_back(unit, rate, norms[0:1, :], upstream)).astype(BF16)
        small[:, u0 : u0 + width] += nn(noisy[at, :].astype(F32).T.astype(BF16), grad_zero)
        grad_start = (keep_root * nt(grad_zero, up_low[...]) - error[at, :]).T
        upper = grad_start.astype(BF16)
        lower = (grad_start - upper.astype(F32)).astype(BF16)
        hot = (columns[at, 0:1] == ids).astype(F32).astype(BF16)
        small[:, e0 : e0 + vocab] += nn(upper, hot) + nn(lower, hot)
        return carry

    lax.fori_loop(0, tiles // 2, through_one, 0)
    pump("thin", ("second", 0, 1, 2))
    lax.fori_loop(tiles // 2, tiles, through_one, 0)
    lanes = emb
    n0 = e0 + vocab
    for k in range(6):
        for j in range(width // lanes):
            row = k * (width // lanes) + j
            small[row : row + 1, n0 : n0 + lanes] = norm_grads[k : k + 1, j * lanes : (j + 1) * lanes]
    if not fused:
        row = lax.broadcasted_iota(jnp.int32, out_scalars.shape, 0)
        out_scalars[...] = jnp.where(row == 1, loss, jnp.where(row == 2, weight_total, 0.0))
        for slot, b in ((0, 1), (1, 3)):
            sent(post_copy(b, slot))
            kept_copy(b, 2 + slot).wait()
        for b in range(4):
            sent(thin_copy(b))
            thin_kept(b).wait()
        return

    group = small.shape[1] // 4
    for q in range(4):
        value = small[:, q * group : (q + 1) * group].astype(BF16)
        rows = slice((q % 2) * small.shape[0], (q % 2 + 1) * small.shape[0])
        mine = core == q // 2

        @pl.when(mine)
        def keep():
            tiny.own[0, rows, :] = value

        @pl.when(jnp.logical_not(mine))
        def give():
            small_own[rows, :] = value

    give_copy = tiny.pair_copy(0, small_own)
    give_copy.start()
    tiny.take(0)
    pump("thin", ("third", 0, 1, 2))
    tiny.first(0)
    squares = wide.result(0) + wide.result(1) + wide.result(2) + wide.result(3) + thin.result(3)
    tiny.second(0)
    tiny.third(0)
    squares = squares + tiny.result(0)
    tiny_shard[...] = tiny_out[0].astype(BF16)
    gather = QuickGather(tiny_shard, tiny_whole, gather_refs, 16)
    gather.begin()
    squares = squares + thin.result(0) + thin.result(1) + thin.result(2)
    row = lax.broadcasted_iota(jnp.int32, scalars.shape, 0)
    scalars[...] = jnp.where(row == 0, squares, jnp.where(row == 1, loss, 0.0))
    exchange = Exchange(scalars, slots_all, all_send, all_recv, devices)
    exchange.start()
    gather.spread()
    gather.ready()
    exchange.arrive()
    out_scalars[...] = jnp.where(row == 2, weight_total, exchange.total())
    for q in range(4):
        rows = slice((q % 2) * small.shape[0], (q % 2 + 1) * small.shape[0])
        out_small[:, q * group : (q + 1) * group] = tiny_whole[q // 2, rows, :].astype(F32)
    for slot, b in ((0, 1), (1, 3)):
        sent(post_copy(b, slot))
    for b in range(4):
        sent(thin_copy(b))
    give_copy.wait_send()
    gather.finish()
    exchange.finish()
    for b in range(4):
        wide.finish(b)
        thin.finish(b)
    tiny.finish(0)


def run_backward(fused, wide_whole, thin_whole, tokens, buckets, counted, counts, start, noisy, table_low, kept, up_weight, down_weight, norms, steps, vocab_used):
    zero, one, two, qkv, key_t, att, probs, act, slope, first_t, second_t = kept
    length, width = zero.shape
    pairs = width // SPAN
    blocks = length // SPAN
    emb, vocab = start.shape[1], table_low.shape[0]
    dma, vmem = pltpu.SemaphoreType.DMA, pltpu.VMEM
    anywhere, inside = pl.BlockSpec(memory_space=pl.ANY), pl.BlockSpec(memory_space=pltpu.VMEM)
    spread = 2 * width + vocab + emb
    group = spread // 4
    rows = width // 16

    def made(shape, dtype=BF16):
        return jax.ShapeDtypeStruct(shape, dtype)

    wide_out = made((4, rows, width), F32) if fused else made((4, 2, width, width))
    thin_out = made((4, rows, width // 2), F32) if fused else made((4, 2, width, width // 2))
    out_shape = [wide_out, thin_out, made((emb, spread), F32), made((8, 128), F32)]
    if fused:
        out_shape += [made((4, width, width)), made((4, width, width // 2)), made((1, 2 * emb, group))]
    else:
        out_shape += [made((8, 128))] * 3
    scratch = [
        vmem((length, width), F32),
        vmem((length, width), F32),
        vmem((length, width), F32),
        vmem((length, width), BF16),
        vmem((width, length), BF16),
        vmem((width, length), BF16),
        vmem((length, width), BF16),
        vmem((4, length, width), BF16),
        vmem((4, width, width), BF16),
        vmem((2, length, SPAN), F32),
        vmem((2, blocks // 2, WINDOW, 2 * SPAN), BF16),
        vmem((length, emb), F32),
        vmem((8, width), F32),
        vmem((2 if fused else 4, width, width), BF16),
        vmem((4 if fused else 8, width, width // 2), BF16),
        vmem((2 * emb, group), BF16),
        vmem((8, 128), F32),
        vmem((length, 8), F32),
        vmem((emb, width), BF16),
        vmem((width, emb), BF16),
        dma((4,)),
        dma((4,)),
        dma((12,)),
        dma((2,)),
        dma((12,)),
    ]
    if fused:
        scratch += scatter_scratch(4, rows, width) + scatter_scratch(4, rows, width // 2) + scatter_scratch(1, 16, group)
        scratch += [
            vmem((2, width, width), BF16),
            vmem((2 * emb, group), BF16),
            vmem((16, group), BF16),
            vmem((2, 2 * emb, group), BF16),
            vmem((1, 16, group), F32),
            vmem((32, 8, 128), F32),
            dma((32,)),
            dma((32,)),
        ] + quick_sems()
        params = pltpu.CompilerParams(collective_id=1, has_side_effects=True, vmem_limit_bytes=VMEM_LIMIT)
    else:
        params = pltpu.CompilerParams(vmem_limit_bytes=VMEM_LIMIT)
    return pl.pallas_call(
        functools.partial(backward_kernel, fused, (length, width, pairs, vocab_used)),
        out_shape=out_shape,
        in_specs=[anywhere] * 2 + [inside] * 6 + [anywhere] * 11 + [inside] * 4 + [pl.BlockSpec(memory_space=pltpu.SMEM)],
        out_specs=[inside if fused else anywhere] * 2 + [inside] * 2 + [anywhere] * 3,
        scratch_shapes=scratch,
        compiler_params=params,
        name="backward",
    )(wide_whole, thin_whole, tokens, buckets, counted, counts, start, noisy, zero, one, two, qkv, key_t, att, probs, act, slope, first_t, second_t, table_low, up_weight, down_weight, norms, steps)[:4]


def adam_update(weight, grad, first, second, rate, decay):
    first_new = BETA_FIRST * first + (1.0 - BETA_FIRST) * grad
    second_new = BETA_SECOND * second + (1.0 - BETA_SECOND) * grad * grad
    first_hat = first_new / (1.0 - BETA_FIRST**STEP)
    second_hat = second_new / (1.0 - BETA_SECOND**STEP)
    weight_new = weight - rate * (first_hat / (jnp.sqrt(second_hat) + ADAM_EPS) + decay * weight)
    return (first_new, second_new, weight_new)


def clip_factor(squares):
    grad_norm = jnp.sqrt(squares)
    return grad_norm, jnp.minimum(1.0, CLIP_NORM / (grad_norm + 1e-06))


def adam_kernel(wide, thin, small, scalars, *refs):
    states, outs = refs[:24], refs[24:]
    width = wide.shape[2]
    emb = small.shape[0]
    vocab = states[0].shape[0]
    grad_norm, factor = clip_factor(scalars[0:1, 0:1])
    for out, value in zip(outs[:3], (scalars[1:2, 0:1], scalars[2:3, 0:1], grad_norm)):
        out[...] = value

    def step(index, grad, *at):
        rate, decay = (NORM_RATE, 0.0) if index == 7 else (MATRIX_RATE, WEIGHT_DECAY)
        at = at or (Ellipsis,)
        weight, first, second = (ref[at] for ref in states[3 * index : 3 * index + 3])
        values = adam_update(weight, factor * grad, first, second, rate, decay)
        for out, value in zip(outs[3 + 3 * index : 6 + 3 * index], values):
            out[at] = value

    step(0, small[:, 2 * width : -emb].T[:vocab])
    step(1, small[:, width : 2 * width])
    step(2, small[:, :width].T)
    for j in range(3):
        step(3, thin[j], j)
    step(4, thin[3])
    for h in range(2):
        cols = slice(h * width, (h + 1) * width)
        step(5, wide[h], slice(None), cols)
        step(6, wide[2 + h], slice(None), cols)
    per = width // emb
    for k in range(6):
        for j in range(per):
            row = k * per + j
            step(7, small[row : row + 1, -emb:], slice(k, k + 1), slice(j * emb, (j + 1) * emb))


def run_adam(wide, thin, small, scalars, states):
    inside = pl.BlockSpec(memory_space=pltpu.VMEM)
    out_shape = [jax.ShapeDtypeStruct((1, 1), F32)] * 3
    out_shape += [jax.ShapeDtypeStruct(states[3 * (k // 3)].shape, F32) for k in range(24)]
    return pl.pallas_call(
        adam_kernel,
        out_shape=out_shape,
        in_specs=[inside] * 28,
        out_specs=[inside] * 27,
        compiler_params=pltpu.CompilerParams(vmem_limit_bytes=VMEM_LIMIT),
        name="adam",
    )(wide, thin, small, scalars, *states)


def shards_of(qkv_weight, out_t, fc_weight, proj_t):
    width = fc_weight.shape[1] // 2
    wide = [array[:, h * width : (h + 1) * width] for array in (fc_weight, proj_t) for h in range(2)]
    return jnp.stack(wide).astype(BF16), jnp.concatenate([qkv_weight, out_t[None]]).astype(BF16)


def finished(results):
    return tuple(value.T if k in (15, 16, 17, 21, 22, 23) else value for k, value in enumerate(results))


def per_device(fused, token_ids, segment_ids, timesteps, noise, bucket_ids, counted, embed, up_weight, down_weight, qkv_weight, out_weight, fc_weight, proj_weight, norm_params, embed_m, embed_v, up_m, up_v, down_m, down_v, qkv_m, qkv_v, out_m, out_v, fc_m, fc_v, proj_m, proj_v, norm_m, norm_v):
    length = token_ids.shape[1]
    vocab, emb = embed.shape
    width = up_weight.shape[1]
    places = jnp.asarray(place_table(length, width))
    if fused:
        sources = (qkv_weight, out_weight.T, fc_weight, proj_weight.T)
    else:

        def gathered(shard):
            return lax.all_gather(lax.all_gather(shard, "dp", axis=1, tiled=True), "mp", axis=1)

        sources = tuple(map(gathered, shards_of(qkv_weight, out_weight.T, fc_weight, proj_weight.T)))
    wide_whole, thin_whole, counts, start, noisy, table_low, *kept = run_forward(
        fused, sources, token_ids, segment_ids, timesteps, noise, bucket_ids, counted, embed, up_weight, norm_params, places
    )
    if not fused:
        wide_whole, thin_whole = sources
        counts = lax.psum(counts, "dp")
    wide, thin, small, scalars = run_backward(
        fused, wide_whole, thin_whole, token_ids, bucket_ids, counted, counts, start, noisy, table_low, kept, up_weight, down_weight, norm_params, timesteps, vocab
    )
    states = (
        embed, embed_m, embed_v, up_weight, up_m, up_v, down_weight, down_m, down_v, qkv_weight, qkv_m, qkv_v,
        out_weight.T, out_m.T, out_v.T, fc_weight, fc_m, fc_v, proj_weight.T, proj_m.T, proj_v.T, norm_params, norm_m, norm_v,
    )
    if fused:
        results = list(run_adam(wide, thin, small, scalars, states))
        results[:3] = [value.reshape(()) for value in results[:3]]
        return finished(results)

    def owned(blocks):
        blocks = lax.psum_scatter(blocks.astype(F32), "mp", scatter_dimension=1, tiled=False)
        return lax.psum_scatter(blocks, "dp", scatter_dimension=1, tiled=True)

    wide, thin = owned(wide), owned(thin)
    small, loss_sum = lax.psum((small, scalars[1, 0]), ("dp", "mp"))
    squares = lax.psum(jnp.sum(wide * wide) + jnp.sum(thin * thin), ("dp", "mp")) + jnp.sum(small * small)
    grad_norm, factor = clip_factor(squares)
    grads = (
        small[:, 2 * width : -emb].T[:vocab],
        small[:, width : 2 * width],
        small[:, :width].T,
        thin[:3],
        thin[3],
        jnp.concatenate([wide[0], wide[1]], axis=1),
        jnp.concatenate([wide[2], wide[3]], axis=1),
        small[: 6 * width // emb, -emb:].reshape(6, width),
    )
    results = [loss_sum, scalars[2, 0], grad_norm]
    for index, grad in enumerate(grads):
        rate, decay = (NORM_RATE, 0.0) if index == 7 else (MATRIX_RATE, WEIGHT_DECAY)
        weight, first, second = states[3 * index : 3 * index + 3]
        results.extend(adam_update(weight, factor * grad, first, second, rate, decay))
    return finished(results)


def solution(mesh):
    fused = mesh.shape["dp"] == 16 and mesh.shape["mp"] == 2
    state = {"copied": P(), "qkv": P(None, "dp", "mp"), "tall": P("mp", "dp"), "wide": P("dp", "mp")}
    kinds = ["copied"] * 3 + ["qkv", "tall", "wide", "tall", "copied"]
    weights = [state[kind] for kind in kinds]
    moments = [state[kind] for kind in kinds for unused in range(2)]
    placed = (
        P("dp", None), P("dp", None), P("dp"), P("dp", None, None), P("dp", None), P("dp", None),
        *weights,
        *moments,
    )
    outs = (P(), P(), P()) + tuple(state[kind] for kind in kinds for unused in range(3))
    return jax.shard_map(
        functools.partial(per_device, fused), mesh=mesh, in_specs=placed, out_specs=outs, check_vma=False
    )
```

```python
import functools
import math

import jax
import jax.numpy as jnp
import numpy as np
from jax import lax
from jax.experimental import pallas as pl
from jax.experimental.pallas import tpu as pltpu
from jax.sharding import PartitionSpec as P

HEAD_DIM = 64
NB = 16
T_STEPS = 2000
STEP = 10

NORM_EPS = 1e-05
MASKED = -1e30
BETA_FIRST = 0.9
BETA_SECOND = 0.999
ADAM_EPS = 1e-08
MATRIX_RATE = 0.05
NORM_RATE = 0.5
WEIGHT_DECAY = 0.1
CLIP_NORM = 0.01

TILE = 256
SPAN = 128
WINDOW = 384
MESH = pl.DeviceIdType.MESH
F32 = jnp.float32
BF16 = jnp.bfloat16
VMEM_LIMIT = 62 * 2**20


def nn(left, right):
    return jnp.dot(left, right, preferred_element_type=F32)


def nt(left, right):
    return lax.dot_general(
        left, right, (((1,), (1,)), ((), ())), preferred_element_type=F32
    )


def sine_row(step, width):
    half = width // 2
    lane = lax.broadcasted_iota(jnp.int32, (1, half), 1).astype(F32)
    angles = step * jnp.exp(lane * (-math.log(10000.0) / half))
    return jnp.concatenate([jnp.sin(angles), jnp.cos(angles)], axis=1)


def place_table(length, width):
    half = width // 2
    freqs = np.exp(-math.log(10000.0) * np.arange(half, dtype=np.float64) / half)
    angles = np.arange(length, dtype=np.float64)[:, None] * freqs[None, :]
    return np.concatenate([np.sin(angles), np.cos(angles)], axis=-1).astype(np.float32)


def norm_stats(values):
    width = values.shape[-1]
    center = values - jnp.sum(values, axis=-1, keepdims=True) * (1.0 / width)
    spread = jnp.sum(center * center, axis=-1, keepdims=True) * (1.0 / width)
    rate = lax.rsqrt(spread + NORM_EPS)
    return center * rate, rate


def norm_back(unit, rate, gain, upstream):
    width = unit.shape[-1]
    scaled = upstream * gain
    first = jnp.sum(scaled, axis=-1, keepdims=True) * (1.0 / width)
    second = jnp.sum(scaled * unit, axis=-1, keepdims=True) * (1.0 / width)
    return rate * (scaled - first - unit * second)


def column_sum(values):
    return jnp.sum(values, axis=0, keepdims=True)


def rows_at(index, count):
    return pl.ds(pl.multiple_of(index * count, count), count)


def guarded(condition, action):
    if condition is None:
        action()
    else:
        pl.when(condition)(action)


def position():
    me = lax.axis_index("dp")
    return me, lax.axis_index("mp"), me // 4, lax.rem(me // 2, 2), lax.rem(me, 2)


def index_of(z, y, x):
    return z * 4 + y * 2 + x


def neighbours():
    me, core, z, y, x = position()
    return (index_of(z, y, 1 - x), core), (index_of(z, 1 - y, x), core), (me, 1 - core)


def remote(source, target, send_sem, recv_sem, device):
    return pltpu.make_async_remote_copy(
        src_ref=source,
        dst_ref=target,
        send_sem=send_sem,
        recv_sem=recv_sem,
        device_id=device,
        device_id_type=MESH,
    )


def greet(devices):
    me, core = position()[:2]
    barrier = pltpu.get_barrier_semaphore()
    for device in devices:

        @pl.when(jnp.logical_or(device[0] != me, device[1] != core))
        def signal():
            pl.semaphore_signal(barrier, inc=1, device_id=device, device_id_type=MESH)


def assemble(devices):
    pl.semaphore_wait(pltpu.get_barrier_semaphore(), len(devices) - 1)


class Exchange:
    def __init__(self, source, slots, sems, devices):
        self.source, self.slots, self.sems = source, slots, sems
        me, core = position()[:2]
        self.devices = [(device, jnp.logical_or(device[0] != me, device[1] != core)) for device in devices]
        self.mine = me if len(devices) == 16 else 2 * me + core

    def start(self):
        for device, other in self.devices:
            guarded(other, lambda: remote(self.source, self.slots.at[self.mine], self.sems.at[0], self.sems.at[1], device).start())

    def all_but_one(self):
        rest = self.slots.at[: len(self.devices) - 1]
        return remote(rest, rest, self.sems.at[0], self.sems.at[1], neighbours()[2])

    def arrive(self):
        self.all_but_one().wait_recv()

    def total(self):
        self.slots[self.mine] = self.source[...]
        value = self.slots[0]
        for slot in range(1, len(self.devices)):
            value = value + self.slots[slot]
        return value

    def finish(self):
        self.all_but_one().wait_send()


def same_core():
    core = position()[1]
    return [(d, core) for d in range(16)]


def every_device():
    return [(d, c) for d in range(16) for c in range(2)]


class Gather:
    def __init__(self, shard, whole, sems, rows):
        self.shard, self.whole, self.rows = shard, whole, rows
        (self.local_s, self.up_s, self.down_s, self.plane_s, self.pair_s, self.line_r, self.turn_r, self.last_r, self.pair_r) = sems
        self.xn, self.yn, self.pair = neighbours()
        self.me, self.core, self.z, self.y, self.x = position()
        self.up = (jnp.minimum(self.me + 4, 15), self.core)
        self.down = (jnp.maximum(self.me - 4, 0), self.core)

    def piece(self, b, c, d):
        return self.whole.at[b, c, rows_at(d, self.rows), :]

    def send(self, b, d, own, device, sem, recv, condition=None):
        source = self.shard.at[b] if own else self.piece(b, self.core, d)
        guarded(condition, lambda: remote(source, self.piece(b, self.core, d), sem, recv, device).start())

    def pieces(self, b, count, sem, recv):
        some = self.whole.at[b, self.core, : count * self.rows, :]
        return remote(some, some, sem, recv, self.pair)

    def spread(self, b, d, zz, own=False, condition=None):
        odd = lax.rem(zz, 2)
        for step in range(2):
            along_y = odd if step == 0 else 1 - odd
            device = (index_of(self.z, jnp.where(along_y == 1, 1 - self.y, self.y), jnp.where(along_y == 1, self.x, 1 - self.x)), self.core)
            recv = self.turn_r.at[b, zz] if step == 0 else self.last_r.at[b]
            self.send(b, d, own, device, self.plane_s.at[b], recv, condition)
        self.send(b, d, own, self.pair, self.pair_s.at[b], self.pair_r.at[b], condition)

    def local(self, b):
        return pltpu.make_async_copy(self.shard.at[b], self.piece(b, self.core, self.me), self.local_s.at[b])

    def begin(self, b):
        self.local(b).start()
        self.send(b, self.me, True, self.up, self.up_s.at[b], self.line_r.at[b, self.z], self.z < 3)
        self.send(b, self.me, True, self.down, self.down_s.at[b], self.line_r.at[b, self.z], self.z > 0)
        self.spread(b, self.me, self.z, True)

    def hop(self, b, distance):
        z = self.z
        for source, there, onward, device, sem in (
            (jnp.maximum(z - distance, 0), z >= distance, z < 3, self.up, self.up_s),
            (jnp.minimum(z + distance, 3), z + distance <= 3, z > 0, self.down, self.down_s),
        ):
            d = index_of(source, self.y, self.x)
            guarded(there, lambda: self.pieces(b, 1, self.up_s.at[b], self.line_r.at[b, source]).wait_recv())
            if distance < 3:
                self.send(b, d, False, device, sem.at[b], self.line_r.at[b, source], jnp.logical_and(there, onward))
            self.spread(b, d, source, False, there)

    def turn(self, b):
        for zz in range(4):
            yy, xx = (1 - self.y, self.x) if zz % 2 else (self.y, 1 - self.x)
            d = index_of(zz, yy, xx)
            self.pieces(b, 1, self.up_s.at[b], self.turn_r.at[b, zz]).wait_recv()
            self.send(b, d, False, self.xn if zz % 2 else self.yn, self.plane_s.at[b], self.last_r.at[b])
            self.send(b, d, False, self.pair, self.pair_s.at[b], self.pair_r.at[b])

    def last(self, b):
        self.pieces(b, 8, self.up_s.at[b], self.last_r.at[b]).wait_recv()
        for zz in range(4):
            yy, xx = (self.y, 1 - self.x) if zz % 2 else (1 - self.y, self.x)
            for d in (index_of(zz, yy, xx), index_of(zz, 1 - self.y, 1 - self.x)):
                self.send(b, d, False, self.pair, self.pair_s.at[b], self.pair_r.at[b])

    def ready(self, b):
        self.local(b).wait()
        self.pieces(b, 16, self.up_s.at[b], self.pair_r.at[b]).wait_recv()

    def finish(self):
        for b in range(self.shard.shape[0]):
            self.pieces(b, 12, self.plane_s.at[b], self.pair_r.at[b]).wait_send()
            self.pieces(b, 16, self.pair_s.at[b], self.pair_r.at[b]).wait_send()
            for z in range(4):

                @pl.when(self.z == z)
                def line():
                    if z < 3:
                        self.pieces(b, z + 1, self.up_s.at[b], self.pair_r.at[b]).wait_send()
                    if z > 0:
                        self.pieces(b, 4 - z, self.down_s.at[b], self.pair_r.at[b]).wait_send()


class QuickGather:
    def __init__(self, shard, whole, sems, rows):
        self.shard, self.whole, self.rows, self.sems = shard, whole, rows, sems
        self.me, self.core, self.z, self.y, self.x = position()

    def piece(self, c, d):
        return self.whole.at[rows_at(16 * c + d, self.rows), :]

    def send(self, d, own, device, recv, condition=None):
        source = self.shard if own else self.piece(self.core, d)
        guarded(condition, lambda: remote(source, self.piece(self.core, d), self.sems.at[1], self.sems.at[recv], device).start())

    def pieces(self, count, recv):
        some = self.whole.at[: count * self.rows, :]
        return remote(some, some, self.sems.at[1], self.sems.at[recv], (self.me, 1 - self.core))

    def local(self):
        return pltpu.make_async_copy(self.shard, self.piece(self.core, self.me), self.sems.at[0])

    def plane(self, zz, own, condition=None):
        d = index_of(zz, self.y, self.x)
        for yy, xx in ((self.y, 1 - self.x), (1 - self.y, self.x), (1 - self.y, 1 - self.x)):
            for c in range(2):
                self.send(d, own, (index_of(self.z, yy, xx), c), 3, condition)

    def begin(self):
        self.local().start()
        for zz in range(4):
            there = index_of(zz, self.y, self.x)
            self.send(self.me, True, (there, self.core), 2, self.z != zz)
            self.send(self.me, True, (there, 1 - self.core), 3)
        self.plane(self.z, True)

    def spread(self):
        self.pieces(3, 2).wait_recv()
        for zz in range(4):
            self.plane(zz, False, self.z != zz)

    def ready(self):
        self.local().wait()
        self.pieces(28, 3).wait_recv()

    def finish(self):
        self.pieces(31, 2).wait_send()


GATHER_REFS = 9


def gather_sems(count):
    dma = pltpu.SemaphoreType.DMA
    one, four = dma((count,)), dma((count, 4))
    return [one, one, one, one, one, four, four, one, one]


class Scatter:
    def __init__(self, refs, landed, loaded, out, rows):
        (self.own, self.near, self.far, self.lined, self.pair_s, self.pair_r, self.load_s) = refs[:7]
        self.near_s, self.near_r, self.far_s, self.far_r, self.line_s, self.line_r = refs[7:]
        self.landed, self.loaded, self.out, self.rows = landed, loaded, out, rows
        self.xn, self.yn, self.pair = neighbours()
        self.me, self.core, self.z, self.y, self.x = position()

    def piece(self, b, zz, yy, xx):
        return self.own.at[b, rows_at(index_of(zz, yy, xx), self.rows), :]

    def pair_copy(self, b, source):
        return remote(source, self.landed.at[b], self.pair_s.at[b], self.pair_r.at[b], self.pair)

    def load(self, b):
        return pltpu.make_async_copy(self.landed.at[b], self.loaded[b], self.load_s.at[b])

    def near_copy(self, b, zz, i):
        place, device = ((zz, i, 1 - self.x), self.xn) if zz % 2 else ((zz, 1 - self.y, i), self.yn)
        group = jnp.where(i == self.onward(zz), 0, 1)
        return remote(
            self.piece(b, *place), self.near.at[b, zz, i], self.near_s.at[b], self.near_r.at[b, group], device
        )

    def onward(self, zz):
        return 1 - self.y if zz % 2 else 1 - self.x

    def far_place(self, zz):
        return (zz, 1 - self.y, self.x) if zz % 2 else (zz, self.y, 1 - self.x)

    def far_copy(self, b, zz):
        return remote(
            self.piece(b, *self.far_place(zz)), self.far.at[b, zz], self.far_s.at[b], self.far_r.at[b],
            self.yn if zz % 2 else self.xn,
        )

    def line_copy(self, b, zz):
        there = (index_of(zz, self.y, self.x), self.core)
        return remote(
            self.near.at[b, zz, 1 - self.onward(zz)], self.lined.at[b, self.z], self.line_s.at[b], self.line_r.at[b], there
        )

    def pieces(self, b, count, send_sem, recv_sem):
        some = self.own.at[b, : count * self.rows, :]
        return remote(some, some, send_sem.at[b], recv_sem, self.pair)

    def take(self, b):
        self.pair_copy(b, self.own.at[b]).wait_recv()
        self.load(b).start()

    def first(self, b):
        self.load(b).wait()
        loaded = self.loaded[b]

        def add(d, carry):
            at = rows_at(d, self.rows)
            self.own[b, at, :] = (self.own[b, at, :].astype(F32) + loaded[at, :].astype(F32)).astype(self.own.dtype)
            return carry

        lax.fori_loop(0, 16, add, 0)
        for zz in range(4):
            self.near_copy(b, zz, self.onward(zz)).start()
        for zz in range(4):
            self.near_copy(b, zz, 1 - self.onward(zz)).start()

    def second(self, b):
        self.pieces(b, 4, self.near_s, self.near_r.at[b, 0]).wait_recv()
        for zz in range(4):
            i = self.onward(zz)
            place = self.far_place(zz)
            value = self.piece(b, *place)[...].astype(F32) + self.near[b, zz, i].astype(F32)
            self.piece(b, *place)[...] = value.astype(self.own.dtype)
            self.far_copy(b, zz).start()

    def third(self, b):
        self.pieces(b, 4, self.near_s, self.near_r.at[b, 1]).wait_recv()
        self.pieces(b, 4, self.near_s, self.far_r.at[b]).wait_recv()
        for zz in range(4):
            i = 1 - self.onward(zz)
            value = self.piece(b, zz, self.y, self.x)[...].astype(F32) + self.near[b, zz, i].astype(F32) + self.far[b, zz].astype(F32)

            @pl.when(self.z == zz)
            def keep():
                self.out[b] = value

            @pl.when(self.z != zz)
            def give():
                self.near[b, zz, i] = value.astype(self.near.dtype)
                self.line_copy(b, zz).start()

    def result(self, b):
        self.pieces(b, 3, self.near_s, self.line_r.at[b]).wait_recv()
        for zz in range(4):

            @pl.when(self.z != zz)
            def add():
                self.out[b] += self.lined[b, zz].astype(F32)

        value = self.out[b]
        return jnp.sum(value * value, keepdims=True)

    def finish(self, b):
        self.pieces(b, 8, self.near_s, self.line_r.at[b]).wait_send()
        self.pieces(b, 4, self.far_s, self.line_r.at[b]).wait_send()
        self.pieces(b, 3, self.line_s, self.line_r.at[b]).wait_send()


SCATTER_REFS = 13


def scatter_scratch(count, rows, columns):
    dma, vmem = pltpu.SemaphoreType.DMA, pltpu.VMEM
    return [
        vmem((count, 16 * rows, columns), BF16),
        vmem((count, 4, 2, rows, columns), BF16),
        vmem((count, 4, rows, columns), BF16),
        vmem((count, 4, rows, columns), BF16),
        dma((count,)), dma((count,)), dma((count,)),
        dma((count,)), dma((count, 2)), dma((count,)), dma((count,)), dma((count,)), dma((count,)),
    ]


def gelu_parts(values):
    root = 0.7978845608028654
    square = values * values
    half = 0.5 + 0.5 * jnp.tanh(values * (root + (root * 0.044715) * square))
    active = values * half
    return active, half + active * (1.0 - half) * (2.0 * root + (6.0 * root * 0.044715) * square)


def halves_of(shape, axis, scale):
    low = lax.broadcasted_iota(jnp.int32, shape, axis) < HEAD_DIM
    return jnp.where(low, scale, 0.0).astype(BF16), jnp.where(low, 0.0, scale).astype(BF16)


def pick_halves(wide):
    low = lax.broadcasted_iota(jnp.int32, (2 * HEAD_DIM, SPAN), 0) < HEAD_DIM
    return jnp.where(low, wide[:, :SPAN], wide[:, SPAN:])


def window_start(block, blocks):
    return min(max(block - 1, 0), blocks - WINDOW // SPAN) * SPAN


def column_table(rows, length):
    rows = rows + [jnp.zeros((1, length), F32)] * (8 - len(rows))
    return jnp.concatenate(rows, axis=0).T


def one_hot(ids, vocab):
    lanes = lax.broadcasted_iota(jnp.int32, (ids.shape[0], vocab), 1).astype(F32)
    return ids == lanes


def forward_kernel(fused, shapes, *refs):
    length, width, pairs = shapes
    blocks = length // SPAN
    tiles = length // TILE
    half = width // 2
    sources = 4 if fused else 2
    (
        tokens, segments, steps, noise_in, buckets, counted, embed_in, up_in, norms, places_in,
        wide_whole, thin_whole, count_out, start, noisy, table_low, zero_out, one_out, two_out, qkv_out, keyt_out, att_out, probs_out, act_out, slope_out, first_t_out, second_t_out,
        h_zero, h_one, h_two, normed, normed_t, qkv, key_t, value_t, att, probs, act, slope, weights, bias, places, table, table3, columns, count_own, noise, embed, up_weight,
        out_sems, probs_sems, weight_sems, in_sems,
    ) = refs[sources : sources + 53]
    rest = refs[sources + 53 :]
    core = lax.axis_index("mp")
    saves = []

    def save(source, target):
        copy = pltpu.make_async_copy(source, target, out_sems.at[len(saves)])
        copy.start()
        saves.append(copy)

    if fused:
        everyone = same_core() + [neighbours()[2]]
        greet(everyone)
        qkv_weight, out_weight, fc_weight, proj_weight = rest[:4]
        wide_shard, thin_shard, counts, count_sems = rest[4:8]
        rows = wide_shard.shape[1]
        wide = Gather(wide_shard, wide_whole, rest[8 : 8 + GATHER_REFS], rows)
        thin = Gather(thin_shard, thin_whole, rest[8 + GATHER_REFS :], rows)
        gathers = {"wide": wide, "thin": thin}
        moves = list(zip(refs[:4], rest[:4]))
    else:
        moves = []
    moves += [(noise_in.at[core], noise), (embed_in, embed), (up_in, up_weight), (places_in, places)]
    fetches = [pltpu.make_async_copy(source, target, in_sems.at[k]) for k, (source, target) in enumerate(moves)]
    for copy in fetches:
        copy.start()
    if fused:
        wide_from, thin_from = wide_whole, thin_whole
        for copy in fetches[:4]:
            copy.wait()
        for j in range(3):
            thin_shard[j] = qkv_weight[j].astype(BF16)
        thin_shard[3] = out_weight[...].astype(BF16)
        for h in range(2):
            cols = slice(h * width, (h + 1) * width)
            wide_shard[h] = fc_weight[:, cols].astype(BF16)
            wide_shard[2 + h] = proj_weight[:, cols].astype(BF16)
    else:
        wide_from, thin_from = refs[:2]

    def pump(*items):
        if fused:
            for which, name, b, *more in items:
                getattr(gathers[which], name)(b, *more)

    live = counted[...].astype(F32)
    lane = lax.broadcasted_iota(jnp.int32, count_own.shape, 1)
    own_counts = jnp.zeros(count_own.shape, F32)
    for bucket in range(NB):
        found = jnp.sum(jnp.where(buckets[...] == bucket, live, 0.0), keepdims=True)
        own_counts = jnp.where(lane == bucket, found, own_counts)
    count_own[...] = own_counts
    token_row = tokens[pl.ds(core, 1), :].astype(F32)
    segment_row = segments[pl.ds(core, 1), :].astype(F32)
    columns[...] = column_table([token_row, segment_row], length)
    emb = embed.shape[1]
    for copy in fetches[-4:]:
        copy.wait()
    table[...] = jnp.zeros(table.shape, F32)
    table[: embed.shape[0], :] = embed[...]
    left = table[...]
    for third in range(3):
        part = left.astype(BF16)
        table3[:, third * emb : (third + 1) * emb] = part
        if third == 0:
            table_low[...] = part
        left = left - part.astype(F32)
    step = jnp.full((1, 1), steps[core], jnp.int32).astype(F32)
    keep = 1.0 - jnp.sqrt(step * (1.0 / T_STEPS) + 0.0001)
    keep_root, noise_root = jnp.sqrt(keep), jnp.sqrt(1.0 - keep)
    time_row = sine_row(step, width)
    up_low = up_weight[...].astype(BF16)

    def embed_tile(r):
        at = rows_at(r, TILE)
        hot = one_hot(columns[at, 0:1], table.shape[0]).astype(F32).astype(BF16)
        thirds = nn(hot, table3[...])
        first = thirds[:, :emb] + thirds[:, emb : 2 * emb] + thirds[:, 2 * emb :]
        start[at, :] = first
        low = (keep_root * first + noise_root * noise[at, :]).astype(BF16)
        noisy[at, :] = low
        hidden = nn(low, up_low) + places[at, :] + time_row
        h_zero[at, :] = hidden
        unit = norm_stats(hidden)[0]
        scaled = unit * norms[0:1, :] + norms[1:2, :]
        normed[at, :] = scaled.astype(BF16)
        normed_t[0, :, at] = scaled.T.astype(BF16)

    if fused:
        assemble(everyone)
        exchange = Exchange(count_own, counts, count_sems, same_core())
        exchange.start()
    early = range(3)
    pump(*[("thin", "begin", b) for b in early])
    for r in range(tiles):
        embed_tile(r)
        if r < 3:
            pump(*[("thin", "hop", b, r + 1) for b in early])
    pump(*[("thin", "turn", b) for b in early])
    second_group = [("thin", 3), ("wide", 0), ("wide", 1)]
    third_group = [("wide", 2), ("wide", 3)]

    def steps(group, name, *more):
        return [(which, name, b, *more) for which, b in group]

    pump(*steps(second_group, "begin"))
    save(h_zero, zero_out)
    save(normed_t.at[0], first_t_out)
    for i in range(blocks):
        w0 = window_start(i, blocks)
        same = columns[w0 : w0 + WINDOW, 1:2] == segment_row[:, i * SPAN : (i + 1) * SPAN]
        bias[i] = jnp.where(same, 0.0, MASKED)
    pump(*[("thin", "last", b) for b in early])

    def load_wide(b, c, slot):
        return pltpu.make_async_copy(wide_from.at[b, c], weights.at[slot], weight_sems.at[slot])

    def load_thin(b, c):
        slot, side = 2 * (b // 2) + c, b % 2
        return pltpu.make_async_copy(
            thin_from.at[b, c], weights.at[slot, :, side * half : (side + 1) * half], weight_sems.at[slot + 8 * side]
        )

    pump(*[("thin", "ready", b) for b in early])
    for c in range(2):
        for b in early:
            load_thin(b, c).start()
    pump(*steps(second_group, "hop", 1))
    for c in range(2):
        for b in early:
            load_thin(b, c).wait()
    for c in range(2):

        def project(r, carry):
            at = rows_at(r, TILE)
            rows = normed[at, :]
            first = nn(rows, weights[c])
            values = nn(rows, weights[2 + c, :, :half])
            cols = slice(c * half, (c + 1) * half)
            qkv[0, at, cols] = first[:, :half].astype(BF16)
            qkv[1, at, cols] = first[:, half:].astype(BF16)
            qkv[2, at, cols] = values.astype(BF16)
            key_t[cols, at] = first[:, half:].T.astype(BF16)
            value_t[cols, at] = values.T.astype(BF16)
            return carry

        lax.fori_loop(0, tiles, project, 0, unroll=True)
        if c == 0:
            pump(*steps(second_group, "hop", 2))
    for j in range(3):
        save(qkv.at[j], qkv_out.at[j])
    save(key_t, keyt_out)

    def probs_copy(pair, slot):
        return pltpu.make_async_copy(probs.at[slot], probs_out.at[pl.ds(pair * blocks, blocks)], probs_sems.at[slot])

    low, high = halves_of((1, SPAN), 1, 0.125)

    def attend(pair, carry):
        slot = lax.rem(pair, 2)
        cols = pl.ds(pl.multiple_of(pair * SPAN, SPAN), SPAN)

        @pl.when(pair >= 2)
        def free():
            probs_copy(pair - 2, slot).wait()

        def ask(i):
            w0 = window_start(i, blocks)
            queries = qkv[0, i * SPAN : (i + 1) * SPAN, cols]
            both = jnp.concatenate([queries * low, queries * high], axis=0)
            return nt(qkv[1, w0 : w0 + WINDOW, cols], both)

        def answer(i, prob):
            w0 = window_start(i, blocks)
            mixed = nn(value_t[cols, w0 : w0 + WINDOW], prob)
            att[i * SPAN : (i + 1) * SPAN, cols] = pick_halves(mixed).T.astype(BF16)

        ahead, behind = ask(0), None
        for i in range(blocks):
            mask = bias[i]
            scores = ahead + jnp.concatenate([mask, mask], axis=1)
            if i + 1 < blocks:
                ahead = ask(i + 1)
            if i > 0:
                answer(i - 1, behind)
            most = jnp.max(scores, axis=0, keepdims=True)
            raised = jnp.exp(scores - most)
            share = 1.0 / jnp.sum(raised, axis=0, keepdims=True)
            behind = (raised * share).astype(BF16)
            probs[slot, i] = behind
        answer(blocks - 1, behind)
        probs_copy(pair, slot).start()
        return carry

    middle = [
        steps(second_group, "hop", 3) + steps(third_group, "begin"),
        steps(second_group[:2], "turn"),
        steps(second_group[2:], "turn") + steps(third_group, "hop", 1),
        steps(second_group[:1], "last"),
        steps(third_group, "hop", 2),
        [],
    ]
    for part in range(6):
        lax.fori_loop(part * pairs // 6, (part + 1) * pairs // 6, attend, 0)
        pump(*middle[part])
    for pair in (pairs - 2, pairs - 1):
        probs_copy(pair, pair % 2).wait()
    save(att, att_out)
    pump(("thin", "ready", 3))
    for c in range(2):
        load_thin(3, c).start()
    for c in range(2):
        load_thin(3, c).wait()

    def after_attention(r, carry):
        at = rows_at(r, TILE)
        mixed = att[at, :]
        total = nt(mixed[:, :half], weights[2, :, half:]) + nt(mixed[:, half:], weights[3, :, half:])
        hidden = h_zero[at, :] + total
        h_one[at, :] = hidden
        unit = norm_stats(hidden)[0]
        scaled = unit * norms[2:3, :] + norms[3:4, :]
        normed[at, :] = scaled.astype(BF16)
        normed_t[1, :, at] = scaled.T.astype(BF16)
        return carry

    lax.fori_loop(0, tiles, after_attention, 0, unroll=True)
    save(h_one, one_out)
    save(normed_t.at[1], second_t_out)
    pump(*steps(third_group, "hop", 3), *steps(second_group[1:], "last"), *steps(second_group[1:], "ready"))
    for j in range(4):
        load_wide(j // 2, j % 2, 4 + j).start()
    for j in range(4):
        load_wide(j // 2, j % 2, 4 + j).wait()
        stages = [(slice(k, k + TILE), slice(r, r + 2 * TILE)) for k in range(0, width, TILE) for r in range(0, length, 2 * TILE)]

        def before_gelu(stage):
            chunk, at = stage
            return nn(normed[at, :], weights[4 + j, :, chunk])

        ahead = before_gelu(stages[0])
        for k, (chunk, at) in enumerate(stages):
            before = ahead
            if k + 1 < len(stages):
                ahead = before_gelu(stages[k + 1])
            active, bend = gelu_parts(before)
            act[j, at, chunk] = active.astype(BF16)
            slope[j, at, chunk] = bend.astype(BF16)
        save(act.at[j], act_out.at[j])
        save(slope.at[j], slope_out.at[j])
        if j < 2:
            pump(("wide", "turn", 2 + j))
        else:
            pump(("wide", "last", j), ("wide", "ready", j))
            for c in range(2):
                load_wide(j, c, 2 * (j - 2) + c).start()

    for h in range(2):
        for c in range(2):
            load_wide(2 + h, c, 2 * h + c).wait()

        def shrink(r, carry):
            at = rows_at(r, TILE)
            total = (h_two if h else h_one)[at, :]
            for j in (2 * h, 2 * h + 1):
                total = total + nt(act[j, at, :], weights[j])
            h_two[at, :] = total
            return carry

        lax.fori_loop(0, tiles, shrink, 0, unroll=True)
    save(h_two, two_out)
    if fused:
        exchange.arrive()
        count_out[...] = exchange.total()
        wide.finish()
        thin.finish()
        exchange.finish()
    else:
        count_out[...] = count_own[...]
    for copy in saves:
        copy.wait()


def run_forward(fused, sources, tokens, segments, steps, noise, buckets, counted, embed, up_weight, norms, places):
    length, width = places.shape
    pairs = width // SPAN
    blocks = length // SPAN
    dma, vmem = pltpu.SemaphoreType.DMA, pltpu.VMEM
    anywhere, inside = pl.BlockSpec(memory_space=pl.ANY), pl.BlockSpec(memory_space=pltpu.VMEM)
    vocab, emb = embed.shape
    padded = -(-vocab // 128) * 128

    def made(shape, dtype=BF16):
        return jax.ShapeDtypeStruct(shape, dtype)

    out_shape = [
        made((4, 2, width, width)),
        made((4, 2, width, width // 2)),
        made((8, 128), F32),
        made((length, emb), F32),
        made((length, emb)),
        made((padded, emb)),
        made((length, width), F32),
        made((length, width), F32),
        made((length, width), F32),
        made((3, length, width)),
        made((width, length)),
        made((length, width)),
        made((pairs * blocks, WINDOW, 2 * SPAN)),
        made((4, length, width)),
        made((4, length, width)),
        made((width, length)),
        made((width, length)),
    ]
    scratch = [
        vmem((length, width), F32),
        vmem((length, width), F32),
        vmem((length, width), F32),
        vmem((length, width), BF16),
        vmem((2, width, length), BF16),
        vmem((3, length, width), BF16),
        vmem((width, length), BF16),
        vmem((width, length), BF16),
        vmem((length, width), BF16),
        vmem((2, blocks, WINDOW, 2 * SPAN), BF16),
        vmem((4, length, width), BF16),
        vmem((4, length, width), BF16),
        vmem((8, width, width), BF16),
        vmem((blocks, WINDOW, SPAN), F32),
        vmem((length, width), F32),
        vmem((padded, emb), F32),
        vmem((padded, 3 * emb), BF16),
        vmem((length, 8), F32),
        vmem((8, 128), F32),
        vmem((length, emb), F32),
        vmem((vocab, emb), F32),
        vmem((emb, width), F32),
        dma((20,)),
        dma((2,)),
        dma((12,)),
        dma((8,)),
    ]
    params = dict(vmem_limit_bytes=VMEM_LIMIT)
    if fused:
        rows = width // 16
        scratch += [vmem(source.shape, F32) for source in sources]
        scratch += [vmem((4, rows, width), BF16), vmem((4, rows, width // 2), BF16)]
        scratch += [vmem((16, 8, 128), F32), dma((2,))] + gather_sems(4) + gather_sems(4)
        params.update(collective_id=0, has_side_effects=True)
    return pl.pallas_call(
        functools.partial(forward_kernel, fused, (length, width, pairs)),
        out_shape=out_shape,
        in_specs=[anywhere] * len(sources)
        + [inside, inside, pl.BlockSpec(memory_space=pltpu.SMEM), anywhere]
        + [inside] * 2
        + [anywhere] * 2
        + [inside, anywhere],
        out_specs=[anywhere] * 2 + [inside] * 4 + [anywhere] * 11,
        scratch_shapes=scratch,
        compiler_params=pltpu.CompilerParams(**params),
        name="forward",
    )(*sources, tokens, segments, steps, noise, buckets, counted, embed, up_weight, norms, places)


def backward_kernel(fused, shapes, *refs):
    length, width, pairs, vocab_used = shapes
    blocks = length // SPAN
    tiles = length // TILE
    half = width // 2
    (
        wide_whole, thin_whole, tokens, buckets, counted, counts, start, noisy, zero_in, one_in, two_in, qkv_in, keyt_in, att_in, probs_in, act_in, slope_in, first_t_in, second_t_in,
        embed_low, up_weight, down_weight, norms, steps,
        out_wide, out_thin, out_small, out_scalars, wide_landed, thin_landed, small_landed,
        hidden, grad, back, branch, branch_t, normed_t, pre, slots, weights, acc, probs, error, norm_grads, posted, thin_posted, scalars, columns, up_low, down_low,
        load_sems, slot_sems, weight_sems, probs_sems, post_sems,
    ) = refs[:55]
    core = lax.axis_index("mp")
    small = out_small
    emb = start.shape[1]
    vocab = embed_low.shape[0]
    side = width // TILE

    if fused:
        rest = refs[55:]
        n = SCATTER_REFS
        loaded, tiny_shard, tiny_out, slots_all, all_sems, quick_sems = rest[3 * n :]
        group = out_small.shape[1] // 4
        tiny_loaded = branch.at[: 2 * emb, :group]
        small_own = branch.at[2 * emb : 4 * emb, :group]
        tiny_whole = pre.at[: 4 * emb, :group]
        wide_loaded = [loaded.at[b // 2] for b in range(4)]
        thin_loaded = [loaded.at[b // 2, :, (b % 2) * half : (b % 2 + 1) * half] for b in range(4)]
        wide = Scatter(rest[:n], wide_landed, wide_loaded, out_wide, width // 16)
        thin = Scatter(rest[n : 2 * n], thin_landed, thin_loaded, out_thin, width // 16)
        tiny = Scatter(rest[2 * n : 3 * n], small_landed, [tiny_loaded], tiny_out, 16)
        devices = every_device()
        greet(devices)

    def pump(scatter_name, *steps):
        if fused:
            scatter = wide if scatter_name == "wide" else thin
            for name, *members in steps:
                for b in members:
                    getattr(scatter, name)(b)

    def posted_half(b):
        return posted.at[b // 2, :, (b % 2) * half : (b % 2 + 1) * half]

    def post_copy(b, slot):
        if fused:
            return wide.pair_copy(b, posted.at[slot])
        return pltpu.make_async_copy(posted.at[slot], out_wide.at[b, 1 - core], post_sems.at[slot])

    def thin_copy(b):
        if fused:
            return thin.pair_copy(b, posted_half(b))
        return pltpu.make_async_copy(thin_posted.at[b], out_thin.at[b, 1 - core], post_sems.at[4 + b])

    def kept_copy(b, slot):
        return pltpu.make_async_copy(posted.at[slot], out_wide.at[b, core], post_sems.at[slot])

    def thin_kept(b):
        return pltpu.make_async_copy(thin_posted.at[4 + b], out_thin.at[b, core], post_sems.at[8 + b])

    def sent(copy):
        (copy.wait_send if fused else copy.wait)()

    def fetch(source, target, k):
        copy = pltpu.make_async_copy(source, target, load_sems.at[k])
        copy.start()
        return copy

    def load_weights(b, c, slot):
        return pltpu.make_async_copy(wide_whole.at[b, c], weights.at[slot], weight_sems.at[slot])

    def load_thin(b, c):
        slot, part = 2 * (b // 2) + c, b % 2
        return pltpu.make_async_copy(
            thin_whole.at[b, c], weights.at[slot, :, part * half : (part + 1) * half], weight_sems.at[4 + 2 * b + c]
        )

    def load_slot(source, slot):
        return pltpu.make_async_copy(source, slots.at[slot], slot_sems.at[slot])

    def feed(s):
        h, c = s // 2, (1 - core if s % 2 == 0 else core)
        first = 2 * (s % 2)
        return [
            load_weights(h, c, first),
            load_weights(2 + h, c, first + 1),
            load_slot(act_in.at[2 * h + c], first),
            load_slot(slope_in.at[2 * h + c], first + 1),
        ]

    two_copy = fetch(two_in, hidden, 0)
    normed_copy = fetch(second_t_in, normed_t, 1)
    for copy in feed(0):
        copy.start()
    norm_grads[...] = jnp.zeros(norm_grads.shape, F32)
    columns[...] = jnp.zeros(columns.shape, F32)
    small[...] = jnp.zeros(small.shape, F32)
    count_row = counts[0:1, :]
    live_total = jnp.sum(count_row, keepdims=True)
    bucket_weight = live_total / (NB * jnp.maximum(count_row, 1.0))
    weight_total = jnp.sum(count_row * bucket_weight, keepdims=True)
    bucket_row = buckets[pl.ds(core, 1), :]
    scale = jnp.zeros((1, length), F32)
    for bucket in range(NB):
        scale = jnp.where(bucket_row == bucket, bucket_weight[:, bucket : bucket + 1], scale)
    scale = scale * counted[pl.ds(core, 1), :].astype(F32)
    columns[0:1, :] = tokens[pl.ds(core, 1), :].astype(F32)
    columns[1:2, :] = scale
    columns[2:3, :] = scale / weight_total
    step = jnp.full((1, 1), steps[core], jnp.int32).astype(F32)
    keep_root = jnp.sqrt(1.0 - jnp.sqrt(step * (1.0 / T_STEPS) + 0.0001))
    up_low[...] = up_weight[...].astype(BF16)
    down_low[...] = down_weight[...].astype(BF16)
    ids = lax.broadcasted_iota(jnp.int32, (TILE, vocab), 1).astype(F32)
    pad_row = jnp.where(lax.broadcasted_iota(jnp.int32, (1, vocab), 1) < vocab_used, 0.0, MASKED)
    two_copy.wait()
    d0, u0, e0 = 0, width, 2 * width

    def add_norm(row, upstream, unit):
        norm_grads[row : row + 1, :] += column_sum(upstream * unit)
        norm_grads[row + 1 : row + 2, :] += column_sum(upstream)

    def head(r, loss):
        at = rows_at(r, TILE)
        unit, rate = norm_stats(hidden[at, :])
        ended = (unit * norms[4:5, :] + norms[5:6, :]).astype(BF16)
        predicted = nn(ended, down_low[...])
        pred_low = predicted.astype(BF16)
        logits = nt(pred_low, embed_low[...]) + pad_row
        most = jnp.max(logits, axis=-1, keepdims=True)
        raised = jnp.exp(logits - most)
        total = jnp.sum(raised, axis=-1, keepdims=True)
        table = columns[:, at].T
        hit = table[:, 0:1] == ids
        picked = jnp.sum(jnp.where(hit, logits, 0.0), axis=-1, keepdims=True)
        miss = predicted - start[at, :]
        per_token = jnp.sum(miss * miss, axis=-1, keepdims=True) * (1.0 / emb) + (jnp.log(total) + most) - picked
        loss = loss + jnp.sum(table[:, 1:2] * per_token, keepdims=True)
        coef = table[:, 2:3]
        grad_logits = (coef * (raised * (1.0 / total) - jnp.where(hit, 1.0, 0.0))).astype(BF16)
        grad_error = coef * 2.0 * miss * (1.0 / emb)
        error[at, :] = grad_error
        grad_pred = nn(grad_logits, embed_low[...]) + grad_error
        grad_pred_low = grad_pred.astype(BF16)
        small[:, d0 : d0 + width] += nn(grad_pred.T.astype(BF16), ended)
        small[:, e0 : e0 + vocab] += nn(predicted.T.astype(BF16), grad_logits)
        upstream = nt(grad_pred_low, down_low[...])
        add_norm(4, upstream, unit)
        result = norm_back(unit, rate, norms[4:5, :], upstream)
        grad[at, :] = result
        branch[at, :] = result.astype(BF16)
        branch_t[:, at] = result.T.astype(BF16)
        return loss

    loss = lax.fori_loop(0, tiles, head, jnp.zeros((1, 1), F32))
    one_copy = fetch(one_in, hidden, 0)
    normed_copy.wait()

    for s in range(4):
        h = s // 2
        if s < 3:
            for copy in feed(s + 1):
                copy.start()
        for copy in feed(s):
            copy.wait()
        first = 2 * (s % 2)
        fc, proj, active, bend = weights.at[first], weights.at[first + 1], slots.at[first], slots.at[first + 1]

        def through(r):
            at = slice(r * TILE, (r + 1) * TILE)
            pushed = (nn(branch[at, :], proj[...]) * bend[at, :].astype(F32)).astype(BF16)
            pre[at, :] = pushed
            return pushed

        ahead = through(0)
        for r in range(tiles):
            at = slice(r * TILE, (r + 1) * TILE)
            pushed = ahead
            if r + 1 < tiles:
                ahead = through(r + 1)
            value = nt(pushed, fc[...])
            if s == 0:
                back[at, :] = value
            else:
                back[at, :] += value
        mine = s % 2 == 1
        if s == 2:
            sent(post_copy(0, 0))
            sent(post_copy(2, 1))
        if s == 2:
            pump("wide", ("first", 0, 2))
        if s == 3 and not fused:
            kept_copy(0, 2).wait()
            kept_copy(2, 3).wait()

        def weigh(m, carry):
            at = rows_at(m, TILE)
            fc_grad = nn(normed_t[at, :], pre[...]).astype(BF16)
            proj_grad = nn(branch_t[at, :], active[...]).astype(BF16)
            if mine and fused:
                wide.own[h, at, :] = fc_grad
                wide.own[2 + h, at, :] = proj_grad
            else:
                posted[2 if mine else 0, at, :] = fc_grad
                posted[3 if mine else 1, at, :] = proj_grad
            return carry

        lax.fori_loop(0, side, weigh, 0, unroll=True)
        if s == 0 and fused:
            assemble(devices)
        if not mine:
            post_copy(h, 0).start()
            post_copy(2 + h, 1).start()
        elif not fused:
            kept_copy(h, 2).start()
            kept_copy(2 + h, 3).start()
        if mine:
            pump("wide", ("take", h, 2 + h))

    for c in range(2):
        for b in range(4):
            load_thin(b, c).start()
    att_copy = fetch(att_in, pre, 2)
    first_t_copy = fetch(first_t_in, normed_t, 1)
    load_slot(qkv_in.at[0], 0).start()
    load_slot(qkv_in.at[2], 2).start()
    one_copy.wait()

    def through_two(r, carry):
        at = rows_at(r, TILE)
        unit, rate = norm_stats(hidden[at, :])
        upstream = back[at, :]
        add_norm(2, upstream, unit)
        result = grad[at, :] + norm_back(unit, rate, norms[2:3, :], upstream)
        grad[at, :] = result
        branch[at, :] = result.astype(BF16)
        branch_t[:, at] = result.T.astype(BF16)
        return carry

    lax.fori_loop(0, tiles, through_two, 0)
    zero_copy = fetch(zero_in, hidden, 0)
    pump("wide", ("first", 1, 3))
    att_copy.wait()

    def other_half(c):
        return pl.ds(pl.multiple_of(c * half, SPAN), half)

    def store(which, b, at, value):
        if fused and which == 1:
            thin.own[b, at, :] = value
        elif fused:
            posted_half(b)[at, :] = value
        else:
            thin_posted[4 * which + b, at, :] = value

    def out_weigh(m, carry):
        at = rows_at(m, TILE)
        for which in range(2):
            c = core if which else 1 - core
            store(which, 3, at, nn(branch_t[at, :], pre[:, other_half(c)]).astype(BF16))
        return carry

    if fused:
        sent(post_copy(1, 0))
        sent(post_copy(3, 1))
    lax.fori_loop(0, side, out_weigh, 0, unroll=True)
    thin_copy(3).start()
    if not fused:
        thin_kept(3).start()
    for c in range(2):
        for b in range(4):
            load_thin(b, c).wait()
    keyt_copy = fetch(keyt_in, branch_t, 3)

    def spread_att(r, carry):
        at = rows_at(r, TILE)
        rows = branch[at, :]
        for c in range(2):
            slots[3, at, c * half : (c + 1) * half] = nn(rows, weights[2 + c, :, half:]).astype(BF16)
        return carry

    lax.fori_loop(0, tiles, spread_att, 0, unroll=True)
    pump("wide", ("second", 0, 2))
    pump("thin", ("take", 3), ("first", 3))
    count = blocks // 2

    def probs_copy(unit):
        slot = lax.rem(unit, 2)
        return pltpu.make_async_copy(probs_in.at[pl.ds(unit * count, count)], probs.at[slot], probs_sems.at[slot])

    probs_copy((1 - core) * pairs).start()
    load_slot(qkv_in.at[0], 0).wait()
    load_slot(qkv_in.at[2], 2).wait()
    keyt_copy.wait()
    low, high = halves_of((1, SPAN), 1, 0.125)
    low_one, high_one = halves_of((1, SPAN), 1, 1.0)

    def attend(pair, carry):
        cols = pl.ds(pl.multiple_of(pair * SPAN, SPAN), SPAN)
        acc[...] = jnp.zeros(acc.shape, F32)
        for part in range(2):
            unit = 2 * pair + part

            @pl.when(lax.rem(unit + 1, pairs) != 0)
            def ahead():
                probs_copy(unit + 1).start()

            probs_copy(unit).wait()

            def ask(k):
                i = part * count + k
                w0 = window_start(i, blocks)
                up_rows = slots[3, i * SPAN : (i + 1) * SPAN, cols]
                ups = jnp.concatenate([up_rows * low_one, up_rows * high_one], axis=0)
                return ups, nt(slots[2, w0 : w0 + WINDOW, cols], ups)

            ahead = ask(0)
            for k in range(count):
                i = part * count + k
                w0 = window_start(i, blocks)
                here = slice(i * SPAN, (i + 1) * SPAN)
                there = slice(w0, w0 + WINDOW)
                ups, grad_probs = ahead
                if k + 1 < count:
                    ahead = ask(k + 1)
                queries = slots[0, here, cols]
                asks = jnp.concatenate([queries * low, queries * high], axis=0)
                prob = probs[part, k]
                wide_probs = prob.astype(F32)
                inner = jnp.sum(grad_probs * wide_probs, axis=0, keepdims=True)
                grad_scores = (wide_probs * (grad_probs - inner)).astype(BF16)
                acc[1, there, :] += nn(prob, ups)
                acc[0, there, :] += nn(grad_scores, asks)
                asked = nn(branch_t[cols, there], grad_scores)
                slots[0, here, cols] = (pick_halves(asked).T * 0.125).astype(BF16)
        slots[1, :, cols] = acc[0].astype(BF16)
        slots[2, :, cols] = acc[1].astype(BF16)
        return carry

    def qkv_weigh(which):
        cols = other_half(core if which else 1 - core)

        def body(m, carry):
            at = rows_at(m, TILE)
            rows = normed_t[at, :]
            for j in range(3):
                store(which, j, at, nn(rows, slots[j, :, cols]).astype(BF16))
            return carry

        lax.fori_loop(0, side, body, 0, unroll=True)

    few = pairs // 2
    for which in range(2):
        base = (core if which else 1 - core) * few
        lax.fori_loop(base, base + 1, attend, 0)
        if which == 1:
            pump("wide", ("third", 0, 2))
        lax.fori_loop(base + 1, base + few, attend, 0)
        if which == 0:
            probs_copy(core * pairs).start()
            first_t_copy.wait()
            pump("wide", ("second", 1, 3))
        else:
            pump("thin", ("second", 3), ("take", 0, 1))
        qkv_weigh(which)
        for j in range(3):
            if which == 0:
                thin_copy(j).start()
            elif not fused:
                thin_kept(j).start()
    zero_copy.wait()
    pump("thin", ("take", 2), ("first", 0, 1, 2))
    pump("wide", ("third", 1, 3))

    def through_one(r, carry):
        at = rows_at(r, TILE)
        upstream = jnp.zeros((TILE, width), F32)
        for c in range(2):
            cols = slice(c * half, (c + 1) * half)
            upstream = upstream + nt(slots[0, at, cols], weights[c, :, :half])
            upstream = upstream + nt(slots[1, at, cols], weights[c, :, half:])
            upstream = upstream + nt(slots[2, at, cols], weights[2 + c, :, :half])
        unit, rate = norm_stats(hidden[at, :])
        add_norm(0, upstream, unit)
        grad_zero = (grad[at, :] + norm_back(unit, rate, norms[0:1, :], upstream)).astype(BF16)
        small[:, u0 : u0 + width] += nn(noisy[at, :].astype(F32).T.astype(BF16), grad_zero)
        grad_start = (keep_root * nt(grad_zero, up_low[...]) - error[at, :]).T
        upper = grad_start.astype(BF16)
        lower = (grad_start - upper.astype(F32)).astype(BF16)
        hot = (columns[:, at].T[:, 0:1] == ids).astype(F32).astype(BF16)
        small[:, e0 : e0 + vocab] += nn(upper, hot) + nn(lower, hot)
        return carry

    lax.fori_loop(0, tiles // 2, through_one, 0)
    pump("thin", ("second", 0, 1, 2), ("third", 3))
    lax.fori_loop(tiles // 2, tiles, through_one, 0)
    lanes = emb
    n0 = e0 + vocab
    for k in range(6):
        for j in range(width // lanes):
            row = k * (width // lanes) + j
            small[row : row + 1, n0 : n0 + lanes] = norm_grads[k : k + 1, j * lanes : (j + 1) * lanes]
    if not fused:
        row = lax.broadcasted_iota(jnp.int32, out_scalars.shape, 0)
        out_scalars[...] = jnp.where(row == 1, loss, jnp.where(row == 2, weight_total, 0.0))
        for slot, b in ((0, 1), (1, 3)):
            sent(post_copy(b, slot))
            kept_copy(b, 2 + slot).wait()
        for b in range(4):
            sent(thin_copy(b))
            thin_kept(b).wait()
        return

    for q in range(4):
        value = small[:, q * group : (q + 1) * group].astype(BF16)
        rows = slice((q % 2) * small.shape[0], (q % 2 + 1) * small.shape[0])
        mine = core == q // 2

        @pl.when(mine)
        def keep():
            tiny.own[0, rows, :] = value

        @pl.when(jnp.logical_not(mine))
        def give():
            small_own[rows, :] = value

    give_copy = tiny.pair_copy(0, small_own)
    give_copy.start()
    tiny.take(0)
    pump("thin", ("third", 0, 1, 2))
    tiny.first(0)
    squares = wide.result(0) + wide.result(1) + wide.result(2) + wide.result(3) + thin.result(3)
    tiny.second(0)
    tiny.third(0)
    squares = squares + tiny.result(0)
    tiny_shard[...] = tiny_out[0].astype(BF16)
    gather = QuickGather(tiny_shard, tiny_whole, quick_sems, 16)
    gather.begin()
    squares = squares + thin.result(0) + thin.result(1) + thin.result(2)
    row = lax.broadcasted_iota(jnp.int32, scalars.shape, 0)
    scalars[...] = jnp.where(row == 0, squares, jnp.where(row == 1, loss, 0.0))
    exchange = Exchange(scalars, slots_all, all_sems, devices)
    exchange.start()
    gather.spread()
    gather.ready()
    exchange.arrive()
    out_scalars[...] = jnp.where(row == 2, weight_total, exchange.total())
    for q in range(4):
        rows = slice((q % 2) * small.shape[0], (q % 2 + 1) * small.shape[0])
        out_small[:, q * group : (q + 1) * group] = tiny_whole[(q // 2) * 2 * emb : (q // 2 + 1) * 2 * emb, :][rows, :].astype(F32)
    for b in range(4):
        sent(thin_copy(b))
    give_copy.wait_send()
    gather.finish()
    exchange.finish()
    for b in range(4):
        wide.finish(b)
        thin.finish(b)
    tiny.finish(0)


def run_backward(fused, wide_whole, thin_whole, tokens, buckets, counted, counts, start, noisy, table_low, kept, up_weight, down_weight, norms, steps, vocab_used):
    zero, one, two, qkv, key_t, att, probs, act, slope, first_t, second_t = kept
    length, width = zero.shape
    pairs = width // SPAN
    blocks = length // SPAN
    emb, vocab = start.shape[1], table_low.shape[0]
    dma, vmem = pltpu.SemaphoreType.DMA, pltpu.VMEM
    anywhere, inside = pl.BlockSpec(memory_space=pl.ANY), pl.BlockSpec(memory_space=pltpu.VMEM)
    spread = 2 * width + vocab + emb
    group = spread // 4
    rows = width // 16

    def made(shape, dtype=BF16):
        return jax.ShapeDtypeStruct(shape, dtype)

    wide_out = made((4, rows, width), F32) if fused else made((4, 2, width, width))
    thin_out = made((4, rows, width // 2), F32) if fused else made((4, 2, width, width // 2))
    out_shape = [wide_out, thin_out, made((emb, spread), F32), made((8, 128), F32)]
    if fused:
        out_shape += [made((4, width, width)), made((4, width, width // 2)), made((1, 2 * emb, group))]
    else:
        out_shape += [made((8, 128))] * 3
    scratch = [
        vmem((length, width), F32),
        vmem((length, width), F32),
        vmem((length, width), F32),
        vmem((length, width), BF16),
        vmem((width, length), BF16),
        vmem((width, length), BF16),
        vmem((length, width), BF16),
        vmem((4, length, width), BF16),
        vmem((4, width, width), BF16),
        vmem((2, length, SPAN), F32),
        vmem((2, blocks // 2, WINDOW, 2 * SPAN), BF16),
        vmem((length, emb), F32),
        vmem((8, width), F32),
        vmem((2 if fused else 4, width, width), BF16),
        vmem((8, 128) if fused else (8, width, width // 2), BF16),
        vmem((8, 128), F32),
        vmem((8, length), F32),
        vmem((emb, width), BF16),
        vmem((width, emb), BF16),
        dma((4,)),
        dma((4,)),
        dma((12,)),
        dma((2,)),
        dma((12,)),
    ]
    if fused:
        scratch += scatter_scratch(4, rows, width) + scatter_scratch(4, rows, width // 2) + scatter_scratch(1, 16, group)
        scratch += [
            vmem((2, width, width), BF16),
            vmem((16, group), BF16),
            vmem((1, 16, group), F32),
            vmem((32, 8, 128), F32),
            dma((2,)),
            dma((4,)),
        ]
        params = pltpu.CompilerParams(collective_id=1, has_side_effects=True, vmem_limit_bytes=VMEM_LIMIT)
    else:
        params = pltpu.CompilerParams(vmem_limit_bytes=VMEM_LIMIT)
    return pl.pallas_call(
        functools.partial(backward_kernel, fused, (length, width, pairs, vocab_used)),
        out_shape=out_shape,
        in_specs=[anywhere] * 2 + [inside] * 6 + [anywhere] * 11 + [inside] * 4 + [pl.BlockSpec(memory_space=pltpu.SMEM)],
        out_specs=[inside if fused else anywhere] * 2 + [inside] * 2 + [anywhere] * 3,
        scratch_shapes=scratch,
        compiler_params=params,
        name="backward",
    )(wide_whole, thin_whole, tokens, buckets, counted, counts, start, noisy, zero, one, two, qkv, key_t, att, probs, act, slope, first_t, second_t, table_low, up_weight, down_weight, norms, steps)[:4]


def adam_update(weight, grad, first, second, rate, decay):
    first_new = BETA_FIRST * first + (1.0 - BETA_FIRST) * grad
    second_new = BETA_SECOND * second + (1.0 - BETA_SECOND) * grad * grad
    first_hat = first_new / (1.0 - BETA_FIRST**STEP)
    second_hat = second_new / (1.0 - BETA_SECOND**STEP)
    weight_new = weight - rate * (first_hat / (jnp.sqrt(second_hat) + ADAM_EPS) + decay * weight)
    return (first_new, second_new, weight_new)


def clip_factor(squares):
    grad_norm = jnp.sqrt(squares)
    return grad_norm, jnp.minimum(1.0, CLIP_NORM / (grad_norm + 1e-06))


def adam_kernel(wide, thin, small, scalars, *refs):
    states, outs = refs[:24], refs[24:]
    width = wide.shape[2]
    emb = small.shape[0]
    vocab = states[0].shape[0]
    grad_norm, factor = clip_factor(scalars[0:1, 0:1])
    for out, value in zip(outs[:3], (scalars[1:2, 0:1], scalars[2:3, 0:1], grad_norm)):
        out[...] = value

    def step(index, grad, *at):
        rate, decay = (NORM_RATE, 0.0) if index == 7 else (MATRIX_RATE, WEIGHT_DECAY)
        at = at or (Ellipsis,)
        weight, first, second = (ref[at] for ref in states[3 * index : 3 * index + 3])
        values = adam_update(weight, factor * grad, first, second, rate, decay)
        for out, value in zip(outs[3 + 3 * index : 6 + 3 * index], values):
            out[at] = value

    step(0, small[:, 2 * width : -emb].T[:vocab])
    step(1, small[:, width : 2 * width])
    step(2, small[:, :width].T)
    for j in range(3):
        step(3, thin[j], j)
    step(4, thin[3])
    for h in range(2):
        cols = slice(h * width, (h + 1) * width)
        step(5, wide[h], slice(None), cols)
        step(6, wide[2 + h], slice(None), cols)
    per = width // emb
    for k in range(6):
        for j in range(per):
            row = k * per + j
            step(7, small[row : row + 1, -emb:], slice(k, k + 1), slice(j * emb, (j + 1) * emb))


def run_adam(wide, thin, small, scalars, states):
    inside = pl.BlockSpec(memory_space=pltpu.VMEM)
    out_shape = [jax.ShapeDtypeStruct((1, 1), F32)] * 3
    out_shape += [jax.ShapeDtypeStruct(states[3 * (k // 3)].shape, F32) for k in range(24)]
    return pl.pallas_call(
        adam_kernel,
        out_shape=out_shape,
        in_specs=[inside] * 28,
        out_specs=[inside] * 27,
        compiler_params=pltpu.CompilerParams(vmem_limit_bytes=VMEM_LIMIT),
        name="adam",
    )(wide, thin, small, scalars, *states)


def shards_of(qkv_weight, out_t, fc_weight, proj_t):
    width = fc_weight.shape[1] // 2
    wide = [array[:, h * width : (h + 1) * width] for array in (fc_weight, proj_t) for h in range(2)]
    return jnp.stack(wide).astype(BF16), jnp.concatenate([qkv_weight, out_t[None]]).astype(BF16)


def finished(results):
    return tuple(value.T if k in (15, 16, 17, 21, 22, 23) else value for k, value in enumerate(results))


def per_device(fused, token_ids, segment_ids, timesteps, noise, bucket_ids, counted, embed, up_weight, down_weight, qkv_weight, out_weight, fc_weight, proj_weight, norm_params, embed_m, embed_v, up_m, up_v, down_m, down_v, qkv_m, qkv_v, out_m, out_v, fc_m, fc_v, proj_m, proj_v, norm_m, norm_v):
    length = token_ids.shape[1]
    vocab, emb = embed.shape
    width = up_weight.shape[1]
    places = jnp.asarray(place_table(length, width))
    if fused:
        sources = (qkv_weight, out_weight.T, fc_weight, proj_weight.T)
    else:

        def gathered(shard):
            return lax.all_gather(lax.all_gather(shard, "dp", axis=1, tiled=True), "mp", axis=1)

        sources = tuple(map(gathered, shards_of(qkv_weight, out_weight.T, fc_weight, proj_weight.T)))
    wide_whole, thin_whole, counts, start, noisy, table_low, *kept = run_forward(
        fused, sources, token_ids, segment_ids, timesteps, noise, bucket_ids, counted, embed, up_weight, norm_params, places
    )
    if not fused:
        wide_whole, thin_whole = sources
        counts = lax.psum(counts, "dp")
    wide, thin, small, scalars = run_backward(
        fused, wide_whole, thin_whole, token_ids, bucket_ids, counted, counts, start, noisy, table_low, kept, up_weight, down_weight, norm_params, timesteps, vocab
    )
    states = (
        embed, embed_m, embed_v, up_weight, up_m, up_v, down_weight, down_m, down_v, qkv_weight, qkv_m, qkv_v,
        out_weight.T, out_m.T, out_v.T, fc_weight, fc_m, fc_v, proj_weight.T, proj_m.T, proj_v.T, norm_params, norm_m, norm_v,
    )
    if fused:
        results = list(run_adam(wide, thin, small, scalars, states))
        results[:3] = [value.reshape(()) for value in results[:3]]
        return finished(results)

    def owned(blocks):
        blocks = lax.psum_scatter(blocks.astype(F32), "mp", scatter_dimension=1, tiled=False)
        return lax.psum_scatter(blocks, "dp", scatter_dimension=1, tiled=True)

    wide, thin = owned(wide), owned(thin)
    small, loss_sum = lax.psum((small, scalars[1, 0]), ("dp", "mp"))
    squares = lax.psum(jnp.sum(wide * wide) + jnp.sum(thin * thin), ("dp", "mp")) + jnp.sum(small * small)
    grad_norm, factor = clip_factor(squares)
    grads = (
        small[:, 2 * width : -emb].T[:vocab],
        small[:, width : 2 * width],
        small[:, :width].T,
        thin[:3],
        thin[3],
        jnp.concatenate([wide[0], wide[1]], axis=1),
        jnp.concatenate([wide[2], wide[3]], axis=1),
        small[: 6 * width // emb, -emb:].reshape(6, width),
    )
    results = [loss_sum, scalars[2, 0], grad_norm]
    for index, grad in enumerate(grads):
        rate, decay = (NORM_RATE, 0.0) if index == 7 else (MATRIX_RATE, WEIGHT_DECAY)
        weight, first, second = states[3 * index : 3 * index + 3]
        results.extend(adam_update(weight, factor * grad, first, second, rate, decay))
    return finished(results)


def solution(mesh):
    fused = mesh.shape["dp"] == 16 and mesh.shape["mp"] == 2
    state = {"copied": P(), "qkv": P(None, "dp", "mp"), "tall": P("mp", "dp"), "wide": P("dp", "mp")}
    kinds = ["copied"] * 3 + ["qkv", "tall", "wide", "tall", "copied"]
    weights = [state[kind] for kind in kinds]
    moments = [state[kind] for kind in kinds for unused in range(2)]
    placed = (
        P("dp", None), P("dp", None), P("dp"), P("dp", None, None), P("dp", None), P("dp", None),
        *weights,
        *moments,
    )
    outs = (P(), P(), P()) + tuple(state[kind] for kind in kinds for unused in range(3))
    return jax.shard_map(
        functools.partial(per_device, fused), mesh=mesh, in_specs=placed, out_specs=outs, check_vma=False
    )
```

```python
import functools
import math

import jax
import jax.numpy as jnp
import numpy as np
from jax import lax
from jax.experimental import pallas as pl
from jax.experimental.pallas import tpu as pltpu
from jax.sharding import PartitionSpec as P

HEAD_DIM = 64
NB = 16
T_STEPS = 2000
STEP = 10

NORM_EPS = 1e-05
MASKED = -1e30
BETA_FIRST = 0.9
BETA_SECOND = 0.999
ADAM_EPS = 1e-08
MATRIX_RATE = 0.05
NORM_RATE = 0.5
WEIGHT_DECAY = 0.1
CLIP_NORM = 0.01

TILE = 256
SPAN = 128
WINDOW = 384
MESH = pl.DeviceIdType.MESH
F32 = jnp.float32
BF16 = jnp.bfloat16
VMEM_LIMIT = 62 * 2**20


def nn(left, right):
    return jnp.dot(left, right, preferred_element_type=F32)


def nt(left, right):
    return lax.dot_general(
        left, right, (((1,), (1,)), ((), ())), preferred_element_type=F32
    )


def sine_row(step, width):
    half = width // 2
    lane = lax.broadcasted_iota(jnp.int32, (1, half), 1).astype(F32)
    angles = step * jnp.exp(lane * (-math.log(10000.0) / half))
    return jnp.concatenate([jnp.sin(angles), jnp.cos(angles)], axis=1)


def place_table(length, width):
    half = width // 2
    freqs = np.exp(-math.log(10000.0) * np.arange(half, dtype=np.float64) / half)
    angles = np.arange(length, dtype=np.float64)[:, None] * freqs[None, :]
    return np.concatenate([np.sin(angles), np.cos(angles)], axis=-1).astype(np.float32)


def norm_stats(values):
    width = values.shape[-1]
    center = values - jnp.sum(values, axis=-1, keepdims=True) * (1.0 / width)
    spread = jnp.sum(center * center, axis=-1, keepdims=True) * (1.0 / width)
    rate = lax.rsqrt(spread + NORM_EPS)
    return center * rate, rate


def norm_back(unit, rate, gain, upstream):
    width = unit.shape[-1]
    scaled = upstream * gain
    first = jnp.sum(scaled, axis=-1, keepdims=True) * (1.0 / width)
    second = jnp.sum(scaled * unit, axis=-1, keepdims=True) * (1.0 / width)
    return rate * (scaled - first - unit * second)


def column_sum(values):
    return jnp.sum(values, axis=0, keepdims=True)


def rows_at(index, count):
    return pl.ds(pl.multiple_of(index * count, count), count)


def guarded(condition, action):
    if condition is None:
        action()
    else:
        pl.when(condition)(action)


def position():
    me = lax.axis_index("dp")
    return me, lax.axis_index("mp"), me // 4, lax.rem(me // 2, 2), lax.rem(me, 2)


def index_of(z, y, x):
    return z * 4 + y * 2 + x


def neighbours():
    me, core, z, y, x = position()
    return (index_of(z, y, 1 - x), core), (index_of(z, 1 - y, x), core), (me, 1 - core)


def remote(source, target, send_sem, recv_sem, device):
    return pltpu.make_async_remote_copy(
        src_ref=source,
        dst_ref=target,
        send_sem=send_sem,
        recv_sem=recv_sem,
        device_id=device,
        device_id_type=MESH,
    )


def greet(devices):
    me, core = position()[:2]
    barrier = pltpu.get_barrier_semaphore()
    for device in devices:

        @pl.when(jnp.logical_or(device[0] != me, device[1] != core))
        def signal():
            pl.semaphore_signal(barrier, inc=1, device_id=device, device_id_type=MESH)


def assemble(devices):
    pl.semaphore_wait(pltpu.get_barrier_semaphore(), len(devices) - 1)


class Exchange:
    def __init__(self, source, slots, sems, devices):
        self.source, self.slots, self.sems = source, slots, sems
        me, core = position()[:2]
        self.devices = [(device, jnp.logical_or(device[0] != me, device[1] != core)) for device in devices]
        self.mine = me if len(devices) == 16 else 2 * me + core

    def start(self):
        for device, other in self.devices:
            guarded(other, lambda: remote(self.source, self.slots.at[self.mine], self.sems.at[0], self.sems.at[1], device).start())

    def all_but_one(self):
        rest = self.slots.at[: len(self.devices) - 1]
        return remote(rest, rest, self.sems.at[0], self.sems.at[1], neighbours()[2])

    def arrive(self):
        self.all_but_one().wait_recv()

    def total(self):
        self.slots[self.mine] = self.source[...]
        value = self.slots[0]
        for slot in range(1, len(self.devices)):
            value = value + self.slots[slot]
        return value

    def finish(self):
        self.all_but_one().wait_send()


def same_core():
    core = position()[1]
    return [(d, core) for d in range(16)]


def every_device():
    return [(d, c) for d in range(16) for c in range(2)]


class Gather:
    def __init__(self, shard, whole, sems, rows, planes=()):
        self.shard, self.whole, self.rows, self.planes = shard, whole, rows, planes
        (self.local_s, self.up_s, self.down_s, self.plane_s, self.pair_s, self.line_r, self.turn_r, self.last_r, self.pair_r) = sems
        self.xn, self.yn, self.pair = neighbours()
        self.me, self.core, self.z, self.y, self.x = position()
        self.up = (jnp.minimum(self.me + 4, 15), self.core)
        self.down = (jnp.maximum(self.me - 4, 0), self.core)

    def piece(self, b, c, d):
        return self.whole.at[b, c, rows_at(d, self.rows), :]

    def send(self, b, d, own, device, sem, recv, condition=None):
        source = self.shard.at[b] if own else self.piece(b, self.core, d)
        guarded(condition, lambda: remote(source, self.piece(b, self.core, d), sem, recv, device).start())

    def pieces(self, b, count, sem, recv):
        some = self.whole.at[b, self.core, : count * self.rows, :]
        return remote(some, some, sem, recv, self.pair)

    def spread(self, b, d, zz, own=False, condition=None):
        odd = lax.rem(zz, 2)
        for step in range(2):
            along_y = odd if step == 0 else 1 - odd
            device = (index_of(self.z, jnp.where(along_y == 1, 1 - self.y, self.y), jnp.where(along_y == 1, self.x, 1 - self.x)), self.core)
            recv = self.turn_r.at[b, zz] if step == 0 else self.last_r.at[b]
            self.send(b, d, own, device, self.plane_s.at[b], recv, condition)
        self.send(b, d, own, self.pair, self.pair_s.at[b], self.pair_r.at[b], condition)

    def local(self, b):
        return pltpu.make_async_copy(self.shard.at[b], self.piece(b, self.core, self.me), self.local_s.at[b])

    def plane(self, b, zz):
        return self.whole.at[b, self.core, rows_at(zz, 4 * self.rows), :]

    def plane_send(self, b, zz, device, sem, recv, condition=None):
        guarded(condition, lambda: remote(self.plane(b, zz), self.plane(b, zz), sem, recv, device).start())

    def begin(self, b):
        self.local(b).start()
        if b in self.planes:
            for yy, xx in ((self.y, 1 - self.x), (1 - self.y, self.x), (1 - self.y, 1 - self.x)):
                device = (index_of(self.z, yy, xx), self.core)
                self.send(b, self.me, True, device, self.plane_s.at[b], self.turn_r.at[b, 0])
            return
        self.send(b, self.me, True, self.up, self.up_s.at[b], self.line_r.at[b, self.z], self.z < 3)
        self.send(b, self.me, True, self.down, self.down_s.at[b], self.line_r.at[b, self.z], self.z > 0)
        self.spread(b, self.me, self.z, True)

    def hop(self, b, distance):
        z = self.z
        if b in self.planes:
            for source, there, upward in (
                (jnp.maximum(z - distance, 0), z >= distance, True),
                (jnp.minimum(z + distance, 3), z + distance <= 3, False),
            ):
                onward = jnp.logical_and(there, z < 3 if upward else z > 0)
                guarded(there, lambda: self.pieces(b, 4, self.up_s.at[b], self.line_r.at[b, source]).wait_recv())
                if distance < 3:
                    device, sem = (self.up, self.up_s) if upward else (self.down, self.down_s)
                    self.plane_send(b, source, device, sem.at[b], self.line_r.at[b, source], onward)
                self.plane_send(b, source, self.pair, self.pair_s.at[b], self.pair_r.at[b], there)
            return
        for source, there, onward, device, sem in (
            (jnp.maximum(z - distance, 0), z >= distance, z < 3, self.up, self.up_s),
            (jnp.minimum(z + distance, 3), z + distance <= 3, z > 0, self.down, self.down_s),
        ):
            d = index_of(source, self.y, self.x)
            guarded(there, lambda: self.pieces(b, 1, self.up_s.at[b], self.line_r.at[b, source]).wait_recv())
            if distance < 3:
                self.send(b, d, False, device, sem.at[b], self.line_r.at[b, source], jnp.logical_and(there, onward))
            self.spread(b, d, source, False, there)

    def turn(self, b):
        if b in self.planes:
            self.local(b).wait()
            self.pieces(b, 3, self.up_s.at[b], self.turn_r.at[b, 0]).wait_recv()
            self.plane_send(b, self.z, self.up, self.up_s.at[b], self.line_r.at[b, self.z], self.z < 3)
            self.plane_send(b, self.z, self.down, self.down_s.at[b], self.line_r.at[b, self.z], self.z > 0)
            self.plane_send(b, self.z, self.pair, self.pair_s.at[b], self.pair_r.at[b])
            return
        for zz in range(4):
            yy, xx = (1 - self.y, self.x) if zz % 2 else (self.y, 1 - self.x)
            d = index_of(zz, yy, xx)
            self.pieces(b, 1, self.up_s.at[b], self.turn_r.at[b, zz]).wait_recv()
            self.send(b, d, False, self.xn if zz % 2 else self.yn, self.plane_s.at[b], self.last_r.at[b])
            self.send(b, d, False, self.pair, self.pair_s.at[b], self.pair_r.at[b])

    def last(self, b):
        self.pieces(b, 8, self.up_s.at[b], self.last_r.at[b]).wait_recv()
        for zz in range(4):
            yy, xx = (self.y, 1 - self.x) if zz % 2 else (1 - self.y, self.x)
            for d in (index_of(zz, yy, xx), index_of(zz, 1 - self.y, 1 - self.x)):
                self.send(b, d, False, self.pair, self.pair_s.at[b], self.pair_r.at[b])

    def ready(self, b):
        if b not in self.planes:
            self.local(b).wait()
        self.pieces(b, 16, self.up_s.at[b], self.pair_r.at[b]).wait_recv()

    def finish(self):
        for b in range(self.shard.shape[0]):
            whole_plane = b in self.planes
            per = 4 if whole_plane else 1
            self.pieces(b, 3 if whole_plane else 12, self.plane_s.at[b], self.pair_r.at[b]).wait_send()
            self.pieces(b, 16, self.pair_s.at[b], self.pair_r.at[b]).wait_send()
            for z in range(4):

                @pl.when(self.z == z)
                def line():
                    if z < 3:
                        self.pieces(b, per * (z + 1), self.up_s.at[b], self.pair_r.at[b]).wait_send()
                    if z > 0:
                        self.pieces(b, per * (4 - z), self.down_s.at[b], self.pair_r.at[b]).wait_send()


class QuickGather:
    def __init__(self, shard, whole, sems, rows):
        self.shard, self.whole, self.rows, self.sems = shard, whole, rows, sems
        self.me, self.core, self.z, self.y, self.x = position()

    def piece(self, c, d):
        return self.whole.at[rows_at(16 * c + d, self.rows), :]

    def send(self, d, own, device, recv, condition=None):
        source = self.shard if own else self.piece(self.core, d)
        guarded(condition, lambda: remote(source, self.piece(self.core, d), self.sems.at[1], self.sems.at[recv], device).start())

    def pieces(self, count, recv):
        some = self.whole.at[: count * self.rows, :]
        return remote(some, some, self.sems.at[1], self.sems.at[recv], (self.me, 1 - self.core))

    def local(self):
        return pltpu.make_async_copy(self.shard, self.piece(self.core, self.me), self.sems.at[0])

    def plane(self, zz, own, condition=None):
        d = index_of(zz, self.y, self.x)
        for k, (yy, xx) in enumerate(((self.y, 1 - self.x), (1 - self.y, self.x), (1 - self.y, 1 - self.x))):
            self.send(d, own, (index_of(self.z, yy, xx), self.core), 4 + k, condition)
        self.send(d, own, (self.me, 1 - self.core), 3, condition)

    def begin(self):
        self.local().start()
        for zz in range(4):
            self.send(self.me, True, (index_of(zz, self.y, self.x), self.core), 2, self.z != zz)
        self.plane(self.z, True)

    def spread(self):
        self.pieces(3, 2).wait_recv()
        for zz in range(4):
            self.plane(zz, False, self.z != zz)

    def share(self):
        for k, (yy, xx) in enumerate(((self.y, 1 - self.x), (1 - self.y, self.x), (1 - self.y, 1 - self.x))):
            self.pieces(4, 4 + k).wait_recv()
            for zz in range(4):
                self.send(index_of(zz, yy, xx), False, (self.me, 1 - self.core), 3)

    def ready(self):
        self.local().wait()
        self.pieces(16, 3).wait_recv()

    def finish(self):
        self.pieces(31, 2).wait_send()


GATHER_REFS = 9


def gather_sems(count):
    dma = pltpu.SemaphoreType.DMA
    one, four = dma((count,)), dma((count, 4))
    return [one, one, one, one, one, four, four, one, one]


class Scatter:
    def __init__(self, refs, landed, loaded, out, rows):
        (self.own, self.near, self.far, self.lined, self.pair_s, self.pair_r, self.load_s) = refs[:7]
        self.near_s, self.near_r, self.far_s, self.far_r, self.line_s, self.line_r = refs[7:]
        self.landed, self.loaded, self.out, self.rows = landed, loaded, out, rows
        self.xn, self.yn, self.pair = neighbours()
        self.me, self.core, self.z, self.y, self.x = position()

    def piece(self, b, zz, yy, xx):
        return self.own.at[b, rows_at(index_of(zz, yy, xx), self.rows), :]

    def pair_copy(self, b, source):
        return remote(source, self.landed.at[b], self.pair_s.at[b], self.pair_r.at[b], self.pair)

    def load(self, b):
        return pltpu.make_async_copy(self.landed.at[b], self.loaded[b], self.load_s.at[b])

    def near_copy(self, b, zz, i):
        place, device = ((zz, i, 1 - self.x), self.xn) if zz % 2 else ((zz, 1 - self.y, i), self.yn)
        group = jnp.where(i == self.onward(zz), 0, 1)
        return remote(
            self.piece(b, *place), self.near.at[b, zz, i], self.near_s.at[b], self.near_r.at[b, group], device
        )

    def onward(self, zz):
        return 1 - self.y if zz % 2 else 1 - self.x

    def far_place(self, zz):
        return (zz, 1 - self.y, self.x) if zz % 2 else (zz, self.y, 1 - self.x)

    def far_copy(self, b, zz):
        return remote(
            self.piece(b, *self.far_place(zz)), self.far.at[b, zz], self.far_s.at[b], self.far_r.at[b],
            self.yn if zz % 2 else self.xn,
        )

    def line_copy(self, b, zz):
        there = (index_of(zz, self.y, self.x), self.core)
        return remote(
            self.near.at[b, zz, 1 - self.onward(zz)], self.lined.at[b, self.z], self.line_s.at[b], self.line_r.at[b], there
        )

    def pieces(self, b, count, send_sem, recv_sem):
        some = self.own.at[b, : count * self.rows, :]
        return remote(some, some, send_sem.at[b], recv_sem, self.pair)

    def take(self, b):
        self.pair_copy(b, self.own.at[b]).wait_recv()
        self.load(b).start()

    def first(self, b):
        self.load(b).wait()
        loaded = self.loaded[b]

        def add(d, carry):
            at = rows_at(d, self.rows)
            self.own[b, at, :] = (self.own[b, at, :].astype(F32) + loaded[at, :].astype(F32)).astype(self.own.dtype)
            return carry

        lax.fori_loop(0, 16, add, 0)
        for zz in range(4):
            self.near_copy(b, zz, self.onward(zz)).start()
        for zz in range(4):
            self.near_copy(b, zz, 1 - self.onward(zz)).start()

    def second(self, b):
        self.pieces(b, 4, self.near_s, self.near_r.at[b, 0]).wait_recv()
        for zz in range(4):
            i = self.onward(zz)
            place = self.far_place(zz)
            value = self.piece(b, *place)[...].astype(F32) + self.near[b, zz, i].astype(F32)
            self.piece(b, *place)[...] = value.astype(self.own.dtype)
            self.far_copy(b, zz).start()

    def third(self, b):
        self.pieces(b, 4, self.near_s, self.near_r.at[b, 1]).wait_recv()
        self.pieces(b, 4, self.near_s, self.far_r.at[b]).wait_recv()
        for zz in range(4):
            i = 1 - self.onward(zz)
            value = self.piece(b, zz, self.y, self.x)[...].astype(F32) + self.near[b, zz, i].astype(F32) + self.far[b, zz].astype(F32)

            @pl.when(self.z == zz)
            def keep():
                self.out[b] = value

            @pl.when(self.z != zz)
            def give():
                self.near[b, zz, i] = value.astype(self.near.dtype)
                self.line_copy(b, zz).start()

    def result(self, b):
        self.pieces(b, 3, self.near_s, self.line_r.at[b]).wait_recv()
        for zz in range(4):

            @pl.when(self.z != zz)
            def add():
                self.out[b] += self.lined[b, zz].astype(F32)

        value = self.out[b]
        return jnp.sum(value * value, keepdims=True)

    def finish(self, b):
        self.pieces(b, 8, self.near_s, self.line_r.at[b]).wait_send()
        self.pieces(b, 4, self.far_s, self.line_r.at[b]).wait_send()
        self.pieces(b, 3, self.line_s, self.line_r.at[b]).wait_send()


SCATTER_REFS = 13


def scatter_scratch(count, rows, columns):
    dma, vmem = pltpu.SemaphoreType.DMA, pltpu.VMEM
    return [
        vmem((count, 16 * rows, columns), BF16),
        vmem((count, 4, 2, rows, columns), BF16),
        vmem((count, 4, rows, columns), BF16),
        vmem((count, 4, rows, columns), BF16),
        dma((count,)), dma((count,)), dma((count,)),
        dma((count,)), dma((count, 2)), dma((count,)), dma((count,)), dma((count,)), dma((count,)),
    ]


def gelu_parts(values):
    root = 0.7978845608028654
    square = values * values
    half = 0.5 + 0.5 * jnp.tanh(values * (root + (root * 0.044715) * square))
    active = values * half
    return active, half + active * (1.0 - half) * (2.0 * root + (6.0 * root * 0.044715) * square)


def halves_of(shape, axis, scale):
    low = lax.broadcasted_iota(jnp.int32, shape, axis) < HEAD_DIM
    return jnp.where(low, scale, 0.0).astype(BF16), jnp.where(low, 0.0, scale).astype(BF16)


def pick_halves(wide):
    low = lax.broadcasted_iota(jnp.int32, (2 * HEAD_DIM, SPAN), 0) < HEAD_DIM
    return jnp.where(low, wide[:, :SPAN], wide[:, SPAN:])


def window_start(block, blocks):
    return min(max(block - 1, 0), blocks - WINDOW // SPAN) * SPAN


def column_table(rows, length):
    rows = rows + [jnp.zeros((1, length), F32)] * (8 - len(rows))
    return jnp.concatenate(rows, axis=0).T


def one_hot(ids, vocab):
    lanes = lax.broadcasted_iota(jnp.int32, (ids.shape[0], vocab), 1).astype(F32)
    return ids == lanes


def forward_kernel(fused, shapes, *refs):
    length, width, pairs = shapes
    blocks = length // SPAN
    tiles = length // TILE
    half = width // 2
    sources = 4 if fused else 2
    (
        tokens, segments, steps, noise_in, buckets, counted, embed_in, up_in, norms, places_in,
        wide_whole, thin_whole, count_out, start, noisy, table_low, zero_out, one_out, two_out, qkv_out, keyt_out, att_out, probs_out, act_out, slope_out, first_t_out, second_t_out,
        h_zero, h_one, h_two, normed, normed_t, qkv, key_t, value_t, att, probs, act, slope, weights, bias, places, table, table3, columns, count_own, noise, embed, up_weight,
        out_sems, probs_sems, weight_sems, in_sems,
    ) = refs[sources : sources + 53]
    rest = refs[sources + 53 :]
    core = lax.axis_index("mp")
    saves = []

    def save(source, target):
        copy = pltpu.make_async_copy(source, target, out_sems.at[len(saves)])
        copy.start()
        saves.append(copy)

    if fused:
        everyone = same_core() + [neighbours()[2]]
        greet(everyone)
        qkv_weight, out_weight, fc_weight, proj_weight = rest[:4]
        wide_shard, thin_shard, counts, count_sems = rest[4:8]
        rows = wide_shard.shape[1]
        wide = Gather(wide_shard, wide_whole, rest[8 : 8 + GATHER_REFS], rows, planes=(3,))
        thin = Gather(thin_shard, thin_whole, rest[8 + GATHER_REFS :], rows)
        gathers = {"wide": wide, "thin": thin}
        moves = list(zip(refs[:4], rest[:4]))
    else:
        moves = []
    moves += [(noise_in.at[core], noise), (embed_in, embed), (up_in, up_weight), (places_in, places)]
    fetches = [pltpu.make_async_copy(source, target, in_sems.at[k]) for k, (source, target) in enumerate(moves)]
    for copy in fetches:
        copy.start()
    if fused:
        wide_from, thin_from = wide_whole, thin_whole
        for copy in fetches[:4]:
            copy.wait()
        for j in range(3):
            thin_shard[j] = qkv_weight[j].astype(BF16)
        thin_shard[3] = out_weight[...].astype(BF16)
        for h in range(2):
            cols = slice(h * width, (h + 1) * width)
            wide_shard[h] = fc_weight[:, cols].astype(BF16)
            wide_shard[2 + h] = proj_weight[:, cols].astype(BF16)
    else:
        wide_from, thin_from = refs[:2]

    def pump(*items):
        if fused:
            for which, name, b, *more in items:
                getattr(gathers[which], name)(b, *more)

    live = counted[...].astype(F32)
    lane = lax.broadcasted_iota(jnp.int32, count_own.shape, 1)
    own_counts = jnp.zeros(count_own.shape, F32)
    for bucket in range(NB):
        found = jnp.sum(jnp.where(buckets[...] == bucket, live, 0.0), keepdims=True)
        own_counts = jnp.where(lane == bucket, found, own_counts)
    count_own[...] = own_counts
    token_row = tokens[pl.ds(core, 1), :].astype(F32)
    segment_row = segments[pl.ds(core, 1), :].astype(F32)
    columns[...] = column_table([token_row, segment_row], length)
    emb = embed.shape[1]
    for copy in fetches[-4:]:
        copy.wait()
    table[...] = jnp.zeros(table.shape, F32)
    table[: embed.shape[0], :] = embed[...]
    left = table[...]
    for third in range(3):
        part = left.astype(BF16)
        table3[:, third * emb : (third + 1) * emb] = part
        if third == 0:
            table_low[...] = part
        left = left - part.astype(F32)
    step = jnp.full((1, 1), steps[core], jnp.int32).astype(F32)
    keep = 1.0 - jnp.sqrt(step * (1.0 / T_STEPS) + 0.0001)
    keep_root, noise_root = jnp.sqrt(keep), jnp.sqrt(1.0 - keep)
    time_row = sine_row(step, width)
    up_low = up_weight[...].astype(BF16)

    def embed_tile(r):
        at = rows_at(r, TILE)
        hot = one_hot(columns[at, 0:1], table.shape[0]).astype(F32).astype(BF16)
        thirds = nn(hot, table3[...])
        first = thirds[:, :emb] + thirds[:, emb : 2 * emb] + thirds[:, 2 * emb :]
        start[at, :] = first
        low = (keep_root * first + noise_root * noise[at, :]).astype(BF16)
        noisy[at, :] = low
        hidden = nn(low, up_low) + places[at, :] + time_row
        h_zero[at, :] = hidden
        unit = norm_stats(hidden)[0]
        scaled = unit * norms[0:1, :] + norms[1:2, :]
        normed[at, :] = scaled.astype(BF16)
        normed_t[0, :, at] = scaled.T.astype(BF16)

    if fused:
        assemble(everyone)
        exchange = Exchange(count_own, counts, count_sems, same_core())
        exchange.start()
    early = range(3)
    pump(*[("thin", "begin", b) for b in early])
    for r in range(tiles):
        embed_tile(r)
        if r < 3:
            pump(*[("thin", "hop", b, r + 1) for b in early])
    pump(*[("thin", "turn", b) for b in early])
    second_group = [("thin", 3), ("wide", 0), ("wide", 1)]
    third_group = [("wide", 2)]

    def steps(group, name, *more):
        return [(which, name, b, *more) for which, b in group]

    pump(*steps(second_group, "begin"), ("wide", "begin", 3))
    save(h_zero, zero_out)
    save(normed_t.at[0], first_t_out)
    for i in range(blocks):
        w0 = window_start(i, blocks)
        same = columns[w0 : w0 + WINDOW, 1:2] == segment_row[:, i * SPAN : (i + 1) * SPAN]
        bias[i] = jnp.where(same, 0.0, MASKED)
    pump(*[("thin", "last", b) for b in early])

    def load_wide(b, c, slot):
        return pltpu.make_async_copy(wide_from.at[b, c], weights.at[slot], weight_sems.at[slot])

    def load_thin(b, c):
        return pltpu.make_async_copy(
            thin_from.at[b, c], weights.at[b, :, c * half : (c + 1) * half], weight_sems.at[b + 8 * c]
        )

    pump(*[("thin", "ready", b) for b in early])
    for c in range(2):
        for b in early:
            load_thin(b, c).start()
    pump(*steps(second_group, "hop", 1))
    for c in range(2):
        for b in early:
            load_thin(b, c).wait()
    for j in early:

        def project(r, carry):
            at = rows_at(r, TILE)
            value = nn(normed[at, :], weights[j])
            qkv[j, at, :] = value.astype(BF16)
            if j > 0:
                (key_t if j == 1 else value_t)[:, at] = value.T.astype(BF16)
            return carry

        lax.fori_loop(0, tiles, project, 0, unroll=True)
        if j > 0:
            pump(*(steps(second_group, "hop", 2) if j == 1 else steps(third_group, "begin")))
    for j in range(3):
        save(qkv.at[j], qkv_out.at[j])
    save(key_t, keyt_out)

    def probs_copy(pair, slot):
        return pltpu.make_async_copy(probs.at[slot], probs_out.at[pl.ds(pair * blocks, blocks)], probs_sems.at[slot])

    low, high = halves_of((1, SPAN), 1, 0.125)

    def attend(pair, carry):
        slot = lax.rem(pair, 2)
        cols = pl.ds(pl.multiple_of(pair * SPAN, SPAN), SPAN)

        @pl.when(pair >= 2)
        def free():
            probs_copy(pair - 2, slot).wait()

        def ask(i):
            w0 = window_start(i, blocks)
            queries = qkv[0, i * SPAN : (i + 1) * SPAN, cols]
            both = jnp.concatenate([queries * low, queries * high], axis=0)
            return nt(qkv[1, w0 : w0 + WINDOW, cols], both)

        def answer(i, prob):
            w0 = window_start(i, blocks)
            mixed = nn(value_t[cols, w0 : w0 + WINDOW], prob)
            att[i * SPAN : (i + 1) * SPAN, cols] = pick_halves(mixed).T.astype(BF16)

        ahead, behind = ask(0), None
        for i in range(blocks):
            mask = bias[i]
            scores = ahead + jnp.concatenate([mask, mask], axis=1)
            if i + 1 < blocks:
                ahead = ask(i + 1)
            if i > 0:
                answer(i - 1, behind)
            most = jnp.max(scores, axis=0, keepdims=True)
            raised = jnp.exp(scores - most)
            share = 1.0 / jnp.sum(raised, axis=0, keepdims=True)
            behind = (raised * share).astype(BF16)
            probs[slot, i] = behind
        answer(blocks - 1, behind)
        probs_copy(pair, slot).start()
        return carry

    middle = [
        steps(second_group, "hop", 3) + [("wide", "turn", 3)],
        steps(third_group, "hop", 1),
        steps(second_group, "turn"),
        steps(third_group, "hop", 2) + [("wide", "hop", 3, 1)],
        steps(second_group[:2], "last") + steps(second_group[:1], "ready"),
        steps(third_group, "hop", 3) + [("wide", "hop", 3, 2)],
    ]
    for part in range(6):
        lax.fori_loop(part * pairs // 6, (part + 1) * pairs // 6, attend, 0)
        pump(*middle[part])
        if part == 4:
            for c in range(2):
                load_thin(3, c).start()
    for pair in (pairs - 2, pairs - 1):
        probs_copy(pair, pair % 2).wait()
    save(att, att_out)
    for c in range(2):
        load_thin(3, c).wait()
    pump(("wide", "ready", 0))
    for c in range(2):
        load_wide(0, c, 4 + c).start()

    def after_attention(r, carry):
        at = rows_at(r, TILE)
        mixed = att[at, :]
        hidden = h_zero[at, :] + nt(mixed, weights[3])
        h_one[at, :] = hidden
        unit = norm_stats(hidden)[0]
        scaled = unit * norms[2:3, :] + norms[3:4, :]
        normed[at, :] = scaled.astype(BF16)
        normed_t[1, :, at] = scaled.T.astype(BF16)
        return carry

    lax.fori_loop(0, tiles, after_attention, 0, unroll=True)
    save(h_one, one_out)
    save(normed_t.at[1], second_t_out)
    pump(*steps(third_group, "turn"), ("wide", "last", 1))
    for j in range(4):
        load_wide(j // 2, j % 2, 4 + j).wait()
        stages = [(slice(k, k + TILE), slice(r, r + 2 * TILE)) for k in range(0, width, TILE) for r in range(0, length, 2 * TILE)]

        def before_gelu(stage):
            chunk, at = stage
            return nn(normed[at, :], weights[4 + j, :, chunk])

        ahead = before_gelu(stages[0])
        for k, (chunk, at) in enumerate(stages):
            before = ahead
            if k + 1 < len(stages):
                ahead = before_gelu(stages[k + 1])
            active, bend = gelu_parts(before)
            act[j, at, chunk] = active.astype(BF16)
            slope[j, at, chunk] = bend.astype(BF16)
        save(act.at[j], act_out.at[j])
        save(slope.at[j], slope_out.at[j])
        if j == 0:
            pump(("wide", "ready", 1))
            for c in range(2):
                load_wide(1, c, 6 + c).start()
            pump(("wide", "hop", 3, 3), ("wide", "last", 2))
        elif j > 1:
            pump(("wide", "ready", j))
            for c in range(2):
                load_wide(j, c, 2 * (j - 2) + c).start()

    for h in range(2):
        for c in range(2):
            load_wide(2 + h, c, 2 * h + c).wait()

        for r in range(tiles):
            at = slice(r * TILE, (r + 1) * TILE)
            total = (h_two if h else h_one)[at, :]
            for j in (2 * h, 2 * h + 1):
                total = total + nt(act[j, at, :], weights[j])
            h_two[at, :] = total
            if h:
                save(h_two.at[at, :], two_out.at[at, :])

    if fused:
        exchange.arrive()
        count_out[...] = exchange.total()
        wide.finish()
        thin.finish()
        exchange.finish()
    else:
        count_out[...] = count_own[...]
    for copy in saves:
        copy.wait()


def run_forward(fused, sources, tokens, segments, steps, noise, buckets, counted, embed, up_weight, norms, places):
    length, width = places.shape
    pairs = width // SPAN
    blocks = length // SPAN
    dma, vmem = pltpu.SemaphoreType.DMA, pltpu.VMEM
    anywhere, inside = pl.BlockSpec(memory_space=pl.ANY), pl.BlockSpec(memory_space=pltpu.VMEM)
    vocab, emb = embed.shape
    padded = -(-vocab // 128) * 128

    def made(shape, dtype=BF16):
        return jax.ShapeDtypeStruct(shape, dtype)

    out_shape = [
        made((4, 2, width, width)),
        made((4, 2, width, width // 2)),
        made((8, 128), F32),
        made((length, emb), F32),
        made((length, emb)),
        made((padded, emb)),
        made((length, width), F32),
        made((length, width), F32),
        made((length, width), F32),
        made((3, length, width)),
        made((width, length)),
        made((length, width)),
        made((pairs * blocks, WINDOW, 2 * SPAN)),
        made((4, length, width)),
        made((4, length, width)),
        made((width, length)),
        made((width, length)),
    ]
    scratch = [
        vmem((length, width), F32),
        vmem((length, width), F32),
        vmem((length, width), F32),
        vmem((length, width), BF16),
        vmem((2, width, length), BF16),
        vmem((3, length, width), BF16),
        vmem((width, length), BF16),
        vmem((width, length), BF16),
        vmem((length, width), BF16),
        vmem((2, blocks, WINDOW, 2 * SPAN), BF16),
        vmem((4, length, width), BF16),
        vmem((4, length, width), BF16),
        vmem((8, width, width), BF16),
        vmem((blocks, WINDOW, SPAN), F32),
        vmem((length, width), F32),
        vmem((padded, emb), F32),
        vmem((padded, 3 * emb), BF16),
        vmem((length, 8), F32),
        vmem((8, 128), F32),
        vmem((length, emb), F32),
        vmem((vocab, emb), F32),
        vmem((emb, width), F32),
        dma((24,)),
        dma((2,)),
        dma((12,)),
        dma((8,)),
    ]
    params = dict(vmem_limit_bytes=VMEM_LIMIT)
    if fused:
        rows = width // 16
        scratch += [vmem(source.shape, F32) for source in sources]
        scratch += [vmem((4, rows, width), BF16), vmem((4, rows, width // 2), BF16)]
        scratch += [vmem((16, 8, 128), F32), dma((2,))] + gather_sems(4) + gather_sems(4)
        params.update(collective_id=0, has_side_effects=True)
    return pl.pallas_call(
        functools.partial(forward_kernel, fused, (length, width, pairs)),
        out_shape=out_shape,
        in_specs=[anywhere] * len(sources)
        + [inside, inside, pl.BlockSpec(memory_space=pltpu.SMEM), anywhere]
        + [inside] * 2
        + [anywhere] * 2
        + [inside, anywhere],
        out_specs=[anywhere] * 2 + [inside] * 4 + [anywhere] * 11,
        scratch_shapes=scratch,
        compiler_params=pltpu.CompilerParams(**params),
        name="forward",
    )(*sources, tokens, segments, steps, noise, buckets, counted, embed, up_weight, norms, places)


def backward_kernel(fused, shapes, *refs):
    length, width, pairs, vocab_used = shapes
    blocks = length // SPAN
    tiles = length // TILE
    half = width // 2
    (
        wide_whole, thin_whole, tokens, buckets, counted, counts, start, noisy, zero_in, one_in, two_in, qkv_in, keyt_in, att_in, probs_in, act_in, slope_in, first_t_in, second_t_in,
        embed_low, up_weight, down_weight, norms, steps,
        out_wide, out_thin, out_small, out_scalars, wide_landed, thin_landed, small_landed,
        hidden, grad, back, branch, branch_t, normed_t, pre, slots, weights, acc, probs, error, norm_grads, posted, thin_posted, scalars, columns, up_low, down_low,
        load_sems, slot_sems, weight_sems, probs_sems, post_sems,
    ) = refs[:55]
    core = lax.axis_index("mp")
    small = out_small
    emb = start.shape[1]
    vocab = embed_low.shape[0]
    side = width // TILE

    if fused:
        rest = refs[55:]
        n = SCATTER_REFS
        loaded, tiny_shard, tiny_out, slots_all, all_sems, quick_sems = rest[3 * n :]
        group = out_small.shape[1] // 4
        tiny_loaded = branch.at[: 2 * emb, :group]
        small_own = branch.at[2 * emb : 4 * emb, :group]
        tiny_whole = pre.at[: 4 * emb, :group]
        wide_loaded = [loaded.at[b % 2] for b in range(4)]
        thin_loaded = [loaded.at[b // 2, :, (b % 2) * half : (b % 2 + 1) * half] for b in range(4)]
        wide = Scatter(rest[:n], wide_landed, wide_loaded, out_wide, width // 16)
        thin = Scatter(rest[n : 2 * n], thin_landed, thin_loaded, out_thin, width // 16)
        tiny = Scatter(rest[2 * n : 3 * n], small_landed, [tiny_loaded], tiny_out, 16)
        devices = every_device()
        greet(devices)

    def pump(scatter_name, *steps):
        if fused:
            scatter = wide if scatter_name == "wide" else thin
            for name, *members in steps:
                for b in members:
                    getattr(scatter, name)(b)

    def posted_half(b):
        return posted.at[b // 2, :, (b % 2) * half : (b % 2 + 1) * half]

    def post_copy(b, slot):
        if fused:
            return wide.pair_copy(b, posted.at[slot])
        return pltpu.make_async_copy(posted.at[slot], out_wide.at[b, 1 - core], post_sems.at[slot])

    def thin_copy(b):
        if fused:
            return thin.pair_copy(b, posted_half(b))
        return pltpu.make_async_copy(thin_posted.at[b], out_thin.at[b, 1 - core], post_sems.at[4 + b])

    def kept_copy(b, slot):
        return pltpu.make_async_copy(posted.at[slot], out_wide.at[b, core], post_sems.at[slot])

    def thin_kept(b):
        return pltpu.make_async_copy(thin_posted.at[4 + b], out_thin.at[b, core], post_sems.at[8 + b])

    def sent(copy):
        (copy.wait_send if fused else copy.wait)()

    def fetch(source, target, k):
        copy = pltpu.make_async_copy(source, target, load_sems.at[k])
        copy.start()
        return copy

    def load_weights(b, c, slot):
        return pltpu.make_async_copy(wide_whole.at[b, c], weights.at[slot], weight_sems.at[slot])

    def load_thin(b, c):
        return pltpu.make_async_copy(
            thin_whole.at[b, c], weights.at[b, :, c * half : (c + 1) * half], weight_sems.at[4 + 2 * b + c]
        )

    def load_slot(source, slot):
        return pltpu.make_async_copy(source, slots.at[slot], slot_sems.at[slot])

    def other_first(k):
        return 1 - core if k == 0 else core

    def act_load(k):
        return load_slot(act_in.at[2 * (k % 2) + other_first(k // 2)], k)

    def slope_load(s):
        return load_slot(slope_in.at[2 * (s // 2) + other_first(s % 2)], s)

    def feed(s):
        c = other_first(s % 2)
        return [load_weights(s // 2, c, 2 * (s % 2)), load_weights(2 + s // 2, c, 2 * (s % 2) + 1)]

    start_copy = fetch(start, error, 3)
    two_copies = [
        fetch(two_in.at[r * TILE : (r + 1) * TILE, :], hidden.at[r * TILE : (r + 1) * TILE, :], 4 + r) for r in range(tiles)
    ]
    normed_copy = fetch(second_t_in, normed_t, 1)
    for k in range(4):
        act_load(k).start()
    for copy in feed(0) + feed(1):
        copy.start()
    norm_grads[...] = jnp.zeros(norm_grads.shape, F32)
    columns[...] = jnp.zeros(columns.shape, F32)
    small[...] = jnp.zeros(small.shape, F32)
    count_row = counts[0:1, :]
    live_total = jnp.sum(count_row, keepdims=True)
    bucket_weight = live_total / (NB * jnp.maximum(count_row, 1.0))
    weight_total = jnp.sum(count_row * bucket_weight, keepdims=True)
    bucket_row = buckets[pl.ds(core, 1), :]
    scale = jnp.zeros((1, length), F32)
    for bucket in range(NB):
        scale = jnp.where(bucket_row == bucket, bucket_weight[:, bucket : bucket + 1], scale)
    scale = scale * counted[pl.ds(core, 1), :].astype(F32)
    columns[0:1, :] = tokens[pl.ds(core, 1), :].astype(F32)
    columns[1:2, :] = scale
    columns[2:3, :] = scale / weight_total
    step = jnp.full((1, 1), steps[core], jnp.int32).astype(F32)
    keep_root = jnp.sqrt(1.0 - jnp.sqrt(step * (1.0 / T_STEPS) + 0.0001))
    up_low[...] = up_weight[...].astype(BF16)
    down_low[...] = down_weight[...].astype(BF16)
    ids = lax.broadcasted_iota(jnp.int32, (TILE, vocab), 1).astype(F32)
    pad_row = jnp.where(lax.broadcasted_iota(jnp.int32, (1, vocab), 1) < vocab_used, 0.0, MASKED)
    start_copy.wait()
    d0, u0, e0 = 0, width, 2 * width

    def add_norm(row, upstream, unit):
        norm_grads[row : row + 1, :] += column_sum(upstream * unit)
        norm_grads[row + 1 : row + 2, :] += column_sum(upstream)

    def head(r, loss):
        at = rows_at(r, TILE)
        unit, rate = norm_stats(hidden[at, :])
        ended = (unit * norms[4:5, :] + norms[5:6, :]).astype(BF16)
        predicted = nn(ended, down_low[...])
        pred_low = predicted.astype(BF16)
        logits = nt(pred_low, embed_low[...]) + pad_row
        most = jnp.max(logits, axis=-1, keepdims=True)
        raised = jnp.exp(logits - most)
        total = jnp.sum(raised, axis=-1, keepdims=True)
        table = columns[:, at].T
        hit = table[:, 0:1] == ids
        picked = jnp.sum(jnp.where(hit, logits, 0.0), axis=-1, keepdims=True)
        miss = predicted - error[at, :]
        per_token = jnp.sum(miss * miss, axis=-1, keepdims=True) * (1.0 / emb) + (jnp.log(total) + most) - picked
        loss = loss + jnp.sum(table[:, 1:2] * per_token, keepdims=True)
        coef = table[:, 2:3]
        grad_logits = (coef * (raised * (1.0 / total) - jnp.where(hit, 1.0, 0.0))).astype(BF16)
        grad_error = coef * 2.0 * miss * (1.0 / emb)
        error[at, :] = grad_error
        grad_pred = nn(grad_logits, embed_low[...]) + grad_error
        grad_pred_low = grad_pred.astype(BF16)
        small[:, d0 : d0 + width] += nn(grad_pred.T.astype(BF16), ended)
        small[:, e0 : e0 + vocab] += nn(predicted.T.astype(BF16), grad_logits)
        upstream = nt(grad_pred_low, down_low[...])
        add_norm(4, upstream, unit)
        result = norm_back(unit, rate, norms[4:5, :], upstream)
        grad[at, :] = result
        branch[at, :] = result.astype(BF16)
        branch_t[:, at] = result.T.astype(BF16)
        return loss

    loss = jnp.zeros((1, 1), F32)
    for r in range(tiles):
        two_copies[r].wait()
        loss = head(r, loss)
    one_copy = fetch(one_in, hidden, 0)
    normed_copy.wait()

    def weigh(left, right, h, kind, mine):
        slot = (2 if mine else 0) + kind if not fused else kind

        def body(m, carry):
            at = rows_at(m, TILE)
            value = nn(left[at, :], right[...]).astype(BF16)
            if mine and fused:
                wide.own[2 * kind + h, at, :] = value
            else:
                posted[slot, at, :] = value
            return carry

        b = 2 * kind + h
        if h == 1 and not mine:
            sent(post_copy(b - 1, slot))
        if h == 1 and mine and not fused:
            kept_copy(b - 1, slot).wait()
        lax.fori_loop(0, side, body, 0, unroll=True)
        if not mine:
            post_copy(b, slot).start()
        elif fused:
            wide.take(b)
        else:
            kept_copy(b, slot).start()

    if fused:
        assemble(devices)
    for k in range(4):
        act_load(k).wait()
        weigh(branch_t, slots.at[k], k % 2, 1, k >= 2)
        slope_load(k).start()
    pump("wide", ("first", 2, 3))

    for s in range(4):
        h = s // 2
        for copy in feed(s):
            copy.wait()
        slope_load(s).wait()
        first = 2 * (s % 2)
        fc, proj, bend = weights.at[first], weights.at[first + 1], slots.at[s]

        def through(r):
            at = slice(r * TILE, (r + 1) * TILE)
            pushed = (nn(branch[at, :], proj[...]) * bend[at, :].astype(F32)).astype(BF16)
            pre[at, :] = pushed
            return pushed

        ahead = through(0)
        for r in range(tiles):
            at = slice(r * TILE, (r + 1) * TILE)
            pushed = ahead
            if r + 1 < tiles:
                ahead = through(r + 1)
            value = nt(pushed, fc[...])
            if s == 0:
                back[at, :] = value
            else:
                back[at, :] += value
        if s < 2:
            for copy in feed(s + 2):
                copy.start()
        if s == 2:
            pump("wide", ("first", 0))
        weigh(normed_t, pre, h, 0, s % 2 == 1)
        if s == 3:
            pump("wide", ("second", 2, 3))

    for c in range(2):
        for b in range(4):
            load_thin(b, c).start()
    att_copy = fetch(att_in, pre, 2)
    first_t_copy = fetch(first_t_in, normed_t, 1)
    load_slot(qkv_in.at[0], 0).start()
    load_slot(qkv_in.at[2], 2).start()
    one_copy.wait()

    def through_two(r, carry):
        at = rows_at(r, TILE)
        unit, rate = norm_stats(hidden[at, :])
        upstream = back[at, :]
        add_norm(2, upstream, unit)
        result = grad[at, :] + norm_back(unit, rate, norms[2:3, :], upstream)
        grad[at, :] = result
        branch[at, :] = result.astype(BF16)
        branch_t[:, at] = result.T.astype(BF16)
        return carry

    lax.fori_loop(0, tiles, through_two, 0)
    zero_copy = fetch(zero_in, hidden, 0)
    pump("wide", ("first", 1))
    att_copy.wait()

    def other_half(c):
        return pl.ds(pl.multiple_of(c * half, SPAN), half)

    def store(which, b, at, value):
        if fused and which == 1:
            thin.own[b, at, :] = value
        elif fused:
            posted_half(b)[at, :] = value
        else:
            thin_posted[4 * which + b, at, :] = value

    def out_weigh(m, carry):
        at = rows_at(m, TILE)
        for which in range(2):
            c = core if which else 1 - core
            store(which, 3, at, nn(branch_t[at, :], pre[:, other_half(c)]).astype(BF16))
        return carry

    if fused:
        sent(post_copy(1, 0))
        sent(post_copy(3, 1))
    lax.fori_loop(0, side, out_weigh, 0, unroll=True)
    thin_copy(3).start()
    if not fused:
        thin_kept(3).start()
    for c in range(2):
        for b in range(4):
            load_thin(b, c).wait()
    keyt_copy = fetch(keyt_in, branch_t, 3)

    def spread_att(r, carry):
        at = rows_at(r, TILE)
        slots[3, at, :] = nn(branch[at, :], weights[3]).astype(BF16)
        return carry

    lax.fori_loop(0, tiles, spread_att, 0, unroll=True)
    pump("wide", ("second", 0))
    pump("thin", ("take", 3), ("first", 3))
    count = blocks // 2

    def probs_copy(unit):
        slot = lax.rem(unit, 2)
        return pltpu.make_async_copy(probs_in.at[pl.ds(unit * count, count)], probs.at[slot], probs_sems.at[slot])

    probs_copy((1 - core) * pairs).start()
    load_slot(qkv_in.at[0], 0).wait()
    load_slot(qkv_in.at[2], 2).wait()
    keyt_copy.wait()
    low, high = halves_of((1, SPAN), 1, 0.125)
    low_one, high_one = halves_of((1, SPAN), 1, 1.0)

    def attend(pair, carry):
        cols = pl.ds(pl.multiple_of(pair * SPAN, SPAN), SPAN)
        acc[...] = jnp.zeros(acc.shape, F32)
        for part in range(2):
            unit = 2 * pair + part

            @pl.when(lax.rem(unit + 1, pairs) != 0)
            def ahead():
                probs_copy(unit + 1).start()

            probs_copy(unit).wait()

            def ask(k):
                i = part * count + k
                w0 = window_start(i, blocks)
                up_rows = slots[3, i * SPAN : (i + 1) * SPAN, cols]
                ups = jnp.concatenate([up_rows * low_one, up_rows * high_one], axis=0)
                return ups, nt(slots[2, w0 : w0 + WINDOW, cols], ups)

            ahead = ask(0)
            for k in range(count):
                i = part * count + k
                w0 = window_start(i, blocks)
                here = slice(i * SPAN, (i + 1) * SPAN)
                there = slice(w0, w0 + WINDOW)
                ups, grad_probs = ahead
                if k + 1 < count:
                    ahead = ask(k + 1)
                queries = slots[0, here, cols]
                asks = jnp.concatenate([queries * low, queries * high], axis=0)
                prob = probs[part, k]
                wide_probs = prob.astype(F32)
                inner = jnp.sum(grad_probs * wide_probs, axis=0, keepdims=True)
                grad_scores = (wide_probs * (grad_probs - inner)).astype(BF16)
                acc[1, there, :] += nn(prob, ups)
                acc[0, there, :] += nn(grad_scores, asks)
                asked = nn(branch_t[cols, there], grad_scores)
                slots[0, here, cols] = (pick_halves(asked).T * 0.125).astype(BF16)
        slots[1, :, cols] = acc[0].astype(BF16)
        slots[2, :, cols] = acc[1].astype(BF16)
        return carry

    def qkv_weigh(which):
        cols = other_half(core if which else 1 - core)

        def body(m, carry):
            at = rows_at(m, TILE)
            rows = normed_t[at, :]
            for j in range(3):
                store(which, j, at, nn(rows, slots[j, :, cols]).astype(BF16))
            return carry

        lax.fori_loop(0, side, body, 0, unroll=True)

    few = pairs // 2
    for which in range(2):
        base = (core if which else 1 - core) * few
        lax.fori_loop(base, base + few - 1, attend, 0)
        if which == 1:
            pump("wide", ("third", 0))
        lax.fori_loop(base + few - 1, base + few, attend, 0)
        if which == 0:
            probs_copy(core * pairs).start()
            first_t_copy.wait()
            pump("wide", ("second", 1), ("third", 2, 3))
        else:
            pump("thin", ("second", 3), ("take", 0, 1))
            pump("wide", ("third", 1))
        qkv_weigh(which)
        for j in range(3):
            if which == 0:
                thin_copy(j).start()
            elif not fused:
                thin_kept(j).start()
    zero_copy.wait()
    pump("thin", ("take", 2), ("first", 0, 1, 2))

    def towards_one(r):
        at = slice(r * TILE, (r + 1) * TILE)
        return nt(slots[0, at, :], weights[0]) + nt(slots[1, at, :], weights[1]) + nt(slots[2, at, :], weights[2])

    def through_one(r, upstream):
        at = slice(r * TILE, (r + 1) * TILE)
        unit, rate = norm_stats(hidden[at, :])
        add_norm(0, upstream, unit)
        grad_zero = (grad[at, :] + norm_back(unit, rate, norms[0:1, :], upstream)).astype(BF16)
        small[:, u0 : u0 + width] += nn(noisy[at, :].astype(F32).T.astype(BF16), grad_zero)
        grad_start = (keep_root * nt(grad_zero, up_low[...]) - error[at, :]).T
        upper = grad_start.astype(BF16)
        lower = (grad_start - upper.astype(F32)).astype(BF16)
        hot = (columns[:, at].T[:, 0:1] == ids).astype(F32).astype(BF16)
        both = jnp.concatenate([upper, lower], axis=1)
        small[:, e0 : e0 + vocab] += nn(both, jnp.concatenate([hot, hot], axis=0))

    ahead = towards_one(0)
    for r in range(tiles):
        upstream = ahead
        if r + 1 < tiles:
            ahead = towards_one(r + 1)
        through_one(r, upstream)
        if r == 0:
            pump("thin", ("third", 3))
        if r == 2:
            pump("thin", ("second", 0, 1, 2))
    squares = jnp.zeros((1, 1), F32)
    if fused:
        squares = wide.result(0) + wide.result(2) + wide.result(3)
    lanes = emb
    n0 = e0 + vocab
    for k in range(6):
        for j in range(width // lanes):
            row = k * (width // lanes) + j
            small[row : row + 1, n0 : n0 + lanes] = norm_grads[k : k + 1, j * lanes : (j + 1) * lanes]
    if not fused:
        row = lax.broadcasted_iota(jnp.int32, out_scalars.shape, 0)
        out_scalars[...] = jnp.where(row == 1, loss, jnp.where(row == 2, weight_total, 0.0))
        for slot, b in ((0, 1), (1, 3)):
            sent(post_copy(b, slot))
            kept_copy(b, 2 + slot).wait()
        for b in range(4):
            sent(thin_copy(b))
            thin_kept(b).wait()
        return

    for q in range(4):
        value = small[:, q * group : (q + 1) * group].astype(BF16)
        rows = slice((q % 2) * small.shape[0], (q % 2 + 1) * small.shape[0])
        mine = core == q // 2

        @pl.when(mine)
        def keep():
            tiny.own[0, rows, :] = value

        @pl.when(jnp.logical_not(mine))
        def give():
            small_own[rows, :] = value

    give_copy = tiny.pair_copy(0, small_own)
    give_copy.start()
    tiny.take(0)
    pump("thin", ("third", 0, 1, 2))
    tiny.first(0)
    squares = squares + wide.result(1) + thin.result(3)
    tiny.second(0)
    tiny.third(0)
    squares = squares + tiny.result(0)
    tiny_shard[...] = tiny_out[0].astype(BF16)
    gather = QuickGather(tiny_shard, tiny_whole, quick_sems, 16)
    gather.begin()
    squares = squares + thin.result(0) + thin.result(1) + thin.result(2)
    row = lax.broadcasted_iota(jnp.int32, scalars.shape, 0)
    scalars[...] = jnp.where(row == 0, squares, jnp.where(row == 1, loss, 0.0))
    exchange = Exchange(scalars, slots_all, all_sems, devices)
    exchange.start()
    gather.spread()
    gather.share()
    gather.ready()
    exchange.arrive()
    out_scalars[...] = jnp.where(row == 2, weight_total, exchange.total())
    for q in range(4):
        rows = slice((q % 2) * small.shape[0], (q % 2 + 1) * small.shape[0])
        out_small[:, q * group : (q + 1) * group] = tiny_whole[(q // 2) * 2 * emb : (q // 2 + 1) * 2 * emb, :][rows, :].astype(F32)
    for b in range(4):
        sent(thin_copy(b))
    give_copy.wait_send()
    gather.finish()
    exchange.finish()
    for b in range(4):
        wide.finish(b)
        thin.finish(b)
    tiny.finish(0)


def run_backward(fused, wide_whole, thin_whole, tokens, buckets, counted, counts, start, noisy, table_low, kept, up_weight, down_weight, norms, steps, vocab_used):
    zero, one, two, qkv, key_t, att, probs, act, slope, first_t, second_t = kept
    length, width = zero.shape
    pairs = width // SPAN
    blocks = length // SPAN
    emb, vocab = start.shape[1], table_low.shape[0]
    dma, vmem = pltpu.SemaphoreType.DMA, pltpu.VMEM
    anywhere, inside = pl.BlockSpec(memory_space=pl.ANY), pl.BlockSpec(memory_space=pltpu.VMEM)
    spread = 2 * width + vocab + emb
    group = spread // 4
    rows = width // 16

    def made(shape, dtype=BF16):
        return jax.ShapeDtypeStruct(shape, dtype)

    wide_out = made((4, rows, width), F32) if fused else made((4, 2, width, width))
    thin_out = made((4, rows, width // 2), F32) if fused else made((4, 2, width, width // 2))
    out_shape = [wide_out, thin_out, made((emb, spread), F32), made((8, 128), F32)]
    if fused:
        out_shape += [made((4, width, width)), made((4, width, width // 2)), made((1, 2 * emb, group))]
    else:
        out_shape += [made((8, 128))] * 3
    scratch = [
        vmem((length, width), F32),
        vmem((length, width), F32),
        vmem((length, width), F32),
        vmem((length, width), BF16),
        vmem((width, length), BF16),
        vmem((width, length), BF16),
        vmem((length, width), BF16),
        vmem((4, length, width), BF16),
        vmem((4, width, width), BF16),
        vmem((2, length, SPAN), F32),
        vmem((2, blocks // 2, WINDOW, 2 * SPAN), BF16),
        vmem((length, emb), F32),
        vmem((8, width), F32),
        vmem((2 if fused else 4, width, width), BF16),
        vmem((8, 128) if fused else (8, width, width // 2), BF16),
        vmem((8, 128), F32),
        vmem((8, length), F32),
        vmem((emb, width), BF16),
        vmem((width, emb), BF16),
        dma((12,)),
        dma((4,)),
        dma((12,)),
        dma((2,)),
        dma((12,)),
    ]
    if fused:
        scratch += scatter_scratch(4, rows, width) + scatter_scratch(4, rows, width // 2) + scatter_scratch(1, 16, group)
        scratch += [
            vmem((2, width, width), BF16),
            vmem((16, group), BF16),
            vmem((1, 16, group), F32),
            vmem((32, 8, 128), F32),
            dma((2,)),
            dma((7,)),
        ]
        params = pltpu.CompilerParams(collective_id=1, has_side_effects=True, vmem_limit_bytes=VMEM_LIMIT)
    else:
        params = pltpu.CompilerParams(vmem_limit_bytes=VMEM_LIMIT)
    return pl.pallas_call(
        functools.partial(backward_kernel, fused, (length, width, pairs, vocab_used)),
        out_shape=out_shape,
        in_specs=[anywhere] * 2 + [inside] * 4 + [anywhere, inside] + [anywhere] * 11 + [inside] * 4 + [pl.BlockSpec(memory_space=pltpu.SMEM)],
        out_specs=[inside if fused else anywhere] * 2 + [inside] * 2 + [anywhere] * 3,
        scratch_shapes=scratch,
        compiler_params=params,
        name="backward",
    )(wide_whole, thin_whole, tokens, buckets, counted, counts, start, noisy, zero, one, two, qkv, key_t, att, probs, act, slope, first_t, second_t, table_low, up_weight, down_weight, norms, steps)[:4]


def adam_update(weight, grad, first, second, rate, decay):
    first_new = BETA_FIRST * first + (1.0 - BETA_FIRST) * grad
    second_new = BETA_SECOND * second + (1.0 - BETA_SECOND) * grad * grad
    first_hat = first_new / (1.0 - BETA_FIRST**STEP)
    second_hat = second_new / (1.0 - BETA_SECOND**STEP)
    weight_new = weight - rate * (first_hat / (jnp.sqrt(second_hat) + ADAM_EPS) + decay * weight)
    return (first_new, second_new, weight_new)


def clip_factor(squares):
    grad_norm = jnp.sqrt(squares)
    return grad_norm, jnp.minimum(1.0, CLIP_NORM / (grad_norm + 1e-06))


def adam_kernel(*refs):
    sources, outs, held, made = refs[:28], refs[28:55], refs[55:83], refs[83:107]
    in_sems, out_sems = refs[107:]
    order = [0, 1, 2, 3] + [4 + k for index in (6, 5, 3, 0, 1, 2, 4, 7) for k in range(3 * index, 3 * index + 3)]
    loads = {k: pltpu.make_async_copy(sources[k], held[k], in_sems.at[k]) for k in order}
    for k in order:
        loads[k].start()
    wide, thin, small, scalars = held[:4]
    states = held[4:]
    width = wide.shape[2]
    emb = small.shape[0]
    vocab = states[0].shape[0]
    for k in range(4):
        loads[k].wait()
    grad_norm, factor = clip_factor(scalars[0:1, 0:1])
    for out, value in zip(outs[:3], (scalars[1:2, 0:1], scalars[2:3, 0:1], grad_norm)):
        out[...] = value
    stores = []

    def update(index, pieces):
        rate, decay = (NORM_RATE, 0.0) if index == 7 else (MATRIX_RATE, WEIGHT_DECAY)
        mine = range(3 * index, 3 * index + 3)
        for k in mine:
            loads[4 + k].wait()
        for grad, *at in pieces:
            at = tuple(at) or (Ellipsis,)
            weight, first, second = (states[k][at] for k in mine)
            for k, value in zip(mine, adam_update(weight, factor * grad, first, second, rate, decay)):
                made[k][at] = value
        for k in mine:
            stores.append(pltpu.make_async_copy(made[k], outs[3 + k], out_sems.at[k]))
            stores[-1].start()

    def halves(first):
        return [(wide[first + h], slice(None), slice(h * width, (h + 1) * width)) for h in range(2)]

    update(6, halves(2))
    update(5, halves(0))
    update(3, [(thin[j], j) for j in range(3)])
    update(0, [(small[:, 2 * width : -emb].T[:vocab],)])
    update(1, [(small[:, width : 2 * width],)])
    update(2, [(small[:, :width].T,)])
    update(4, [(thin[3],)])
    per = width // emb
    update(
        7,
        [
            (small[k * per + j : k * per + j + 1, -emb:], slice(k, k + 1), slice(j * emb, (j + 1) * emb))
            for k in range(6)
            for j in range(per)
        ],
    )
    for store in stores:
        store.wait()


def run_adam(wide, thin, small, scalars, states):
    inside, anywhere = pl.BlockSpec(memory_space=pltpu.VMEM), pl.BlockSpec(memory_space=pl.ANY)
    sources = (wide, thin, small, scalars, *states)
    shapes = [states[3 * (k // 3)].shape for k in range(24)]
    return pl.pallas_call(
        adam_kernel,
        out_shape=[jax.ShapeDtypeStruct((1, 1), F32)] * 3 + [jax.ShapeDtypeStruct(shape, F32) for shape in shapes],
        in_specs=[anywhere] * 28,
        out_specs=[inside] * 3 + [anywhere] * 24,
        scratch_shapes=[pltpu.VMEM(source.shape, F32) for source in sources]
        + [pltpu.VMEM(shape, F32) for shape in shapes]
        + [pltpu.SemaphoreType.DMA((28,)), pltpu.SemaphoreType.DMA((24,))],
        compiler_params=pltpu.CompilerParams(vmem_limit_bytes=VMEM_LIMIT),
        name="adam",
    )(*sources)


def shards_of(qkv_weight, out_t, fc_weight, proj_t):
    width = fc_weight.shape[1] // 2
    wide = [array[:, h * width : (h + 1) * width] for array in (fc_weight, proj_t) for h in range(2)]
    return jnp.stack(wide).astype(BF16), jnp.concatenate([qkv_weight, out_t[None]]).astype(BF16)


def finished(results):
    return tuple(value.T if k in (15, 16, 17, 21, 22, 23) else value for k, value in enumerate(results))


def per_device(fused, token_ids, segment_ids, timesteps, noise, bucket_ids, counted, embed, up_weight, down_weight, qkv_weight, out_weight, fc_weight, proj_weight, norm_params, embed_m, embed_v, up_m, up_v, down_m, down_v, qkv_m, qkv_v, out_m, out_v, fc_m, fc_v, proj_m, proj_v, norm_m, norm_v):
    length = token_ids.shape[1]
    vocab, emb = embed.shape
    width = up_weight.shape[1]
    places = jnp.asarray(place_table(length, width))
    if fused:
        sources = (qkv_weight, out_weight.T, fc_weight, proj_weight.T)
    else:

        def gathered(shard):
            return lax.all_gather(lax.all_gather(shard, "dp", axis=1, tiled=True), "mp", axis=1)

        sources = tuple(map(gathered, shards_of(qkv_weight, out_weight.T, fc_weight, proj_weight.T)))
    wide_whole, thin_whole, counts, start, noisy, table_low, *kept = run_forward(
        fused, sources, token_ids, segment_ids, timesteps, noise, bucket_ids, counted, embed, up_weight, norm_params, places
    )
    if not fused:
        wide_whole, thin_whole = sources
        counts = lax.psum(counts, "dp")
    wide, thin, small, scalars = run_backward(
        fused, wide_whole, thin_whole, token_ids, bucket_ids, counted, counts, start, noisy, table_low, kept, up_weight, down_weight, norm_params, timesteps, vocab
    )
    states = (
        embed, embed_m, embed_v, up_weight, up_m, up_v, down_weight, down_m, down_v, qkv_weight, qkv_m, qkv_v,
        out_weight.T, out_m.T, out_v.T, fc_weight, fc_m, fc_v, proj_weight.T, proj_m.T, proj_v.T, norm_params, norm_m, norm_v,
    )
    if fused:
        results = list(run_adam(wide, thin, small, scalars, states))
        results[:3] = [value.reshape(()) for value in results[:3]]
        return finished(results)

    def owned(blocks):
        blocks = lax.psum_scatter(blocks.astype(F32), "mp", scatter_dimension=1, tiled=False)
        return lax.psum_scatter(blocks, "dp", scatter_dimension=1, tiled=True)

    wide, thin = owned(wide), owned(thin)
    small, loss_sum = lax.psum((small, scalars[1, 0]), ("dp", "mp"))
    squares = lax.psum(jnp.sum(wide * wide) + jnp.sum(thin * thin), ("dp", "mp")) + jnp.sum(small * small)
    grad_norm, factor = clip_factor(squares)
    grads = (
        small[:, 2 * width : -emb].T[:vocab],
        small[:, width : 2 * width],
        small[:, :width].T,
        thin[:3],
        thin[3],
        jnp.concatenate([wide[0], wide[1]], axis=1),
        jnp.concatenate([wide[2], wide[3]], axis=1),
        small[: 6 * width // emb, -emb:].reshape(6, width),
    )
    results = [loss_sum, scalars[2, 0], grad_norm]
    for index, grad in enumerate(grads):
        rate, decay = (NORM_RATE, 0.0) if index == 7 else (MATRIX_RATE, WEIGHT_DECAY)
        weight, first, second = states[3 * index : 3 * index + 3]
        results.extend(adam_update(weight, factor * grad, first, second, rate, decay))
    return finished(results)


def solution(mesh):
    fused = mesh.shape["dp"] == 16 and mesh.shape["mp"] == 2
    state = {"copied": P(), "qkv": P(None, "dp", "mp"), "tall": P("mp", "dp"), "wide": P("dp", "mp")}
    kinds = ["copied"] * 3 + ["qkv", "tall", "wide", "tall", "copied"]
    weights = [state[kind] for kind in kinds]
    moments = [state[kind] for kind in kinds for unused in range(2)]
    placed = (
        P("dp", None), P("dp", None), P("dp"), P("dp", None, None), P("dp", None), P("dp", None),
        *weights,
        *moments,
    )
    outs = (P(), P(), P()) + tuple(state[kind] for kind in kinds for unused in range(3))
    return jax.shard_map(
        functools.partial(per_device, fused), mesh=mesh, in_specs=placed, out_specs=outs, check_vma=False
    )
```

```python
import functools
import math

import jax
import jax.numpy as jnp
import numpy as np
from jax import lax
from jax.experimental import pallas as pl
from jax.experimental.pallas import tpu as pltpu
from jax.sharding import PartitionSpec as P

HEAD_DIM = 64
NB = 16
T_STEPS = 2000
STEP = 10

NORM_EPS = 1e-05
MASKED = -1e30
BETA_FIRST = 0.9
BETA_SECOND = 0.999
ADAM_EPS = 1e-08
MATRIX_RATE = 0.05
NORM_RATE = 0.5
WEIGHT_DECAY = 0.1
CLIP_NORM = 0.01

TILE = 256
SPAN = 128
WINDOW = 384
MESH = pl.DeviceIdType.MESH
F32 = jnp.float32
BF16 = jnp.bfloat16
VMEM_LIMIT = 62 * 2**20


def nn(left, right):
    return jnp.dot(left, right, preferred_element_type=F32)


def nt(left, right):
    return lax.dot_general(
        left, right, (((1,), (1,)), ((), ())), preferred_element_type=F32
    )


def sine_row(step, width):
    half = width // 2
    lane = lax.broadcasted_iota(jnp.int32, (1, half), 1).astype(F32)
    angles = step * jnp.exp(lane * (-math.log(10000.0) / half))
    return jnp.concatenate([jnp.sin(angles), jnp.cos(angles)], axis=1)


def place_table(length, width):
    half = width // 2
    freqs = np.exp(-math.log(10000.0) * np.arange(half, dtype=np.float64) / half)
    angles = np.arange(length, dtype=np.float64)[:, None] * freqs[None, :]
    return np.concatenate([np.sin(angles), np.cos(angles)], axis=-1).astype(np.float32)


def norm_stats(values):
    width = values.shape[-1]
    center = values - jnp.sum(values, axis=-1, keepdims=True) * (1.0 / width)
    spread = jnp.sum(center * center, axis=-1, keepdims=True) * (1.0 / width)
    rate = lax.rsqrt(spread + NORM_EPS)
    return center * rate, rate


def norm_back(unit, rate, gain, upstream):
    width = unit.shape[-1]
    scaled = upstream * gain
    first = jnp.sum(scaled, axis=-1, keepdims=True) * (1.0 / width)
    second = jnp.sum(scaled * unit, axis=-1, keepdims=True) * (1.0 / width)
    return rate * (scaled - first - unit * second)


def column_sum(values):
    return jnp.sum(values, axis=0, keepdims=True)


def rows_at(index, count):
    return pl.ds(pl.multiple_of(index * count, count), count)


def guarded(condition, action):
    if condition is None:
        action()
    else:
        pl.when(condition)(action)


def position():
    me = lax.axis_index("dp")
    return me, lax.axis_index("mp"), me // 4, lax.rem(me // 2, 2), lax.rem(me, 2)


def index_of(z, y, x):
    return z * 4 + y * 2 + x


def neighbours():
    me, core, z, y, x = position()
    return (index_of(z, y, 1 - x), core), (index_of(z, 1 - y, x), core), (me, 1 - core)


def remote(source, target, send_sem, recv_sem, device):
    return pltpu.make_async_remote_copy(
        src_ref=source,
        dst_ref=target,
        send_sem=send_sem,
        recv_sem=recv_sem,
        device_id=device,
        device_id_type=MESH,
    )


def greet(devices):
    me, core = position()[:2]
    barrier = pltpu.get_barrier_semaphore()
    for device in devices:

        @pl.when(jnp.logical_or(device[0] != me, device[1] != core))
        def signal():
            pl.semaphore_signal(barrier, inc=1, device_id=device, device_id_type=MESH)


def assemble(devices):
    pl.semaphore_wait(pltpu.get_barrier_semaphore(), len(devices) - 1)


class Exchange:
    def __init__(self, source, slots, sems, devices):
        self.source, self.slots, self.sems = source, slots, sems
        me, core = position()[:2]
        self.devices = [(device, jnp.logical_or(device[0] != me, device[1] != core)) for device in devices]
        self.mine = me if len(devices) == 16 else 2 * me + core

    def start(self):
        for device, other in self.devices:
            guarded(other, lambda: remote(self.source, self.slots.at[self.mine], self.sems.at[0], self.sems.at[1], device).start())

    def all_but_one(self):
        rest = self.slots.at[: len(self.devices) - 1]
        return remote(rest, rest, self.sems.at[0], self.sems.at[1], neighbours()[2])

    def arrive(self):
        self.all_but_one().wait_recv()

    def total(self):
        self.slots[self.mine] = self.source[...]
        value = self.slots[0]
        for slot in range(1, len(self.devices)):
            value = value + self.slots[slot]
        return value

    def finish(self):
        self.all_but_one().wait_send()


def same_core():
    core = position()[1]
    return [(d, core) for d in range(16)]


def every_device():
    return [(d, c) for d in range(16) for c in range(2)]


class Gather:
    def __init__(self, shard, whole, sems, rows, planes=(), side_by_side=False):
        self.shard, self.whole, self.rows, self.planes, self.side_by_side = shard, whole, rows, planes, side_by_side
        (self.local_s, self.up_s, self.down_s, self.plane_s, self.pair_s, self.line_r, self.turn_r, self.last_r, self.pair_r) = sems
        self.xn, self.yn, self.pair = neighbours()
        self.me, self.core, self.z, self.y, self.x = position()
        self.up = (jnp.minimum(self.me + 4, 15), self.core)
        self.down = (jnp.maximum(self.me - 4, 0), self.core)

    def part(self, b, c, rows):
        if self.side_by_side:
            width = self.shard.shape[2]
            return self.whole.at[b, rows, pl.ds(pl.multiple_of(c * width, 128), width)]
        return self.whole.at[b, c, rows, :]

    def piece(self, b, c, d):
        return self.part(b, c, rows_at(d, self.rows))

    def send(self, b, d, own, device, sem, recv, condition=None):
        source = self.shard.at[b] if own else self.piece(b, self.core, d)
        guarded(condition, lambda: remote(source, self.piece(b, self.core, d), sem, recv, device).start())

    def pieces(self, b, count, sem, recv):
        some = self.part(b, self.core, slice(0, count * self.rows))
        return remote(some, some, sem, recv, self.pair)

    def spread(self, b, d, zz, own=False, condition=None):
        odd = lax.rem(zz, 2)
        for step in range(2):
            along_y = odd if step == 0 else 1 - odd
            device = (index_of(self.z, jnp.where(along_y == 1, 1 - self.y, self.y), jnp.where(along_y == 1, self.x, 1 - self.x)), self.core)
            recv = self.turn_r.at[b, zz] if step == 0 else self.last_r.at[b]
            self.send(b, d, own, device, self.plane_s.at[b], recv, condition)
        self.send(b, d, own, self.pair, self.pair_s.at[b], self.pair_r.at[b], condition)

    def local(self, b):
        return pltpu.make_async_copy(self.shard.at[b], self.piece(b, self.core, self.me), self.local_s.at[b])

    def plane(self, b, zz):
        return self.part(b, self.core, rows_at(zz, 4 * self.rows))

    def plane_send(self, b, zz, device, sem, recv, condition=None):
        guarded(condition, lambda: remote(self.plane(b, zz), self.plane(b, zz), sem, recv, device).start())

    def begin(self, b):
        self.local(b).start()
        if b in self.planes:
            for yy, xx in ((self.y, 1 - self.x), (1 - self.y, self.x), (1 - self.y, 1 - self.x)):
                device = (index_of(self.z, yy, xx), self.core)
                self.send(b, self.me, True, device, self.plane_s.at[b], self.turn_r.at[b, 0])
            return
        self.send(b, self.me, True, self.up, self.up_s.at[b], self.line_r.at[b, self.z], self.z < 3)
        self.send(b, self.me, True, self.down, self.down_s.at[b], self.line_r.at[b, self.z], self.z > 0)
        self.spread(b, self.me, self.z, True)

    def hop(self, b, distance):
        z = self.z
        if b in self.planes:
            for source, there, upward in (
                (jnp.maximum(z - distance, 0), z >= distance, True),
                (jnp.minimum(z + distance, 3), z + distance <= 3, False),
            ):
                onward = jnp.logical_and(there, z < 3 if upward else z > 0)
                guarded(there, lambda: self.pieces(b, 4, self.up_s.at[b], self.line_r.at[b, source]).wait_recv())
                if distance < 3:
                    device, sem = (self.up, self.up_s) if upward else (self.down, self.down_s)
                    self.plane_send(b, source, device, sem.at[b], self.line_r.at[b, source], onward)
                self.plane_send(b, source, self.pair, self.pair_s.at[b], self.pair_r.at[b], there)
            return
        for source, there, onward, device, sem in (
            (jnp.maximum(z - distance, 0), z >= distance, z < 3, self.up, self.up_s),
            (jnp.minimum(z + distance, 3), z + distance <= 3, z > 0, self.down, self.down_s),
        ):
            d = index_of(source, self.y, self.x)
            guarded(there, lambda: self.pieces(b, 1, self.up_s.at[b], self.line_r.at[b, source]).wait_recv())
            if distance < 3:
                self.send(b, d, False, device, sem.at[b], self.line_r.at[b, source], jnp.logical_and(there, onward))
            self.spread(b, d, source, False, there)

    def turn(self, b):
        if b in self.planes:
            self.local(b).wait()
            self.pieces(b, 3, self.up_s.at[b], self.turn_r.at[b, 0]).wait_recv()
            self.plane_send(b, self.z, self.up, self.up_s.at[b], self.line_r.at[b, self.z], self.z < 3)
            self.plane_send(b, self.z, self.down, self.down_s.at[b], self.line_r.at[b, self.z], self.z > 0)
            self.plane_send(b, self.z, self.pair, self.pair_s.at[b], self.pair_r.at[b])
            return
        for zz in range(4):
            yy, xx = (1 - self.y, self.x) if zz % 2 else (self.y, 1 - self.x)
            d = index_of(zz, yy, xx)
            self.pieces(b, 1, self.up_s.at[b], self.turn_r.at[b, zz]).wait_recv()
            self.send(b, d, False, self.xn if zz % 2 else self.yn, self.plane_s.at[b], self.last_r.at[b])
            self.send(b, d, False, self.pair, self.pair_s.at[b], self.pair_r.at[b])

    def last(self, b):
        self.pieces(b, 8, self.up_s.at[b], self.last_r.at[b]).wait_recv()
        for zz in range(4):
            yy, xx = (self.y, 1 - self.x) if zz % 2 else (1 - self.y, self.x)
            for d in (index_of(zz, yy, xx), index_of(zz, 1 - self.y, 1 - self.x)):
                self.send(b, d, False, self.pair, self.pair_s.at[b], self.pair_r.at[b])

    def ready(self, b):
        if b not in self.planes:
            self.local(b).wait()
        self.pieces(b, 16, self.up_s.at[b], self.pair_r.at[b]).wait_recv()

    def finish(self):
        for b in range(self.shard.shape[0]):
            whole_plane = b in self.planes
            per = 4 if whole_plane else 1
            self.pieces(b, 3 if whole_plane else 12, self.plane_s.at[b], self.pair_r.at[b]).wait_send()
            self.pieces(b, 16, self.pair_s.at[b], self.pair_r.at[b]).wait_send()
            for z in range(4):

                @pl.when(self.z == z)
                def line():
                    if z < 3:
                        self.pieces(b, per * (z + 1), self.up_s.at[b], self.pair_r.at[b]).wait_send()
                    if z > 0:
                        self.pieces(b, per * (4 - z), self.down_s.at[b], self.pair_r.at[b]).wait_send()


class QuickGather:
    def __init__(self, shard, whole, sems, rows):
        self.shard, self.whole, self.rows, self.sems = shard, whole, rows, sems
        self.me, self.core, self.z, self.y, self.x = position()

    def piece(self, c, d):
        return self.whole.at[rows_at(16 * c + d, self.rows), :]

    def send(self, d, own, device, recv, condition=None):
        source = self.shard if own else self.piece(self.core, d)
        guarded(condition, lambda: remote(source, self.piece(self.core, d), self.sems.at[1], self.sems.at[recv], device).start())

    def pieces(self, count, recv):
        some = self.whole.at[: count * self.rows, :]
        return remote(some, some, self.sems.at[1], self.sems.at[recv], (self.me, 1 - self.core))

    def local(self):
        return pltpu.make_async_copy(self.shard, self.piece(self.core, self.me), self.sems.at[0])

    def plane(self, zz, own, condition=None):
        d = index_of(zz, self.y, self.x)
        for k, (yy, xx) in enumerate(((self.y, 1 - self.x), (1 - self.y, self.x), (1 - self.y, 1 - self.x))):
            self.send(d, own, (index_of(self.z, yy, xx), self.core), 4 + k, condition)
        self.send(d, own, (self.me, 1 - self.core), 3, condition)

    def begin(self):
        self.local().start()
        for zz in range(4):
            self.send(self.me, True, (index_of(zz, self.y, self.x), self.core), 2, self.z != zz)
        self.plane(self.z, True)

    def spread(self):
        self.pieces(3, 2).wait_recv()
        for zz in range(4):
            self.plane(zz, False, self.z != zz)

    def share(self):
        for k, (yy, xx) in enumerate(((self.y, 1 - self.x), (1 - self.y, self.x), (1 - self.y, 1 - self.x))):
            self.pieces(4, 4 + k).wait_recv()
            for zz in range(4):
                self.send(index_of(zz, yy, xx), False, (self.me, 1 - self.core), 3)

    def ready(self):
        self.local().wait()
        self.pieces(16, 3).wait_recv()

    def finish(self):
        self.pieces(31, 2).wait_send()


GATHER_REFS = 9


def gather_sems(count):
    dma = pltpu.SemaphoreType.DMA
    one, four = dma((count,)), dma((count, 4))
    return [one, one, one, one, one, four, four, one, one]


class Scatter:
    def __init__(self, refs, landed, loaded, out, rows):
        (self.own, self.near, self.far, self.lined, self.pair_s, self.pair_r, self.load_s) = refs[:7]
        self.near_s, self.near_r, self.far_s, self.far_r, self.line_s, self.line_r = refs[7:]
        self.landed, self.loaded, self.out, self.rows = landed, loaded, out, rows
        self.xn, self.yn, self.pair = neighbours()
        self.me, self.core, self.z, self.y, self.x = position()

    def piece(self, b, zz, yy, xx):
        return self.own.at[b, rows_at(index_of(zz, yy, xx), self.rows), :]

    def pair_copy(self, b, source):
        return remote(source, self.landed.at[b], self.pair_s.at[b], self.pair_r.at[b], self.pair)

    def load(self, b):
        return pltpu.make_async_copy(self.landed.at[b], self.loaded[b], self.load_s.at[b])

    def near_copy(self, b, zz, i):
        place, device = ((zz, i, 1 - self.x), self.xn) if zz % 2 else ((zz, 1 - self.y, i), self.yn)
        group = jnp.where(i == self.onward(zz), 0, 1)
        return remote(
            self.piece(b, *place), self.near.at[b, zz, i], self.near_s.at[b], self.near_r.at[b, group], device
        )

    def onward(self, zz):
        return 1 - self.y if zz % 2 else 1 - self.x

    def far_place(self, zz):
        return (zz, 1 - self.y, self.x) if zz % 2 else (zz, self.y, 1 - self.x)

    def far_copy(self, b, zz):
        return remote(
            self.piece(b, *self.far_place(zz)), self.far.at[b, zz], self.far_s.at[b], self.far_r.at[b],
            self.yn if zz % 2 else self.xn,
        )

    def line_copy(self, b, zz):
        there = (index_of(zz, self.y, self.x), self.core)
        return remote(
            self.near.at[b, zz, 1 - self.onward(zz)], self.lined.at[b, self.z], self.line_s.at[b], self.line_r.at[b], there
        )

    def pieces(self, b, count, send_sem, recv_sem):
        some = self.own.at[b, : count * self.rows, :]
        return remote(some, some, send_sem.at[b], recv_sem, self.pair)

    def take(self, b):
        self.pair_copy(b, self.own.at[b]).wait_recv()
        self.load(b).start()

    def first(self, b):
        self.load(b).wait()
        loaded = self.loaded[b]

        def add(d, carry):
            at = rows_at(d, self.rows)
            self.own[b, at, :] = (self.own[b, at, :].astype(F32) + loaded[at, :].astype(F32)).astype(self.own.dtype)
            return carry

        lax.fori_loop(0, 16, add, 0)
        for zz in range(4):
            self.near_copy(b, zz, self.onward(zz)).start()
        for zz in range(4):
            self.near_copy(b, zz, 1 - self.onward(zz)).start()

    def second(self, b):
        self.pieces(b, 4, self.near_s, self.near_r.at[b, 0]).wait_recv()
        for zz in range(4):
            i = self.onward(zz)
            place = self.far_place(zz)
            value = self.piece(b, *place)[...].astype(F32) + self.near[b, zz, i].astype(F32)
            self.piece(b, *place)[...] = value.astype(self.own.dtype)
            self.far_copy(b, zz).start()

    def third(self, b):
        self.pieces(b, 4, self.near_s, self.near_r.at[b, 1]).wait_recv()
        self.pieces(b, 4, self.near_s, self.far_r.at[b]).wait_recv()
        for zz in range(4):
            i = 1 - self.onward(zz)
            value = self.piece(b, zz, self.y, self.x)[...].astype(F32) + self.near[b, zz, i].astype(F32) + self.far[b, zz].astype(F32)

            @pl.when(self.z == zz)
            def keep():
                self.out[b] = value

            @pl.when(self.z != zz)
            def give():
                self.near[b, zz, i] = value.astype(self.near.dtype)
                self.line_copy(b, zz).start()

    def result(self, b):
        self.pieces(b, 3, self.near_s, self.line_r.at[b]).wait_recv()
        for zz in range(4):

            @pl.when(self.z != zz)
            def add():
                self.out[b] += self.lined[b, zz].astype(F32)

        value = self.out[b]
        return jnp.sum(value * value, keepdims=True)

    def finish(self, b):
        self.pieces(b, 8, self.near_s, self.line_r.at[b]).wait_send()
        self.pieces(b, 4, self.far_s, self.line_r.at[b]).wait_send()
        self.pieces(b, 3, self.line_s, self.line_r.at[b]).wait_send()


SCATTER_REFS = 13


def scatter_scratch(count, rows, columns):
    dma, vmem = pltpu.SemaphoreType.DMA, pltpu.VMEM
    return [
        vmem((count, 16 * rows, columns), BF16),
        vmem((count, 4, 2, rows, columns), BF16),
        vmem((count, 4, rows, columns), BF16),
        vmem((count, 4, rows, columns), BF16),
        dma((count,)), dma((count,)), dma((count,)),
        dma((count,)), dma((count, 2)), dma((count,)), dma((count,)), dma((count,)), dma((count,)),
    ]


def gelu_parts(values):
    root = 0.7978845608028654
    square = values * values
    half = 0.5 + 0.5 * jnp.tanh(values * (root + (root * 0.044715) * square))
    active = values * half
    return active, half + active * (1.0 - half) * (2.0 * root + (6.0 * root * 0.044715) * square)


def halves_of(shape, axis, scale):
    low = lax.broadcasted_iota(jnp.int32, shape, axis) < HEAD_DIM
    return jnp.where(low, scale, 0.0).astype(BF16), jnp.where(low, 0.0, scale).astype(BF16)


def pick_halves(wide):
    low = lax.broadcasted_iota(jnp.int32, (2 * HEAD_DIM, SPAN), 0) < HEAD_DIM
    return jnp.where(low, wide[:, :SPAN], wide[:, SPAN:])


def window_start(block, blocks):
    return min(max(block - 1, 0), blocks - WINDOW // SPAN) * SPAN


def column_table(rows, length):
    rows = rows + [jnp.zeros((1, length), F32)] * (8 - len(rows))
    return jnp.concatenate(rows, axis=0).T


def one_hot(ids, vocab):
    lanes = lax.broadcasted_iota(jnp.int32, (ids.shape[0], vocab), 1).astype(F32)
    return ids == lanes


def forward_kernel(fused, shapes, *refs):
    length, width, pairs = shapes
    blocks = length // SPAN
    tiles = length // TILE
    half = width // 2
    sources = 4 if fused else 2
    (
        tokens, segments, steps, noise_in, buckets, counted, embed_in, up_in, norms, places_in,
        wide_whole, thin_whole, count_out, start_out, noisy_out, table_out, zero_out, one_out, two_out, qkv_out, keyt_out, att_out, probs_out, act_out, slope_out, first_t_out, second_t_out,
        h_zero, h_one, h_two, normed, normed_t, qkv, key_t, value_t, att, probs, act, slope, weights, bias, places, table, table3, columns, count_own, noise, embed, up_weight, start, noisy, table_low,
        out_sems, probs_sems, weight_sems, in_sems,
    ) = refs[sources : sources + 56]
    rest = refs[sources + 56 :]
    core = lax.axis_index("mp")
    saves = []

    def save(source, target):
        copy = pltpu.make_async_copy(source, target, out_sems.at[len(saves)])
        copy.start()
        saves.append(copy)

    if fused:
        everyone = same_core() + [neighbours()[2]]
        greet(everyone)
        qkv_weight, out_weight, fc_weight, proj_weight = rest[:4]
        wide_shard, thin_shard, counts, count_sems = rest[4:8]
        rows = wide_shard.shape[1]
        wide = Gather(wide_shard, wide_whole, rest[8 : 8 + GATHER_REFS], rows, planes=(3,))
        thin = Gather(thin_shard, thin_whole, rest[8 + GATHER_REFS :], rows, side_by_side=True)
        gathers = {"wide": wide, "thin": thin}
        moves = list(zip(refs[:4], rest[:4]))
    else:
        moves = []
    moves += [(noise_in.at[core], noise), (embed_in, embed), (up_in, up_weight), (places_in, places)]
    fetches = [pltpu.make_async_copy(source, target, in_sems.at[k]) for k, (source, target) in enumerate(moves)]
    for copy in fetches:
        copy.start()
    if fused:
        wide_from, thin_from = wide_whole, thin_whole
        for copy in fetches[:4]:
            copy.wait()
        for j in range(3):
            thin_shard[j] = qkv_weight[j].astype(BF16)
        thin_shard[3] = out_weight[...].astype(BF16)
        for h in range(2):
            cols = slice(h * width, (h + 1) * width)
            wide_shard[h] = fc_weight[:, cols].astype(BF16)
            wide_shard[2 + h] = proj_weight[:, cols].astype(BF16)
    else:
        wide_from, thin_from = refs[:2]

    def pump(*items):
        if fused:
            for which, name, b, *more in items:
                getattr(gathers[which], name)(b, *more)

    live = counted[...].astype(F32)
    lane = lax.broadcasted_iota(jnp.int32, count_own.shape, 1)
    own_counts = jnp.zeros(count_own.shape, F32)
    for bucket in range(NB):
        found = jnp.sum(jnp.where(buckets[...] == bucket, live, 0.0), keepdims=True)
        own_counts = jnp.where(lane == bucket, found, own_counts)
    count_own[...] = own_counts
    token_row = tokens[pl.ds(core, 1), :].astype(F32)
    segment_row = segments[pl.ds(core, 1), :].astype(F32)
    columns[...] = column_table([token_row, segment_row], length)
    emb = embed.shape[1]
    for copy in fetches[-4:]:
        copy.wait()
    table[...] = jnp.zeros(table.shape, F32)
    table[: embed.shape[0], :] = embed[...]
    left = table[...]
    for third in range(3):
        part = left.astype(BF16)
        table3[:, third * emb : (third + 1) * emb] = part
        if third == 0:
            table_low[...] = part
        left = left - part.astype(F32)
    step = jnp.full((1, 1), steps[core], jnp.int32).astype(F32)
    keep = 1.0 - jnp.sqrt(step * (1.0 / T_STEPS) + 0.0001)
    keep_root, noise_root = jnp.sqrt(keep), jnp.sqrt(1.0 - keep)
    time_row = sine_row(step, width)
    up_low = up_weight[...].astype(BF16)

    def embed_tile(r):
        at = rows_at(r, TILE)
        hot = one_hot(columns[at, 0:1], table.shape[0]).astype(F32).astype(BF16)
        thirds = nn(hot, table3[...])
        first = thirds[:, :emb] + thirds[:, emb : 2 * emb] + thirds[:, 2 * emb :]
        start[at, :] = first
        low = (keep_root * first + noise_root * noise[at, :]).astype(BF16)
        noisy[at, :] = low
        hidden = nn(low, up_low) + places[at, :] + time_row
        h_zero[at, :] = hidden
        unit = norm_stats(hidden)[0]
        scaled = unit * norms[0:1, :] + norms[1:2, :]
        normed[at, :] = scaled.astype(BF16)
        normed_t[0, :, at] = scaled.T.astype(BF16)

    if fused:
        assemble(everyone)
        exchange = Exchange(count_own, counts, count_sems, same_core())
        exchange.start()
    early = range(3)
    pump(*[("thin", "begin", b) for b in early])
    embed_tile(0)
    for distance in (1, 2, 3):
        pump(*[("thin", "hop", b, distance) for b in early])
    embed_tile(1)
    pump(*[("thin", "turn", b) for b in early])
    for r in range(2, tiles):
        embed_tile(r)
    second_group = [("thin", 3), ("wide", 0), ("wide", 1)]
    third_group = [("wide", 2)]

    def steps(group, name, *more):
        return [(which, name, b, *more) for which, b in group]

    pump(*steps(second_group, "begin"), ("wide", "begin", 3))
    save(h_zero, zero_out)
    save(start, start_out)
    save(noisy, noisy_out)
    save(table_low, table_out)
    save(normed_t.at[0], first_t_out)
    for i in range(blocks):
        w0 = window_start(i, blocks)
        same = columns[w0 : w0 + WINDOW, 1:2] == segment_row[:, i * SPAN : (i + 1) * SPAN]
        bias[i] = jnp.where(same, 0.0, MASKED)
    pump(*[("thin", "last", b) for b in early])

    def load_wide(b, c, slot):
        return pltpu.make_async_copy(wide_from.at[b, c], weights.at[slot], weight_sems.at[slot])

    def load_thin(b):
        return pltpu.make_async_copy(thin_from.at[b], weights.at[b], weight_sems.at[b])

    for b in early:
        pump(("thin", "ready", b))
        load_thin(b).start()
    pump(*steps(second_group, "hop", 1))
    for j in early:
        load_thin(j).wait()

        def project(r, carry):
            at = rows_at(r, TILE)
            value = nn(normed[at, :], weights[j])
            qkv[j, at, :] = value.astype(BF16)
            if j > 0:
                (key_t if j == 1 else value_t)[:, at] = value.T.astype(BF16)
            return carry

        lax.fori_loop(0, tiles, project, 0, unroll=True)
        if j > 0:
            pump(*(steps(second_group, "hop", 2) if j == 1 else steps(third_group, "begin")))
    for j in range(3):
        save(qkv.at[j], qkv_out.at[j])
    save(key_t, keyt_out)

    def probs_copy(pair, slot):
        return pltpu.make_async_copy(probs.at[slot], probs_out.at[pl.ds(pair * blocks, blocks)], probs_sems.at[slot])

    low, high = halves_of((1, SPAN), 1, 0.125)

    def attend(pair, carry):
        slot = lax.rem(pair, 2)
        cols = pl.ds(pl.multiple_of(pair * SPAN, SPAN), SPAN)

        @pl.when(pair >= 2)
        def free():
            probs_copy(pair - 2, slot).wait()

        def ask(i):
            w0 = window_start(i, blocks)
            queries = qkv[0, i * SPAN : (i + 1) * SPAN, cols]
            both = jnp.concatenate([queries * low, queries * high], axis=0)
            return nt(qkv[1, w0 : w0 + WINDOW, cols], both)

        def answer(i, prob):
            w0 = window_start(i, blocks)
            mixed = nn(value_t[cols, w0 : w0 + WINDOW], prob)
            att[i * SPAN : (i + 1) * SPAN, cols] = pick_halves(mixed).T.astype(BF16)

        ahead, behind = ask(0), None
        for i in range(blocks):
            mask = bias[i]
            scores = ahead + jnp.concatenate([mask, mask], axis=1)
            if i + 1 < blocks:
                ahead = ask(i + 1)
            if i > 0:
                answer(i - 1, behind)
            most = jnp.max(scores, axis=0, keepdims=True)
            raised = jnp.exp(scores - most)
            share = 1.0 / jnp.sum(raised, axis=0, keepdims=True)
            behind = (raised * share).astype(BF16)
            probs[slot, i] = behind
        answer(blocks - 1, behind)
        probs_copy(pair, slot).start()
        return carry

    middle = [
        steps(second_group, "hop", 3) + [("wide", "turn", 3)],
        steps(third_group, "hop", 1),
        steps(second_group, "turn"),
        steps(third_group, "hop", 2) + [("wide", "hop", 3, 1)],
        steps(second_group[:2], "last") + steps(second_group[:1], "ready"),
        steps(third_group, "hop", 3) + [("wide", "hop", 3, 2)],
    ]
    for part in range(6):
        lax.fori_loop(part * pairs // 6, (part + 1) * pairs // 6, attend, 0)
        pump(*middle[part])
        if part == 4:
            load_thin(3).start()
    for pair in (pairs - 2, pairs - 1):
        probs_copy(pair, pair % 2).wait()
    save(att, att_out)
    load_thin(3).wait()
    pump(("wide", "ready", 0))
    for c in range(2):
        load_wide(0, c, 4 + c).start()

    def after_attention(r, carry):
        at = rows_at(r, TILE)
        mixed = att[at, :]
        hidden = h_zero[at, :] + nt(mixed, weights[3])
        h_one[at, :] = hidden
        unit = norm_stats(hidden)[0]
        scaled = unit * norms[2:3, :] + norms[3:4, :]
        normed[at, :] = scaled.astype(BF16)
        normed_t[1, :, at] = scaled.T.astype(BF16)
        return carry

    lax.fori_loop(0, tiles, after_attention, 0, unroll=True)
    save(h_one, one_out)
    save(normed_t.at[1], second_t_out)
    pump(*steps(third_group, "turn"), ("wide", "last", 1))
    for j in range(4):
        load_wide(j // 2, j % 2, 4 + j).wait()
        stages = [(slice(k, k + TILE), slice(r, r + 2 * TILE)) for k in range(0, width, TILE) for r in range(0, length, 2 * TILE)]

        def before_gelu(stage):
            chunk, at = stage
            return nn(normed[at, :], weights[4 + j, :, chunk])

        ahead = before_gelu(stages[0])
        for k, (chunk, at) in enumerate(stages):
            before = ahead
            if k + 1 < len(stages):
                ahead = before_gelu(stages[k + 1])
            active, bend = gelu_parts(before)
            act[j, at, chunk] = active.astype(BF16)
            slope[j, at, chunk] = bend.astype(BF16)
        save(act.at[j], act_out.at[j])
        save(slope.at[j], slope_out.at[j])
        if j == 0:
            pump(("wide", "ready", 1))
            for c in range(2):
                load_wide(1, c, 6 + c).start()
            pump(("wide", "hop", 3, 3), ("wide", "last", 2))
        elif j > 1:
            pump(("wide", "ready", j))
            for c in range(2):
                load_wide(j, c, 2 * (j - 2) + c).start()

    for h in range(2):
        for c in range(2):
            load_wide(2 + h, c, 2 * h + c).wait()

        for r in range(tiles):
            at = slice(r * TILE, (r + 1) * TILE)
            total = (h_two if h else h_one)[at, :]
            for j in (2 * h, 2 * h + 1):
                total = total + nt(act[j, at, :], weights[j])
            h_two[at, :] = total
            if h:
                save(h_two.at[at, :], two_out.at[at, :])

    if fused:
        exchange.arrive()
        count_out[...] = exchange.total()
        wide.finish()
        thin.finish()
        exchange.finish()
    else:
        count_out[...] = count_own[...]
    for copy in saves:
        copy.wait()


def run_forward(fused, sources, tokens, segments, steps, noise, buckets, counted, embed, up_weight, norms, places):
    length, width = places.shape
    pairs = width // SPAN
    blocks = length // SPAN
    dma, vmem = pltpu.SemaphoreType.DMA, pltpu.VMEM
    anywhere, inside = pl.BlockSpec(memory_space=pl.ANY), pl.BlockSpec(memory_space=pltpu.VMEM)
    vocab, emb = embed.shape
    padded = -(-vocab // 128) * 128

    def made(shape, dtype=BF16):
        return jax.ShapeDtypeStruct(shape, dtype)

    out_shape = [
        made((4, 2, width, width)),
        made((4, width, width)),
        made((8, 128), F32),
        made((length, emb), F32),
        made((length, emb)),
        made((padded, emb)),
        made((length, width), F32),
        made((length, width), F32),
        made((length, width), F32),
        made((3, length, width)),
        made((width, length)),
        made((length, width)),
        made((pairs * blocks, WINDOW, 2 * SPAN)),
        made((4, length, width)),
        made((4, length, width)),
        made((width, length)),
        made((width, length)),
    ]
    scratch = [
        vmem((length, width), F32),
        vmem((length, width), F32),
        vmem((length, width), F32),
        vmem((length, width), BF16),
        vmem((2, width, length), BF16),
        vmem((3, length, width), BF16),
        vmem((width, length), BF16),
        vmem((width, length), BF16),
        vmem((length, width), BF16),
        vmem((2, blocks, WINDOW, 2 * SPAN), BF16),
        vmem((4, length, width), BF16),
        vmem((4, length, width), BF16),
        vmem((8, width, width), BF16),
        vmem((blocks, WINDOW, SPAN), F32),
        vmem((length, width), F32),
        vmem((padded, emb), F32),
        vmem((padded, 3 * emb), BF16),
        vmem((length, 8), F32),
        vmem((8, 128), F32),
        vmem((length, emb), F32),
        vmem((vocab, emb), F32),
        vmem((emb, width), F32),
        vmem((length, emb), F32),
        vmem((length, emb), BF16),
        vmem((padded, emb), BF16),
        dma((24,)),
        dma((2,)),
        dma((12,)),
        dma((8,)),
    ]
    params = dict(vmem_limit_bytes=VMEM_LIMIT)
    if fused:
        rows = width // 16
        scratch += [vmem(source.shape, F32) for source in sources]
        scratch += [vmem((4, rows, width), BF16), vmem((4, rows, width // 2), BF16)]
        scratch += [vmem((16, 8, 128), F32), dma((2,))] + gather_sems(4) + gather_sems(4)
        params.update(collective_id=0, has_side_effects=True)
    return pl.pallas_call(
        functools.partial(forward_kernel, fused, (length, width, pairs)),
        out_shape=out_shape,
        in_specs=[anywhere] * len(sources)
        + [inside, inside, pl.BlockSpec(memory_space=pltpu.SMEM), anywhere]
        + [inside] * 2
        + [anywhere] * 2
        + [inside, anywhere],
        out_specs=[anywhere] * 2 + [inside] + [anywhere] * 14,
        scratch_shapes=scratch,
        compiler_params=pltpu.CompilerParams(**params),
        name="forward",
    )(*sources, tokens, segments, steps, noise, buckets, counted, embed, up_weight, norms, places)


def backward_kernel(fused, shapes, *refs):
    length, width, pairs, vocab_used = shapes
    blocks = length // SPAN
    tiles = length // TILE
    half = width // 2
    (
        wide_whole, thin_whole, tokens, buckets, counted, counts, start, noisy, zero_in, one_in, two_in, qkv_in, keyt_in, att_in, probs_in, act_in, slope_in, first_t_in, second_t_in,
        embed_low, up_weight, down_weight, norms, steps,
        out_wide, out_thin, out_small, out_scalars, wide_landed, thin_landed, small_landed,
        hidden, grad, back, branch, branch_t, normed_t, pre, slots, weights, acc, probs, error, norm_grads, posted, thin_posted, scalars, columns, up_low, down_low,
        load_sems, slot_sems, weight_sems, probs_sems, post_sems,
    ) = refs[:55]
    core = lax.axis_index("mp")
    small = out_small
    emb = start.shape[1]
    vocab = embed_low.shape[0]
    side = width // TILE

    if fused:
        rest = refs[55:]
        n = SCATTER_REFS
        loaded, tiny_shard, tiny_out, slots_all, all_sems, quick_sems = rest[3 * n :]
        group = out_small.shape[1] // 4
        tiny_loaded = branch.at[: 2 * emb, :group]
        small_own = branch.at[2 * emb : 4 * emb, :group]
        tiny_whole = pre.at[: 4 * emb, :group]
        wide_loaded = [loaded.at[b % 2] for b in range(4)]
        thin_loaded = [loaded.at[b // 2, :, (b % 2) * half : (b % 2 + 1) * half] for b in range(4)]
        wide = Scatter(rest[:n], wide_landed, wide_loaded, out_wide, width // 16)
        thin = Scatter(rest[n : 2 * n], thin_landed, thin_loaded, out_thin, width // 16)
        tiny = Scatter(rest[2 * n : 3 * n], small_landed, [tiny_loaded], tiny_out, 16)
        devices = every_device()

    def pump(scatter_name, *steps):
        if fused:
            scatter = wide if scatter_name == "wide" else thin
            for name, *members in steps:
                for b in members:
                    getattr(scatter, name)(b)

    def posted_half(b):
        return posted.at[b // 2, :, (b % 2) * half : (b % 2 + 1) * half]

    def post_copy(b, slot):
        if fused:
            return wide.pair_copy(b, posted.at[slot])
        return pltpu.make_async_copy(posted.at[slot], out_wide.at[b, 1 - core], post_sems.at[slot])

    def thin_copy(b):
        if fused:
            return thin.pair_copy(b, posted_half(b))
        return pltpu.make_async_copy(thin_posted.at[b], out_thin.at[b, 1 - core], post_sems.at[4 + b])

    def kept_copy(b, slot):
        return pltpu.make_async_copy(posted.at[slot], out_wide.at[b, core], post_sems.at[slot])

    def thin_kept(b):
        return pltpu.make_async_copy(thin_posted.at[4 + b], out_thin.at[b, core], post_sems.at[8 + b])

    def sent(copy):
        (copy.wait_send if fused else copy.wait)()

    def fetch(source, target, k):
        copy = pltpu.make_async_copy(source, target, load_sems.at[k])
        copy.start()
        return copy

    def load_weights(b, c, slot):
        return pltpu.make_async_copy(wide_whole.at[b, c], weights.at[slot], weight_sems.at[slot])

    def load_thin(b):
        return pltpu.make_async_copy(thin_whole.at[b], weights.at[b], weight_sems.at[4 + b])

    def load_slot(source, slot):
        return pltpu.make_async_copy(source, slots.at[slot], slot_sems.at[slot])

    def other_first(k):
        return 1 - core if k == 0 else core

    def act_load(k):
        return load_slot(act_in.at[2 * (k % 2) + other_first(k // 2)], k)

    def slope_load(s):
        return load_slot(slope_in.at[2 * (s // 2) + other_first(s % 2)], s)

    def feed(s):
        c = other_first(s % 2)
        return [load_weights(s // 2, c, 2 * (s % 2)), load_weights(2 + s // 2, c, 2 * (s % 2) + 1)]

    start_copy = fetch(start, error, 3)
    two_copies = [
        fetch(two_in.at[r * TILE : (r + 1) * TILE, :], hidden.at[r * TILE : (r + 1) * TILE, :], 4 + r) for r in range(tiles)
    ]
    if fused:
        greet(devices)
    normed_copy = fetch(second_t_in, normed_t, 1)
    for k in range(4):
        act_load(k).start()
    for copy in feed(0) + feed(1):
        copy.start()
    norm_grads[...] = jnp.zeros(norm_grads.shape, F32)
    columns[...] = jnp.zeros(columns.shape, F32)
    small[...] = jnp.zeros(small.shape, F32)
    count_row = counts[0:1, :]
    live_total = jnp.sum(count_row, keepdims=True)
    bucket_weight = live_total / (NB * jnp.maximum(count_row, 1.0))
    weight_total = jnp.sum(count_row * bucket_weight, keepdims=True)
    bucket_row = buckets[pl.ds(core, 1), :]
    scale = jnp.zeros((1, length), F32)
    for bucket in range(NB):
        scale = jnp.where(bucket_row == bucket, bucket_weight[:, bucket : bucket + 1], scale)
    scale = scale * counted[pl.ds(core, 1), :].astype(F32)
    columns[0:1, :] = tokens[pl.ds(core, 1), :].astype(F32)
    columns[1:2, :] = scale
    columns[2:3, :] = scale / weight_total
    step = jnp.full((1, 1), steps[core], jnp.int32).astype(F32)
    keep_root = jnp.sqrt(1.0 - jnp.sqrt(step * (1.0 / T_STEPS) + 0.0001))
    up_low[...] = up_weight[...].astype(BF16)
    down_low[...] = down_weight[...].astype(BF16)
    ids = lax.broadcasted_iota(jnp.int32, (TILE, vocab), 1).astype(F32)
    pad_row = jnp.where(lax.broadcasted_iota(jnp.int32, (1, vocab), 1) < vocab_used, 0.0, MASKED)
    start_copy.wait()
    d0, u0, e0 = 0, width, 2 * width

    def add_norm(row, upstream, unit):
        norm_grads[row : row + 1, :] += column_sum(upstream * unit)
        norm_grads[row + 1 : row + 2, :] += column_sum(upstream)

    def head_first(r):
        two_copies[r].wait()
        at = slice(r * TILE, (r + 1) * TILE)
        unit, rate = norm_stats(hidden[at, :])
        ended = (unit * norms[4:5, :] + norms[5:6, :]).astype(BF16)
        predicted = nn(ended, down_low[...])
        return unit, rate, ended, predicted, nt(predicted.astype(BF16), embed_low[...]) + pad_row

    def head(r, loss, before):
        at = slice(r * TILE, (r + 1) * TILE)
        unit, rate, ended, predicted, logits = before
        most = jnp.max(logits, axis=-1, keepdims=True)
        raised = jnp.exp(logits - most)
        total = jnp.sum(raised, axis=-1, keepdims=True)
        table = columns[:, at].T
        hit = table[:, 0:1] == ids
        picked = jnp.sum(jnp.where(hit, logits, 0.0), axis=-1, keepdims=True)
        miss = predicted - error[at, :]
        per_token = jnp.sum(miss * miss, axis=-1, keepdims=True) * (1.0 / emb) + (jnp.log(total) + most) - picked
        loss = loss + jnp.sum(table[:, 1:2] * per_token, keepdims=True)
        coef = table[:, 2:3]
        grad_logits = (coef * (raised * (1.0 / total) - jnp.where(hit, 1.0, 0.0))).astype(BF16)
        grad_error = coef * 2.0 * miss * (1.0 / emb)
        error[at, :] = grad_error
        grad_pred = nn(grad_logits, embed_low[...]) + grad_error
        grad_pred_low = grad_pred.astype(BF16)
        small[:, d0 : d0 + width] += nn(grad_pred.T.astype(BF16), ended)
        small[:, e0 : e0 + vocab] += nn(predicted.T.astype(BF16), grad_logits)
        upstream = nt(grad_pred_low, down_low[...])
        add_norm(4, upstream, unit)
        result = norm_back(unit, rate, norms[4:5, :], upstream)
        grad[at, :] = result
        branch[at, :] = result.astype(BF16)
        branch_t[:, at] = result.T.astype(BF16)
        return loss

    loss = jnp.zeros((1, 1), F32)
    ahead = head_first(0)
    for r in range(tiles):
        before = ahead
        if r + 1 < tiles:
            ahead = head_first(r + 1)
        loss = head(r, loss, before)
    one_copy = fetch(one_in, hidden, 0)
    normed_copy.wait()

    def weigh(left, right, h, kind, mine):
        slot = (2 if mine else 0) + kind if not fused else kind

        def body(m, carry):
            at = rows_at(m, TILE)
            value = nn(left[at, :], right[...]).astype(BF16)
            if mine and fused:
                wide.own[2 * kind + h, at, :] = value
            else:
                posted[slot, at, :] = value
            return carry

        b = 2 * kind + h
        if h == 1 and not mine:
            sent(post_copy(b - 1, slot))
        if h == 1 and mine and not fused:
            kept_copy(b - 1, slot).wait()
        lax.fori_loop(0, side, body, 0, unroll=True)
        if not mine:
            post_copy(b, slot).start()
        elif fused:
            wide.take(b)
        else:
            kept_copy(b, slot).start()

    if fused:
        assemble(devices)
    for k in range(4):
        act_load(k).wait()
        weigh(branch_t, slots.at[k], k % 2, 1, k >= 2)
        slope_load(k).start()
    pump("wide", ("first", 2, 3))

    for s in range(4):
        h = s // 2
        for copy in feed(s):
            copy.wait()
        slope_load(s).wait()
        first = 2 * (s % 2)
        fc, proj, bend = weights.at[first], weights.at[first + 1], slots.at[s]

        def through(r):
            at = slice(r * TILE, (r + 1) * TILE)
            pushed = (nn(branch[at, :], proj[...]) * bend[at, :].astype(F32)).astype(BF16)
            pre[at, :] = pushed
            return pushed

        ahead = through(0)
        for r in range(tiles):
            at = slice(r * TILE, (r + 1) * TILE)
            pushed = ahead
            if r + 1 < tiles:
                ahead = through(r + 1)
            value = nt(pushed, fc[...])
            if s == 0:
                back[at, :] = value
            else:
                back[at, :] += value
        if s < 2:
            for copy in feed(s + 2):
                copy.start()
        if s == 2:
            pump("wide", ("first", 0))
        weigh(normed_t, pre, h, 0, s % 2 == 1)
        if s == 3:
            pump("wide", ("second", 2, 3))

    for b in range(4):
        load_thin(b).start()
    att_copy = fetch(att_in, pre, 2)
    first_t_copy = fetch(first_t_in, normed_t, 1)
    load_slot(qkv_in.at[0], 0).start()
    load_slot(qkv_in.at[2], 2).start()
    one_copy.wait()

    def through_two(r, carry):
        at = rows_at(r, TILE)
        unit, rate = norm_stats(hidden[at, :])
        upstream = back[at, :]
        add_norm(2, upstream, unit)
        result = grad[at, :] + norm_back(unit, rate, norms[2:3, :], upstream)
        grad[at, :] = result
        branch[at, :] = result.astype(BF16)
        branch_t[:, at] = result.T.astype(BF16)
        return carry

    lax.fori_loop(0, tiles, through_two, 0)
    zero_copy = fetch(zero_in, hidden, 0)
    pump("wide", ("first", 1))
    att_copy.wait()

    def other_half(c):
        return pl.ds(pl.multiple_of(c * half, SPAN), half)

    def store(which, b, at, value):
        if fused and which == 1:
            thin.own[b, at, :] = value
        elif fused:
            posted_half(b)[at, :] = value
        else:
            thin_posted[4 * which + b, at, :] = value

    def out_weigh(m, carry):
        at = rows_at(m, TILE)
        for which in range(2):
            c = core if which else 1 - core
            store(which, 3, at, nn(branch_t[at, :], pre[:, other_half(c)]).astype(BF16))
        return carry

    if fused:
        sent(post_copy(1, 0))
        sent(post_copy(3, 1))
    lax.fori_loop(0, side, out_weigh, 0, unroll=True)
    thin_copy(3).start()
    if not fused:
        thin_kept(3).start()
    for b in range(4):
        load_thin(b).wait()
    keyt_copy = fetch(keyt_in, branch_t, 3)

    def spread_att(r, carry):
        at = rows_at(r, TILE)
        slots[3, at, :] = nn(branch[at, :], weights[3]).astype(BF16)
        return carry

    lax.fori_loop(0, tiles, spread_att, 0, unroll=True)
    pump("wide", ("second", 0))
    pump("thin", ("take", 3), ("first", 3))
    count = blocks // 2

    def probs_copy(unit):
        slot = lax.rem(unit, 2)
        return pltpu.make_async_copy(probs_in.at[pl.ds(unit * count, count)], probs.at[slot], probs_sems.at[slot])

    probs_copy((1 - core) * pairs).start()
    load_slot(qkv_in.at[0], 0).wait()
    load_slot(qkv_in.at[2], 2).wait()
    keyt_copy.wait()
    low, high = halves_of((1, SPAN), 1, 0.125)
    low_one, high_one = halves_of((1, SPAN), 1, 1.0)

    def attend(pair, carry):
        cols = pl.ds(pl.multiple_of(pair * SPAN, SPAN), SPAN)
        acc[...] = jnp.zeros(acc.shape, F32)
        for part in range(2):
            unit = 2 * pair + part

            @pl.when(lax.rem(unit + 1, pairs) != 0)
            def ahead():
                probs_copy(unit + 1).start()

            probs_copy(unit).wait()

            def ask(k):
                i = part * count + k
                w0 = window_start(i, blocks)
                up_rows = slots[3, i * SPAN : (i + 1) * SPAN, cols]
                ups = jnp.concatenate([up_rows * low_one, up_rows * high_one], axis=0)
                return ups, nt(slots[2, w0 : w0 + WINDOW, cols], ups)

            ahead = ask(0)
            for k in range(count):
                i = part * count + k
                w0 = window_start(i, blocks)
                here = slice(i * SPAN, (i + 1) * SPAN)
                there = slice(w0, w0 + WINDOW)
                ups, grad_probs = ahead
                if k + 1 < count:
                    ahead = ask(k + 1)
                queries = slots[0, here, cols]
                asks = jnp.concatenate([queries * low, queries * high], axis=0)
                prob = probs[part, k]
                wide_probs = prob.astype(F32)
                inner = jnp.sum(grad_probs * wide_probs, axis=0, keepdims=True)
                grad_scores = (wide_probs * (grad_probs - inner)).astype(BF16)
                acc[1, there, :] += nn(prob, ups)
                acc[0, there, :] += nn(grad_scores, asks)
                asked = nn(branch_t[cols, there], grad_scores)
                slots[0, here, cols] = (pick_halves(asked).T * 0.125).astype(BF16)
        slots[1, :, cols] = acc[0].astype(BF16)
        slots[2, :, cols] = acc[1].astype(BF16)
        return carry

    def qkv_weigh(which):
        cols = other_half(core if which else 1 - core)

        def body(m, carry):
            at = rows_at(m, TILE)
            rows = normed_t[at, :]
            for j in range(3):
                store(which, j, at, nn(rows, slots[j, :, cols]).astype(BF16))
            return carry

        lax.fori_loop(0, side, body, 0, unroll=True)

    few = pairs // 2
    for which in range(2):
        base = (core if which else 1 - core) * few
        lax.fori_loop(base, base + few - 1, attend, 0)
        if which == 1:
            pump("wide", ("third", 0))
        lax.fori_loop(base + few - 1, base + few, attend, 0)
        if which == 0:
            probs_copy(core * pairs).start()
            first_t_copy.wait()
            pump("wide", ("second", 1), ("third", 2, 3))
        else:
            pump("thin", ("second", 3), ("take", 0, 1))
            pump("wide", ("third", 1))
        qkv_weigh(which)
        for j in range(3):
            if which == 0:
                thin_copy(j).start()
            elif not fused:
                thin_kept(j).start()
    zero_copy.wait()
    pump("thin", ("take", 2), ("first", 0, 1, 2))

    def towards_one(r):
        at = slice(r * TILE, (r + 1) * TILE)
        return nt(slots[0, at, :], weights[0]) + nt(slots[1, at, :], weights[1]) + nt(slots[2, at, :], weights[2])

    def through_one(r, upstream):
        at = slice(r * TILE, (r + 1) * TILE)
        unit, rate = norm_stats(hidden[at, :])
        add_norm(0, upstream, unit)
        grad_zero = (grad[at, :] + norm_back(unit, rate, norms[0:1, :], upstream)).astype(BF16)
        small[:, u0 : u0 + width] += nn(noisy[at, :].astype(F32).T.astype(BF16), grad_zero)
        grad_start = (keep_root * nt(grad_zero, up_low[...]) - error[at, :]).T
        upper = grad_start.astype(BF16)
        lower = (grad_start - upper.astype(F32)).astype(BF16)
        hot = (columns[:, at].T[:, 0:1] == ids).astype(F32).astype(BF16)
        both = jnp.concatenate([upper, lower], axis=1)
        small[:, e0 : e0 + vocab] += nn(both, jnp.concatenate([hot, hot], axis=0))

    ahead = towards_one(0)
    for r in range(tiles):
        upstream = ahead
        if r + 1 < tiles:
            ahead = towards_one(r + 1)
        through_one(r, upstream)
        if r == 0:
            pump("thin", ("third", 3))
        if r == 2:
            pump("thin", ("second", 0, 1, 2))
    squares = jnp.zeros((1, 1), F32)
    if fused:
        squares = wide.result(0) + wide.result(2) + wide.result(3)
    lanes = emb
    n0 = e0 + vocab
    for k in range(6):
        for j in range(width // lanes):
            row = k * (width // lanes) + j
            small[row : row + 1, n0 : n0 + lanes] = norm_grads[k : k + 1, j * lanes : (j + 1) * lanes]
    if not fused:
        row = lax.broadcasted_iota(jnp.int32, out_scalars.shape, 0)
        out_scalars[...] = jnp.where(row == 1, loss, jnp.where(row == 2, weight_total, 0.0))
        for slot, b in ((0, 1), (1, 3)):
            sent(post_copy(b, slot))
            kept_copy(b, 2 + slot).wait()
        for b in range(4):
            sent(thin_copy(b))
            thin_kept(b).wait()
        return

    for q in range(4):
        value = small[:, q * group : (q + 1) * group].astype(BF16)
        rows = slice((q % 2) * small.shape[0], (q % 2 + 1) * small.shape[0])
        mine = core == q // 2

        @pl.when(mine)
        def keep():
            tiny.own[0, rows, :] = value

        @pl.when(jnp.logical_not(mine))
        def give():
            small_own[rows, :] = value

    give_copy = tiny.pair_copy(0, small_own)
    give_copy.start()
    tiny.take(0)
    tiny.first(0)
    pump("thin", ("third", 0, 1))
    tiny.second(0)
    squares = squares + wide.result(1) + thin.result(3)
    tiny.third(0)
    pump("thin", ("third", 2))
    squares = squares + tiny.result(0)
    tiny_shard[...] = tiny_out[0].astype(BF16)
    gather = QuickGather(tiny_shard, tiny_whole, quick_sems, 16)
    gather.begin()
    squares = squares + thin.result(0) + thin.result(1) + thin.result(2)
    row = lax.broadcasted_iota(jnp.int32, scalars.shape, 0)
    scalars[...] = jnp.where(row == 0, squares, jnp.where(row == 1, loss, 0.0))
    exchange = Exchange(scalars, slots_all, all_sems, devices)
    exchange.start()
    gather.spread()
    gather.share()
    gather.ready()
    exchange.arrive()
    out_scalars[...] = jnp.where(row == 2, weight_total, exchange.total())
    for q in range(4):
        rows = slice((q % 2) * small.shape[0], (q % 2 + 1) * small.shape[0])
        out_small[:, q * group : (q + 1) * group] = tiny_whole[(q // 2) * 2 * emb : (q // 2 + 1) * 2 * emb, :][rows, :].astype(F32)
    for b in range(4):
        sent(thin_copy(b))
    give_copy.wait_send()
    gather.finish()
    exchange.finish()
    for b in range(4):
        wide.finish(b)
        thin.finish(b)
    tiny.finish(0)


def run_backward(fused, wide_whole, thin_whole, tokens, buckets, counted, counts, start, noisy, table_low, kept, up_weight, down_weight, norms, steps, vocab_used):
    zero, one, two, qkv, key_t, att, probs, act, slope, first_t, second_t = kept
    length, width = zero.shape
    pairs = width // SPAN
    blocks = length // SPAN
    emb, vocab = start.shape[1], table_low.shape[0]
    dma, vmem = pltpu.SemaphoreType.DMA, pltpu.VMEM
    anywhere, inside = pl.BlockSpec(memory_space=pl.ANY), pl.BlockSpec(memory_space=pltpu.VMEM)
    spread = 2 * width + vocab + emb
    group = spread // 4
    rows = width // 16

    def made(shape, dtype=BF16):
        return jax.ShapeDtypeStruct(shape, dtype)

    wide_out = made((4, rows, width), F32) if fused else made((4, 2, width, width))
    thin_out = made((4, rows, width // 2), F32) if fused else made((4, 2, width, width // 2))
    out_shape = [wide_out, thin_out, made((emb, spread), F32), made((8, 128), F32)]
    if fused:
        out_shape += [made((4, width, width)), made((4, width, width // 2)), made((1, 2 * emb, group))]
    else:
        out_shape += [made((8, 128))] * 3
    scratch = [
        vmem((length, width), F32),
        vmem((length, width), F32),
        vmem((length, width), F32),
        vmem((length, width), BF16),
        vmem((width, length), BF16),
        vmem((width, length), BF16),
        vmem((length, width), BF16),
        vmem((4, length, width), BF16),
        vmem((4, width, width), BF16),
        vmem((2, length, SPAN), F32),
        vmem((2, blocks // 2, WINDOW, 2 * SPAN), BF16),
        vmem((length, emb), F32),
        vmem((8, width), F32),
        vmem((2 if fused else 4, width, width), BF16),
        vmem((8, 128) if fused else (8, width, width // 2), BF16),
        vmem((8, 128), F32),
        vmem((8, length), F32),
        vmem((emb, width), BF16),
        vmem((width, emb), BF16),
        dma((12,)),
        dma((4,)),
        dma((12,)),
        dma((2,)),
        dma((12,)),
    ]
    if fused:
        scratch += scatter_scratch(4, rows, width) + scatter_scratch(4, rows, width // 2) + scatter_scratch(1, 16, group)
        scratch += [
            vmem((2, width, width), BF16),
            vmem((16, group), BF16),
            vmem((1, 16, group), F32),
            vmem((32, 8, 128), F32),
            dma((2,)),
            dma((7,)),
        ]
        params = pltpu.CompilerParams(collective_id=1, has_side_effects=True, vmem_limit_bytes=VMEM_LIMIT)
    else:
        params = pltpu.CompilerParams(vmem_limit_bytes=VMEM_LIMIT)
    return pl.pallas_call(
        functools.partial(backward_kernel, fused, (length, width, pairs, vocab_used)),
        out_shape=out_shape,
        in_specs=[anywhere] * 2 + [inside] * 4 + [anywhere, inside] + [anywhere] * 11 + [inside] * 4 + [pl.BlockSpec(memory_space=pltpu.SMEM)],
        out_specs=[inside if fused else anywhere] * 2 + [inside] * 2 + [anywhere] * 3,
        scratch_shapes=scratch,
        compiler_params=params,
        name="backward",
    )(wide_whole, thin_whole, tokens, buckets, counted, counts, start, noisy, zero, one, two, qkv, key_t, att, probs, act, slope, first_t, second_t, table_low, up_weight, down_weight, norms, steps)[:4]


def adam_update(weight, grad, first, second, rate, decay):
    first_new = BETA_FIRST * first + (1.0 - BETA_FIRST) * grad
    second_new = BETA_SECOND * second + (1.0 - BETA_SECOND) * grad * grad
    first_hat = first_new / (1.0 - BETA_FIRST**STEP)
    second_hat = second_new / (1.0 - BETA_SECOND**STEP)
    weight_new = weight - rate * (first_hat / (jnp.sqrt(second_hat) + ADAM_EPS) + decay * weight)
    return (first_new, second_new, weight_new)


def clip_factor(squares):
    grad_norm = jnp.sqrt(squares)
    return grad_norm, jnp.minimum(1.0, CLIP_NORM / (grad_norm + 1e-06))


def adam_kernel(*refs):
    sources, outs, held, made = refs[:28], refs[28:55], refs[55:83], refs[83:107]
    in_sems, out_sems = refs[107:]
    order = [0, 1, 2, 3] + [4 + k for index in (6, 5, 3, 0, 1, 2, 4, 7) for k in range(3 * index, 3 * index + 3)]
    loads = {k: pltpu.make_async_copy(sources[k], held[k], in_sems.at[k]) for k in order}
    for k in order:
        loads[k].start()
    wide, thin, small, scalars = held[:4]
    states = held[4:]
    width = wide.shape[2]
    emb = small.shape[0]
    vocab = states[0].shape[0]
    for k in range(4):
        loads[k].wait()
    grad_norm, factor = clip_factor(scalars[0:1, 0:1])
    for out, value in zip(outs[:3], (scalars[1:2, 0:1], scalars[2:3, 0:1], grad_norm)):
        out[...] = value
    stores = []

    def update(index, pieces):
        rate, decay = (NORM_RATE, 0.0) if index == 7 else (MATRIX_RATE, WEIGHT_DECAY)
        mine = range(3 * index, 3 * index + 3)
        for k in mine:
            loads[4 + k].wait()
        for grad, *at in pieces:
            at = tuple(at) or (Ellipsis,)
            weight, first, second = (states[k][at] for k in mine)
            for k, value in zip(mine, adam_update(weight, factor * grad, first, second, rate, decay)):
                made[k][at] = value
        for k in mine:
            stores.append(pltpu.make_async_copy(made[k], outs[3 + k], out_sems.at[k]))
            stores[-1].start()

    def halves(first):
        return [(wide[first + h], slice(None), slice(h * width, (h + 1) * width)) for h in range(2)]

    update(6, halves(2))
    update(5, halves(0))
    update(3, [(thin[j], j) for j in range(3)])
    update(0, [(small[:, 2 * width : -emb].T[:vocab],)])
    update(1, [(small[:, width : 2 * width],)])
    update(2, [(small[:, :width].T,)])
    update(4, [(thin[3],)])
    per = width // emb
    update(
        7,
        [
            (small[k * per + j : k * per + j + 1, -emb:], slice(k, k + 1), slice(j * emb, (j + 1) * emb))
            for k in range(6)
            for j in range(per)
        ],
    )
    for store in stores:
        store.wait()


def run_adam(wide, thin, small, scalars, states):
    inside, anywhere = pl.BlockSpec(memory_space=pltpu.VMEM), pl.BlockSpec(memory_space=pl.ANY)
    sources = (wide, thin, small, scalars, *states)
    shapes = [states[3 * (k // 3)].shape for k in range(24)]
    return pl.pallas_call(
        adam_kernel,
        out_shape=[jax.ShapeDtypeStruct((1, 1), F32)] * 3 + [jax.ShapeDtypeStruct(shape, F32) for shape in shapes],
        in_specs=[anywhere] * 28,
        out_specs=[inside] * 3 + [anywhere] * 24,
        scratch_shapes=[pltpu.VMEM(source.shape, F32) for source in sources]
        + [pltpu.VMEM(shape, F32) for shape in shapes]
        + [pltpu.SemaphoreType.DMA((28,)), pltpu.SemaphoreType.DMA((24,))],
        compiler_params=pltpu.CompilerParams(vmem_limit_bytes=VMEM_LIMIT),
        name="adam",
    )(*sources)


def shards_of(qkv_weight, out_t, fc_weight, proj_t):
    width = fc_weight.shape[1] // 2
    wide = [array[:, h * width : (h + 1) * width] for array in (fc_weight, proj_t) for h in range(2)]
    return jnp.stack(wide).astype(BF16), jnp.concatenate([qkv_weight, out_t[None]]).astype(BF16)


def finished(results):
    return tuple(value.T if k in (15, 16, 17, 21, 22, 23) else value for k, value in enumerate(results))


def per_device(fused, token_ids, segment_ids, timesteps, noise, bucket_ids, counted, embed, up_weight, down_weight, qkv_weight, out_weight, fc_weight, proj_weight, norm_params, embed_m, embed_v, up_m, up_v, down_m, down_v, qkv_m, qkv_v, out_m, out_v, fc_m, fc_v, proj_m, proj_v, norm_m, norm_v):
    length = token_ids.shape[1]
    vocab, emb = embed.shape
    width = up_weight.shape[1]
    places = jnp.asarray(place_table(length, width))
    if fused:
        sources = (qkv_weight, out_weight.T, fc_weight, proj_weight.T)
    else:

        def gathered(shard):
            return lax.all_gather(lax.all_gather(shard, "dp", axis=1, tiled=True), "mp", axis=1)

        wide_all, thin_all = map(gathered, shards_of(qkv_weight, out_weight.T, fc_weight, proj_weight.T))
        sources = (wide_all, jnp.concatenate([thin_all[:, 0], thin_all[:, 1]], axis=2))
    wide_whole, thin_whole, counts, start, noisy, table_low, *kept = run_forward(
        fused, sources, token_ids, segment_ids, timesteps, noise, bucket_ids, counted, embed, up_weight, norm_params, places
    )
    if not fused:
        wide_whole, thin_whole = sources
        counts = lax.psum(counts, "dp")
    wide, thin, small, scalars = run_backward(
        fused, wide_whole, thin_whole, token_ids, bucket_ids, counted, counts, start, noisy, table_low, kept, up_weight, down_weight, norm_params, timesteps, vocab
    )
    states = (
        embed, embed_m, embed_v, up_weight, up_m, up_v, down_weight, down_m, down_v, qkv_weight, qkv_m, qkv_v,
        out_weight.T, out_m.T, out_v.T, fc_weight, fc_m, fc_v, proj_weight.T, proj_m.T, proj_v.T, norm_params, norm_m, norm_v,
    )
    if fused:
        results = list(run_adam(wide, thin, small, scalars, states))
        results[:3] = [value.reshape(()) for value in results[:3]]
        return finished(results)

    def owned(blocks):
        blocks = lax.psum_scatter(blocks.astype(F32), "mp", scatter_dimension=1, tiled=False)
        return lax.psum_scatter(blocks, "dp", scatter_dimension=1, tiled=True)

    wide, thin = owned(wide), owned(thin)
    small, loss_sum = lax.psum((small, scalars[1, 0]), ("dp", "mp"))
    squares = lax.psum(jnp.sum(wide * wide) + jnp.sum(thin * thin), ("dp", "mp")) + jnp.sum(small * small)
    grad_norm, factor = clip_factor(squares)
    grads = (
        small[:, 2 * width : -emb].T[:vocab],
        small[:, width : 2 * width],
        small[:, :width].T,
        thin[:3],
        thin[3],
        jnp.concatenate([wide[0], wide[1]], axis=1),
        jnp.concatenate([wide[2], wide[3]], axis=1),
        small[: 6 * width // emb, -emb:].reshape(6, width),
    )
    results = [loss_sum, scalars[2, 0], grad_norm]
    for index, grad in enumerate(grads):
        rate, decay = (NORM_RATE, 0.0) if index == 7 else (MATRIX_RATE, WEIGHT_DECAY)
        weight, first, second = states[3 * index : 3 * index + 3]
        results.extend(adam_update(weight, factor * grad, first, second, rate, decay))
    return finished(results)


def solution(mesh):
    fused = mesh.shape["dp"] == 16 and mesh.shape["mp"] == 2
    state = {"copied": P(), "qkv": P(None, "dp", "mp"), "tall": P("mp", "dp"), "wide": P("dp", "mp")}
    kinds = ["copied"] * 3 + ["qkv", "tall", "wide", "tall", "copied"]
    weights = [state[kind] for kind in kinds]
    moments = [state[kind] for kind in kinds for unused in range(2)]
    placed = (
        P("dp", None), P("dp", None), P("dp"), P("dp", None, None), P("dp", None), P("dp", None),
        *weights,
        *moments,
    )
    outs = (P(), P(), P()) + tuple(state[kind] for kind in kinds for unused in range(3))
    return jax.shard_map(
        functools.partial(per_device, fused), mesh=mesh, in_specs=placed, out_specs=outs, check_vma=False
    )
```
